32 devices in a mesh: veh: 8 (over z, y), row: 4 (over x, core).
Axes of the slice: x: 2, y: 2, z: 4, core: 2. Of those that a mesh axis runs over, the one named last changes fastest.
Arguments:
- bev_maps: bfloat16 [64, 32, 64, 128], P('veh', 'row'), may hold values from -6 to 6
- senders: int32 [64, 4], replicated, may hold values from 0 to 63, as said below
- shifts: int32 [64, 4], replicated, may hold values from -1 to 1
- counts: int32 [64], replicated, may hold values from 1 to 4, as said below
- agent_query: bfloat16 [128, 128], replicated, may hold values from -0.5 to 0.5
- agent_keyvalue: bfloat16 [128, 256], replicated, may hold values from -0.5 to 0.5
- agent_out: bfloat16 [128, 128], replicated, may hold values from -0.5 to 0.5
- agent_scale: float32 [4], replicated, may hold values from 1 to 600
- conv_weight: float32 [3, 3, 256], replicated, may hold values from -1.5 to 1.5
- gain_first: float32 [256], replicated, may hold values from 0.1 to 1.9
- window_in: bfloat16 [256, 768], replicated, may hold values from -0.375 to 0.375
- window_out: bfloat16 [256, 256], replicated, may hold values from -0.375 to 0.375
- window_scale: float32 [8], replicated, may hold values from 1 to 600
- gain_second: float32 [256], replicated, may hold values from 0.1 to 1.9
- hidden_up: bfloat16 [256, 512], replicated, may hold values from -0.375 to 0.375
- hidden_down: bfloat16 [512, 256], replicated, may hold values from -0.25 to 0.25
Outputs:
- joined_map: bfloat16 [64, 32, 64, 256], P('veh', 'row')
The draws below stay inside these ranges and needn't reach their ends.
Inputs may be any that keep to these rules, and one draw needn't show every extreme that they name: `senders`: never the receiver itself. Blocks are aligned runs of 8 vehicles; over the live pairs whose receiver lies in one block and whose sender lies in one block, the intersecting tiles (2 - |shift| a pair) number at most 8. Slots a < counts[r] of receiver r are live.
All inputs are finite; a program needn't handle non-finite values.
Results may differ from the reference program's by a relative error of at most 0.0095.
The reference program's roundings to bfloat16 on the way count: a program that leaves them out, or rounds other values in their place, can miss the bound.
Values may be sent and summed in bfloat16 or wider, within the bound.
No kernel may reach another device: no remote copies, remote signals or barrier semaphores. Data moves between devices by JAX's collectives and lax.ppermute only.
A program may use at most 128 MiB of HBM per device.

```python
import math
import jax
import jax.numpy as jnp
from jax import lax

VEH_DEV = 8
AGENTS = 4
CH = 128
WIDTH = 256
HEADS = 8
AGENT_HEADS = 4
MLP = 512
TILE = 32
WIN = 8
MAP_COLS = 64
MAP_ROWS = 32
VEHICLES = 64


def pair_tables(key):
    base_key = jax.random.fold_in(key, 101)
    order_key, local_key, shift_key, count_key, full_key, zero_key, keep_key = jax.random.split(base_key, 7)
    devices = VEHICLES // VEH_DEV
    pair_count = AGENTS * VEH_DEV
    domain = max(devices, pair_count)
    tile_cols = MAP_COLS // TILE
    device_keys = jax.random.split(order_key, devices)
    orders = jax.vmap(lambda single_key: jax.random.permutation(single_key, domain))(device_keys)[:, :pair_count]
    receiver_dev = jnp.arange(devices, dtype=jnp.int32)[:, None]
    source_dev = (receiver_dev + orders % devices) % devices
    local_pick = jax.random.randint(local_key, (devices, pair_count), 0, VEH_DEV)
    receiver_local = (jnp.arange(pair_count, dtype=jnp.int32) // AGENTS)[None, :]
    clash = (source_dev == receiver_dev) & (local_pick == receiver_local)
    local_pick = jnp.where(clash, (local_pick + 1) % VEH_DEV, local_pick)
    senders = (source_dev * VEH_DEV + local_pick).reshape(VEHICLES, AGENTS).astype(jnp.int32)
    shifts = jax.random.randint(shift_key, (VEHICLES, AGENTS), 1 - tile_cols, tile_cols)
    zero_pick = jax.random.randint(zero_key, (VEHICLES, AGENTS), 0, 2) == 0
    shifts = jnp.where(zero_pick, 0, shifts)
    counts = jax.random.randint(count_key, (VEHICLES,), 1, AGENTS + 1)
    keep_full = jax.random.randint(keep_key, (VEHICLES,), 0, 4) != 0
    counts = jnp.where(keep_full, AGENTS, counts)
    full_dev = jax.random.randint(full_key, (), 0, devices)
    on_full = jnp.arange(VEHICLES, dtype=jnp.int32) // VEH_DEV == full_dev
    counts = jnp.where(on_full, AGENTS, counts).astype(jnp.int32)
    shifts = jnp.where(on_full[:, None], 0, shifts).astype(jnp.int32)
    return (senders, shifts, counts)


def draw_senders(key, part):
    return pair_tables(key)[0]


def draw_shifts(key, part):
    return pair_tables(key)[1]


def draw_counts(key, part):
    return pair_tables(key)[2]


def head_scales(key, count, salt):
    salted = jax.random.fold_in(key, salt)
    first_key = jax.random.fold_in(salted, 0)
    scales = jnp.exp(jax.random.uniform(first_key, (count,), jnp.float32, 0.0, math.log(40.0)))
    return scales.astype(jnp.float32)


def draw_agent_scale(key, part):
    return head_scales(key, AGENT_HEADS, 211)


def draw_window_scale(key, part):
    return head_scales(key, HEADS, 223)


def level_of(key, shape, shards, smallest, high):
    factor_of, own = 1.0, jax.random.fold_in(key, 6)
    for axis_at, shards_of in shards:
        draws = jnp.exp(jax.random.uniform(jax.random.fold_in(own, axis_at), (shards_of,), jnp.float32, smallest / len(shards), high / len(shards)))
        factor_of = factor_of * jnp.repeat(draws, shape[axis_at] // shards_of).reshape([-1 if axis == axis_at else 1 for axis in range(len(shape))])
    return factor_of


def scatter_about(rng, shape, scale, reach, pieces=(), held_as=jnp.bfloat16):
    entries = scale * jax.random.normal(rng, shape, jnp.float32)
    if pieces:
        entries = entries * level_of(rng, shape, pieces, -0.22, 0.18)
    return jnp.clip(entries, -reach, reach).astype(held_as)


def setup_inputs(seed: int = 0) -> dict:
    seeds = jax.random.split(jax.random.key(seed), 17)
    return {
        "bev_maps": scatter_about(seeds[0], (VEHICLES, MAP_ROWS, MAP_COLS, CH), 1.0, 6.0, ((0, 8), (1, 4))),
        "senders": draw_senders(jax.random.fold_in(seeds[16], 71), 0),
        "shifts": draw_shifts(jax.random.fold_in(seeds[16], 71), 0),
        "counts": draw_counts(jax.random.fold_in(seeds[16], 71), 0),
        "agent_query": scatter_about(seeds[4], (CH, CH), CH ** -0.5, 0.5),
        "agent_keyvalue": scatter_about(seeds[5], (CH, 2 * CH), CH ** -0.5, 0.5),
        "agent_out": scatter_about(seeds[6], (CH, CH), CH ** -0.5, 0.5),
        "agent_scale": draw_agent_scale(jax.random.fold_in(seeds[16], 71), 0),
        "conv_weight": scatter_about(seeds[8], (3, 3, WIDTH), 0.3, 1.5, (), jnp.float32),
        "gain_first": jnp.clip(1.0 + 0.18 * jax.random.normal(seeds[9], (WIDTH,), jnp.float32), 0.1, 1.9),
        "window_in": scatter_about(seeds[10], (WIDTH, 3 * WIDTH), WIDTH ** -0.5, 0.375),
        "window_out": scatter_about(seeds[11], (WIDTH, WIDTH), WIDTH ** -0.5, 0.375),
        "window_scale": draw_window_scale(jax.random.fold_in(seeds[16], 71), 0),
        "gain_second": jnp.clip(1.0 + 0.18 * jax.random.normal(seeds[13], (WIDTH,), jnp.float32), 0.1, 1.9),
        "hidden_up": scatter_about(seeds[14], (WIDTH, MLP), WIDTH ** -0.5, 0.375),
        "hidden_down": scatter_about(seeds[15], (MLP, WIDTH), MLP ** -0.5, 0.25),
    }


exact_dot = lax.Precision.HIGHEST
norm_eps = 1e-05
unit_eps = 1e-06

def head_spread(tensor, head_count):
    feature_width = tensor.shape[-1]
    member = (jnp.arange(feature_width)[:, None] // (feature_width // head_count) == jnp.arange(head_count)[None, :]).astype(jnp.float32)
    summed = jnp.dot(tensor, member, precision=exact_dot)
    return jnp.dot(summed, member.T, precision=exact_dot)

def unit_heads(tensor, head_count):
    return tensor / jnp.sqrt(head_spread(tensor * tensor, head_count) + unit_eps)

def join_agents(ego_map, own_keyvalue, sent_keyvalue, covered, agent_query, agent_out, agent_scale):
    channels = ego_map.shape[-1]
    head_count = agent_scale.shape[0]
    queries = unit_heads(jnp.dot(ego_map, agent_query, preferred_element_type=jnp.float32), head_count)
    all_kv = jnp.concatenate([own_keyvalue[:, None], sent_keyvalue], axis=1).astype(jnp.float32)
    key_part = unit_heads(all_kv[..., :channels], head_count)
    values = all_kv[..., channels:]
    scale_row = jnp.repeat(agent_scale, channels // head_count)
    scores = head_spread(queries[:, None] * key_part, head_count) * scale_row
    present = jnp.concatenate([jnp.ones_like(covered[:, :1]), covered], axis=1)[..., None]
    scores = jnp.where(present, scores, -1e+30)
    row_top = lax.optimization_barrier(jnp.max(scores, axis=1, keepdims=True))
    weight = jnp.where(present, jnp.exp(scores - row_top), 0.0)
    weight = weight / lax.optimization_barrier(jnp.sum(weight, axis=1, keepdims=True))
    agent_mix = lax.optimization_barrier(jnp.sum(weight * values, axis=1)).astype(jnp.bfloat16)
    joined = jnp.dot(agent_mix, agent_out, preferred_element_type=jnp.float32).astype(jnp.bfloat16)
    return jnp.concatenate([ego_map, joined], axis=-1)

def layer_norm(tensor, gain):
    average = lax.optimization_barrier(jnp.mean(tensor, axis=-1, keepdims=True))
    centred = tensor - average
    spread = lax.optimization_barrier(jnp.mean(centred * centred, axis=-1, keepdims=True))
    return centred * lax.rsqrt(spread + norm_eps) * gain

def to_windows(tensor, head_count):
    batch_size, height, width_cells, feature_width = tensor.shape
    tensor = tensor.reshape(batch_size, height // WIN, WIN, width_cells // WIN, WIN, head_count, feature_width // head_count)
    tensor = tensor.transpose(0, 1, 3, 5, 2, 4, 6)
    return tensor.reshape(batch_size, height // WIN, width_cells // WIN, head_count, WIN * WIN, feature_width // head_count)

def from_windows(tensor, height, width_cells):
    batch_size = tensor.shape[0]
    head_count = tensor.shape[3]
    head_width = tensor.shape[-1]
    tensor = tensor.reshape(batch_size, height // WIN, width_cells // WIN, head_count, WIN, WIN, head_width)
    tensor = tensor.transpose(0, 1, 4, 2, 5, 3, 6)
    return tensor.reshape(batch_size, height, width_cells, head_count * head_width)

def window_layer(padded, conv_weight, gain_first, window_in, window_out, window_scale, gain_second, hidden_up, hidden_down):
    batch_size, height, width_cells, feature_width = padded.shape
    height = height - 2
    widened = jnp.pad(padded, ((0, 0), (0, 0), (1, 1), (0, 0))).astype(jnp.float32)
    mixed_sum = widened[:, 1:height + 1, 1:width_cells + 1]
    for row_step in range(3):
        for col_step in range(3):
            mixed_sum = mixed_sum + widened[:, row_step:row_step + height, col_step:col_step + width_cells] * conv_weight[row_step, col_step]
    hidden = layer_norm(mixed_sum, gain_first).astype(jnp.bfloat16)
    projected = jnp.dot(hidden, window_in, preferred_element_type=jnp.float32)
    head_count = window_scale.shape[0]
    queries = to_windows(unit_heads(projected[..., :feature_width], head_count), head_count)
    key_part = to_windows(unit_heads(projected[..., feature_width:2 * feature_width], head_count), head_count)
    values = to_windows(projected[..., 2 * feature_width:].astype(jnp.bfloat16), head_count)
    scores = jnp.einsum('bxyhqd,bxyhkd->bxyhqk', queries, key_part, precision=exact_dot) * window_scale[:, None, None]
    row_top = lax.optimization_barrier(jnp.max(scores, axis=-1, keepdims=True))
    weight = jnp.exp(scores - row_top)
    weight = (weight / lax.optimization_barrier(jnp.sum(weight, axis=-1, keepdims=True))).astype(jnp.bfloat16)
    attended = jnp.einsum('bxyhqk,bxyhkd->bxyhqd', weight.astype(jnp.float32), values.astype(jnp.float32), precision=exact_dot)
    attended = from_windows(attended, height, width_cells).astype(jnp.bfloat16)
    mixed_sum = mixed_sum + jnp.dot(attended, window_out, preferred_element_type=jnp.float32)
    hidden = layer_norm(mixed_sum, gain_second).astype(jnp.bfloat16)
    inner_act = jax.nn.silu(jnp.dot(hidden, hidden_up, preferred_element_type=jnp.float32)).astype(jnp.bfloat16)
    return (mixed_sum + jnp.dot(inner_act, hidden_down, preferred_element_type=jnp.float32)).astype(jnp.bfloat16)

def reference(bev_maps, senders, shifts, counts, agent_query, agent_keyvalue, agent_out, agent_scale, conv_weight, gain_first, window_in, window_out, window_scale, gain_second, hidden_up, hidden_down):
    vehicles, height, width_cells, channels = bev_maps.shape
    agents = senders.shape[1]
    tile_cols = width_cells // TILE
    cell_count = height * width_cells
    blocked = bev_maps.reshape(vehicles // 4, 4, height, width_cells, channels)
    key_values = lax.map(lambda group_maps: jnp.dot(group_maps, agent_keyvalue, preferred_element_type=jnp.float32).astype(jnp.bfloat16), blocked)
    flat_kv = key_values.reshape(vehicles, height, width_cells, 2 * channels)
    tile_of = jnp.arange(width_cells) // TILE

    def one_group(operands):
        group_maps, group_kv, group_senders, group_shifts, group_counts = operands
        group_size = group_maps.shape[0]
        sent_keyvalue = jnp.take(flat_kv, group_senders.reshape(-1), axis=0)
        shift_flat = group_shifts.reshape(-1)
        sent_keyvalue = jax.vmap(lambda plane_kv, amount: jnp.roll(plane_kv, -amount * TILE, axis=1))(sent_keyvalue, shift_flat)
        shifted = tile_of[None, :] + shift_flat[:, None]
        present_pair = (jnp.arange(agents)[None, :] < group_counts[:, None]).reshape(-1)
        covered = (shifted >= 0) & (shifted < tile_cols) & present_pair[:, None]
        covered = jnp.broadcast_to(covered.reshape(group_size, agents, 1, width_cells), (group_size, agents, height, width_cells)).reshape(group_size, agents, cell_count)
        mixed_in = join_agents(group_maps.reshape(group_size, cell_count, channels), group_kv.reshape(group_size, cell_count, 2 * channels), sent_keyvalue.reshape(group_size, agents, cell_count, 2 * channels), covered, agent_query, agent_out, agent_scale)
        padded = jnp.pad(mixed_in.reshape(group_size, height, width_cells, 2 * channels), ((0, 0), (1, 1), (0, 0), (0, 0)))
        return window_layer(padded, conv_weight, gain_first, window_in, window_out, window_scale, gain_second, hidden_up, hidden_down)
    result = lax.map(one_group, (blocked, key_values, senders.reshape(vehicles // 4, 4, agents), shifts.reshape(vehicles // 4, 4, agents), counts.reshape(vehicles // 4, 4)))
    return result.reshape(vehicles, height, width_cells, 2 * channels)
```

```python
import functools
import math

import jax
import jax.numpy as jnp
from jax import lax
from jax.experimental import pallas as pl
from jax.experimental.pallas import tpu as pltpu
from jax.sharding import PartitionSpec as P

TILE = 32
WIN = 8
HEAD = 32

norm_eps = 1e-05
unit_eps = 1e-06
LOG2E = math.log2(math.e)
VMEM_BYTES = 48 * 2**20

NN = (((1,), (0,)), ((), ()))
NT = (((1,), (1,)), ((), ()))
TN = (((0,), (0,)), ((), ()))


def dot(a, b, dims=NN):
    return lax.dot_general(a, b, dims, preferred_element_type=jnp.float32)


def split(x):
    high = x.astype(jnp.bfloat16)
    return high, (x - high.astype(jnp.float32)).astype(jnp.bfloat16)


def head_sums(x):
    return jnp.sum(x.reshape(x.shape[0] // HEAD, HEAD, x.shape[1]), axis=1, keepdims=True)


def by_head(x, factor):
    return (x.reshape(x.shape[0] // HEAD, HEAD, x.shape[1]) * factor).reshape(x.shape)


def join_kernel(agents, tile_cols, buffers, place, live, ego, *refs):
    bufs, refs = refs[:buffers], refs[buffers:]
    wq, wkv, wout, scale, out, landed, sems = refs
    r = pl.program_id(0)
    height, _, channels = ego.shape[1:]
    slots = agents * tile_cols
    sizes = [b.shape[0] for b in bufs]

    def fetch(i, _):
        @pl.when(live[i] > 0)
        def _():
            start = 0
            for b, size in zip(bufs, sizes):
                here = place[i] - start

                @pl.when((here >= 0) & (here < size))
                def _(b=b, here=here):
                    pltpu.make_async_copy(b.at[here], landed.at[i], sems.at[i]).start()

                start += size

        return 0

    @pl.when(r == 0)
    def _():
        lax.fori_loop(0, landed.shape[0], fetch, 0)

    heads = channels // HEAD
    scale_col = scale[...].reshape(heads, 1, 1)
    for t in range(tile_cols):
        cells = ego[0, :, t * TILE : (t + 1) * TILE, :].reshape(height * TILE, channels)
        queries = dot(wq[...], cells, NT)
        factor = lax.rsqrt(head_sums(queries * queries) + unit_eps) * scale_col

        def agent(x):
            kv = dot(wkv[...], x, NT).astype(jnp.bfloat16).astype(jnp.float32)
            keys, values = kv[:channels], kv[channels:]
            score = head_sums(queries * keys) * factor
            return score * lax.rsqrt(head_sums(keys * keys) + unit_eps), values

        scores, values = [], []
        s, v = agent(cells)
        scores.append(s)
        values.append(v)
        for a in range(agents):
            i = r * slots + a * tile_cols + t

            @pl.when(live[i] > 0)
            def _(i=i):
                pltpu.make_async_copy(bufs[0].at[0], landed.at[i], sems.at[i]).wait()

            x = landed[i].reshape(height * TILE, channels)
            x = jnp.where(live[i] > 0, x, jnp.zeros_like(x))
            s, v = agent(x)
            scores.append(jnp.where(live[i] > 0, s, -1e30))
            values.append(v)
        top = functools.reduce(jnp.maximum, scores)
        weights = [jnp.exp(s - top) for s in scores]
        total = functools.reduce(jnp.add, weights)
        inverse = 1.0 / total
        mix = by_head(values[0], weights[0] * inverse)
        for w, v in zip(weights[1:], values[1:]):
            mix = mix + by_head(v, w * inverse)
        joined = dot(mix.astype(jnp.bfloat16), wout[...], TN)
        out[0, :, t * TILE : (t + 1) * TILE, :] = joined.astype(jnp.bfloat16).reshape(
            height, TILE, channels
        )


def join_agents(maps, bufs, place, live, wq, wkv, wout, scale):
    vehicles, height, width, channels = maps.shape
    tile_cols = width // TILE
    agents = place.shape[0] // (vehicles * tile_cols)
    whole = lambda x: pl.BlockSpec(x.shape, lambda r, *_: (0,) * x.ndim)
    block = pl.BlockSpec((1, height, width, channels), lambda r, *_: (r, 0, 0, 0))
    weights = (wq.T, wkv.T, wout, scale.reshape(-1, 1))
    cells = vehicles * height * width
    return pl.pallas_call(
        functools.partial(join_kernel, agents, tile_cols, len(bufs)),
        out_shape=jax.ShapeDtypeStruct(maps.shape, jnp.bfloat16),
        grid_spec=pltpu.PrefetchScalarGridSpec(
            num_scalar_prefetch=2,
            grid=(vehicles,),
            in_specs=[block]
            + [pl.BlockSpec(memory_space=pl.ANY)] * len(bufs)
            + [whole(w) for w in weights],
            out_specs=block,
            scratch_shapes=[
                pltpu.VMEM((place.shape[0], height, TILE, channels), jnp.bfloat16),
                pltpu.SemaphoreType.DMA((place.shape[0],)),
            ],
        ),
        compiler_params=pltpu.CompilerParams(vmem_limit_bytes=VMEM_BYTES),
        cost_estimate=pl.CostEstimate(
            flops=cells * channels * channels * 20, bytes_accessed=cells * channels * 12, transcendentals=cells * 20
        ),
    )(place, live, maps, *bufs, *weights)


def norm(x, gain):
    average = jnp.mean(x, axis=-1, keepdims=True)
    centred = x - average
    spread = jnp.mean(centred * centred, axis=-1, keepdims=True)
    return (centred * lax.rsqrt(spread + norm_eps) * gain).astype(jnp.bfloat16)


def mixed_half(x, above, below, taps):
    rows, cols, channels = x.shape
    tall = jnp.concatenate([above, x, below], axis=0)

    def column(at):
        part = tall[0:rows] * taps[at]
        part = part + tall[1 : rows + 1] * taps[3 + at]
        return part + tall[2 : rows + 2] * taps[6 + at]

    total = x + column(1)
    place = lax.broadcasted_iota(jnp.int32, (cols, channels), 0)[None]
    flat = (rows * cols, channels)
    left = pltpu.roll(column(0).reshape(flat), 1, 0).reshape(x.shape)
    total = total + jnp.where(place == 0, 0.0, left)
    right = pltpu.roll(column(2).reshape(flat), rows * cols - 1, 0).reshape(x.shape)
    return total + jnp.where(place == cols - 1, 0.0, right)


def window_kernel(ego, joined, ego_up, ego_down, join_up, join_down, taps, gain_one, wq, wk, wv, wo,
                  scale, gain_two, up, down, out, mixed_ref):
    rows, cols, channels = ego.shape[1:]
    width = 2 * channels
    windows = cols // WIN
    in_window = rows * WIN
    cells = rows * cols
    heads = width // HEAD
    f32 = jnp.float32
    for half, (x, above, below) in enumerate(((ego, ego_up, ego_down), (joined, join_up, join_down))):
        lanes = slice(half * channels, (half + 1) * channels)
        part = mixed_half(x[0].astype(f32), above[0].astype(f32), below[0].astype(f32),
                          [taps[i : i + 1, lanes].reshape(1, 1, channels) for i in range(9)])
        part = jnp.swapaxes(part.reshape(rows, windows, WIN, channels), 0, 1)
        mixed_ref[:, lanes] = part.reshape(cells, channels)
    hidden = norm(mixed_ref[...], gain_one[...])
    queries = dot(wq[...], hidden, NT)
    values = dot(wv[...], hidden, NT).astype(jnp.bfloat16)
    keys = dot(hidden, wk[...])
    factor = lax.rsqrt(head_sums(queries * queries) + unit_eps) * scale[...].reshape(heads, 1, 1)
    queries = by_head(queries, factor)
    member = (
        lax.broadcasted_iota(jnp.int32, (width, width), 0) // HEAD
        == lax.broadcasted_iota(jnp.int32, (width, width), 1) // HEAD
    ).astype(f32).astype(jnp.bfloat16)
    square_high, square_low = split(keys * keys)
    keys = keys * lax.rsqrt(dot(square_high, member) + dot(square_low, member) + unit_eps)
    key_high, key_low = split(keys)

    pair = 2 * in_window
    group = 4 * HEAD
    lane = lax.broadcasted_iota(jnp.int32, (width, pair), 1) < in_window
    even = (lax.broadcasted_iota(jnp.int32, (width, pair), 0) // HEAD) % 2 == 0
    blank = jnp.zeros((2 * HEAD, pair), jnp.bfloat16)
    blank_p = jnp.zeros((in_window, 4 * in_window), jnp.bfloat16)
    lane_head = lax.broadcasted_iota(jnp.int32, (HEAD, pair), 1) < in_window
    attended = []
    for p in range(windows // 2):
        straight = queries[:, p * pair : (p + 1) * pair]
        turned = pltpu.roll(straight, in_window, 1)
        blocks = []
        for w in range(2):
            low, high = (straight, turned) if w == 0 else (turned, straight)
            blocks.append(split(jnp.where(even, jnp.where(lane, low, 0.0), jnp.where(lane, 0.0, high))))
        parts = []
        for g in range(width // group):
            channels_of = slice(g * group, (g + 1) * group)
            probs = []
            for w in range(2):
                at = (2 * p + w) * in_window
                k_high = key_high[at : at + in_window, channels_of]
                k_low = key_low[at : at + in_window, channels_of]

                def right(block):
                    block = block[channels_of]
                    return jnp.concatenate(
                        [
                            jnp.concatenate([block[: 2 * HEAD], blank], axis=1),
                            jnp.concatenate([blank, block[2 * HEAD :]], axis=1),
                        ],
                        axis=0,
                    )

                first = dot(jnp.concatenate([k_high, k_low], axis=0), right(blocks[w][0]))
                score = first[:in_window] + first[in_window:] + dot(k_high, right(blocks[w][1]))
                weight = jnp.exp2(score - jnp.max(score, axis=0, keepdims=True))
                weight = weight * (1.0 / jnp.sum(weight, axis=0, keepdims=True))
                weight = weight.astype(jnp.bfloat16)
                probs.append(
                    jnp.concatenate([weight, blank_p] if w == 0 else [blank_p, weight], axis=0)
                )
            v = values[channels_of, p * pair : (p + 1) * pair]
            first, second = dot(v, probs[0]), dot(v, probs[1])
            for h in range(4):
                rows_of = slice(h * HEAD, (h + 1) * HEAD)
                cols_of = slice((h // 2) * pair, (h // 2 + 1) * pair)
                a, b = first[rows_of, cols_of], second[rows_of, cols_of]
                if h % 2 == 0:
                    b = pltpu.roll(b, in_window, 1)
                else:
                    a = pltpu.roll(a, in_window, 1)
                parts.append(jnp.where(lane_head, a, b))
        attended.append(jnp.concatenate(parts, axis=0).astype(jnp.bfloat16))
    attended = jnp.concatenate(attended, axis=1)
    mixed = mixed_ref[...] + dot(attended, wo[...], TN)
    hidden = norm(mixed, gain_two[...])
    inner = dot(hidden, up[...])
    inner = (0.5 * inner * (1.0 + jnp.tanh(0.5 * inner))).astype(jnp.bfloat16)
    result = mixed + dot(inner, down[...])
    result = jnp.swapaxes(result.reshape(windows, rows, WIN, width), 0, 1)
    out[0] = result.reshape(rows, cols, width).astype(jnp.bfloat16)


def window_layer(maps, joined, edges, conv_weight, gain_first, window_in, window_out, window_scale,
                 gain_second, hidden_up, hidden_down):
    vehicles, height, cols, channels = maps.shape
    width = 2 * channels
    whole = lambda x: pl.BlockSpec(x.shape, lambda r: (0,) * x.ndim)
    block = lambda n, c: pl.BlockSpec((1, n, cols, c), lambda r: (r, 0, 0, 0))
    weights = (
        conv_weight.reshape(9, width),
        gain_first[None],
        window_in[:, :width].T,
        window_in[:, width : 2 * width],
        window_in[:, 2 * width :].T,
        window_out,
        (window_scale * LOG2E).reshape(-1, 1),
        gain_second[None],
        hidden_up,
        hidden_down,
    )
    cells = vehicles * height * cols
    return pl.pallas_call(
        window_kernel,
        out_shape=jax.ShapeDtypeStruct((vehicles, height, cols, width), jnp.bfloat16),
        grid=(vehicles,),
        in_specs=[block(height, channels)] * 2 + [block(1, channels)] * 4 + [whole(w) for w in weights],
        out_specs=block(height, width),
        scratch_shapes=[pltpu.VMEM((height * cols, width), jnp.float32)],
        compiler_params=pltpu.CompilerParams(vmem_limit_bytes=VMEM_BYTES),
        cost_estimate=pl.CostEstimate(
            flops=cells * width * width * 30, bytes_accessed=cells * width * 6, transcendentals=cells * width * 4
        ),
    )(maps, joined, *edges, *weights)


def edges_of(x):
    count = lax.axis_size("row")
    rows = x.shape[1]
    above = lax.ppermute(x[:, rows - 1 :], "row", [(i, i + 1) for i in range(count - 1)])
    below = lax.ppermute(x[:, :1], "row", [(i + 1, i) for i in range(count - 1)])
    return above, below


def pack_kernel(tile_cols, chosen, maps, packed, sems):
    def start(i, _):
        column = pl.multiple_of(chosen[i] % tile_cols * TILE, TILE)
        pltpu.make_async_copy(
            maps.at[chosen[i] // tile_cols, :, pl.ds(column, TILE), :], packed.at[i], sems.at[i]
        ).start()
        return 0

    def finish(i, _):
        pltpu.make_async_copy(maps.at[0, :, pl.ds(0, TILE), :], packed.at[i], sems.at[i]).wait()
        return 0

    count = packed.shape[0]
    lax.fori_loop(0, count, start, 0)
    lax.fori_loop(0, count, finish, 0)


def pack_tiles(maps, chosen):
    _, height, width, channels = maps.shape
    count = chosen.shape[0]
    return pl.pallas_call(
        functools.partial(pack_kernel, width // TILE),
        out_shape=jax.ShapeDtypeStruct((count, height, TILE, channels), maps.dtype),
        grid_spec=pltpu.PrefetchScalarGridSpec(
            num_scalar_prefetch=1,
            grid=(1,),
            in_specs=[pl.BlockSpec(maps.shape, lambda i, *_: (0, 0, 0, 0))],
            out_specs=pl.BlockSpec(memory_space=pl.ANY),
            scratch_shapes=[pltpu.SemaphoreType.DMA((count,))],
        ),
        compiler_params=pltpu.CompilerParams(vmem_limit_bytes=VMEM_BYTES),
        cost_estimate=pl.CostEstimate(flops=0, bytes_accessed=4 * maps.size, transcendentals=0),
    )(chosen.astype(jnp.int32), maps)


def exchange(bev_maps, senders, shifts, counts):
    vehicles_here, height, width_cells, channels = bev_maps.shape
    agents = senders.shape[1]
    devices = lax.axis_size("veh")
    myself = lax.axis_index("veh")
    tile_cols = width_cells // TILE
    pairs = vehicles_here * agents
    capacity = tile_cols * max(1, pairs // devices)
    send_all = senders.reshape(devices, pairs)
    shift_all = shifts.reshape(devices, pairs)
    live_all = (jnp.arange(agents)[None, :] < counts[:, None]).reshape(devices, pairs)
    tiles_all = jnp.where(live_all, tile_cols - jnp.abs(shift_all), 0)
    source_all = send_all // vehicles_here
    same = source_all[:, :, None] == source_all[:, None, :]
    before = jnp.arange(pairs)[None, :] < jnp.arange(pairs)[:, None]
    start_all = jnp.sum(jnp.where(same & before[None], tiles_all[:, None, :], 0), axis=2)
    step = jnp.arange(tile_cols, dtype=jnp.int32)
    tile_of = (
        (send_all % vehicles_here * tile_cols + jnp.maximum(shift_all, 0))[:, :, None] + step
    ).reshape(devices, pairs * tile_cols)
    slot_of = jnp.where(
        ((source_all == myself)[:, :, None]) & (step < tiles_all[:, :, None]),
        start_all[:, :, None] + step,
        -1,
    ).reshape(devices, pairs * tile_cols)
    hit = slot_of[:, None, :] == jnp.arange(capacity)[None, :, None]
    chosen = jnp.sum(jnp.where(hit, tile_of[:, None, :], 0), axis=2).reshape(-1)
    packed = pack_tiles(bev_maps, chosen)
    arrived = lax.all_to_all(
        packed.reshape(devices, capacity, height, TILE, channels), "veh", 0, 0, tiled=True
    ).reshape(devices * capacity, height, TILE, channels)
    shifted = step + shift_all[myself][:, None]
    inside = (shifted >= 0) & (shifted < tile_cols) & live_all[myself][:, None]
    place = (
        (source_all[myself] * capacity + start_all[myself])[:, None]
        + step
        - jnp.maximum(-shift_all[myself], 0)[:, None]
    )
    place = jnp.where(inside, place, 0)
    return [arrived], place.reshape(-1).astype(jnp.int32), inside.reshape(-1).astype(jnp.int32)


def on_device(
    bev_maps,
    senders,
    shifts,
    counts,
    agent_query,
    agent_keyvalue,
    agent_out,
    agent_scale,
    conv_weight,
    gain_first,
    window_in,
    window_out,
    window_scale,
    gain_second,
    hidden_up,
    hidden_down,
):
    ego_up, ego_down = edges_of(bev_maps)
    bufs, place, live = exchange(bev_maps, senders, shifts, counts)
    joined = join_agents(
        bev_maps, bufs, place, live, agent_query, agent_keyvalue, agent_out, agent_scale
    )
    join_up, join_down = edges_of(joined)
    return window_layer(
        bev_maps,
        joined,
        (ego_up, ego_down, join_up, join_down),
        conv_weight,
        gain_first,
        window_in,
        window_out,
        window_scale,
        gain_second,
        hidden_up,
        hidden_down,
    )


def solution(mesh):
    split_maps = P("veh", "row", None, None)
    return jax.shard_map(
        on_device,
        mesh=mesh,
        in_specs=(split_maps,) + (P(),) * 15,
        out_specs=split_maps,
        check_vma=False,
    )
```

```python
import functools
import math

import jax
import jax.numpy as jnp
from jax import lax
from jax.experimental import pallas as pl
from jax.experimental.pallas import tpu as pltpu
from jax.sharding import PartitionSpec as P

TILE = 32
WIN = 8
HEAD = 32

norm_eps = 1e-05
unit_eps = 1e-06
LOG2E = math.log2(math.e)
VMEM_BYTES = 48 * 2**20
PHASES = 2

NN = (((1,), (0,)), ((), ()))
NT = (((1,), (1,)), ((), ()))
TN = (((0,), (0,)), ((), ()))


def dot(a, b, dims=NN):
    return lax.dot_general(a, b, dims, preferred_element_type=jnp.float32)


def split(x):
    high = x.astype(jnp.bfloat16)
    return high, (x - high.astype(jnp.float32)).astype(jnp.bfloat16)


def head_sums(x):
    return jnp.sum(x.reshape(x.shape[0] // HEAD, HEAD, x.shape[1]), axis=1, keepdims=True)


def by_head(x, factor):
    return (x.reshape(x.shape[0] // HEAD, HEAD, x.shape[1]) * factor).reshape(x.shape)


def phase_columns(phase):
    run = TILE // PHASES
    return [TILE - 1] + list(range(run + 1)) if phase == 0 else list(range(run + 1, TILE - 1))


def copy_tiles(chosen, pieces, packed, sems):
    def start(i, _):
        pltpu.make_async_copy(pieces.at[chosen[i]], packed.at[i], sems.at[i]).start()
        return 0

    def finish(i, _):
        pltpu.make_async_copy(pieces.at[0], packed.at[i], sems.at[i]).wait()
        return 0

    count = packed.shape[0]
    lax.fori_loop(0, count, start, 0)
    lax.fori_loop(0, count, finish, 0)


def turn_kernel(chosen, maps, turned, first, second, packed, scratch, sems):
    vehicles, rows, cols, channels = maps.shape
    tile_cols = cols // TILE
    run = TILE // PHASES

    def vehicle(v, _):
        for i in range(rows):
            scratch[pl.ds(i, cols, stride=rows), :] = maps[v, i].astype(jnp.float32)
        x = scratch[...].astype(jnp.bfloat16).reshape(cols, rows, channels)
        turned[v] = x
        for t in range(tile_cols):
            at = v * tile_cols + t
            tile = x[t * TILE : (t + 1) * TILE]
            first[at] = jnp.concatenate([tile[TILE - 1 :], tile[: run + 1]], axis=0)
            second[at] = tile[run + 1 : TILE - 1]
        return 0

    lax.fori_loop(0, vehicles, vehicle, 0)
    copy_tiles(chosen, first, packed, sems)


def turn_maps(maps, chosen):
    vehicles, rows, cols, channels = maps.shape
    tiles = vehicles * (cols // TILE)
    count = chosen.shape[0]
    pieces = [(tiles, len(phase_columns(p)), rows, channels) for p in range(PHASES)]
    shapes = [(vehicles, cols, rows, channels), *pieces, (count, *pieces[0][1:])]
    whole = lambda shape: pl.BlockSpec(shape, lambda i, *_: (0,) * len(shape))
    return pl.pallas_call(
        turn_kernel,
        out_shape=[jax.ShapeDtypeStruct(shape, maps.dtype) for shape in shapes],
        grid_spec=pltpu.PrefetchScalarGridSpec(
            num_scalar_prefetch=1,
            grid=(1,),
            in_specs=[whole(maps.shape)],
            out_specs=[whole(shape) for shape in shapes[:3]] + [pl.BlockSpec(memory_space=pl.ANY)],
            scratch_shapes=[
                pltpu.VMEM((rows * cols, channels), jnp.float32),
                pltpu.SemaphoreType.DMA((count,)),
            ],
        ),
        compiler_params=pltpu.CompilerParams(vmem_limit_bytes=VMEM_BYTES),
        cost_estimate=pl.CostEstimate(flops=0, bytes_accessed=10 * maps.size, transcendentals=0),
    )(chosen, maps)


def pack_tiles(pieces, chosen):
    count = chosen.shape[0]
    return pl.pallas_call(
        copy_tiles,
        out_shape=jax.ShapeDtypeStruct((count, *pieces.shape[1:]), pieces.dtype),
        grid_spec=pltpu.PrefetchScalarGridSpec(
            num_scalar_prefetch=1,
            grid=(1,),
            in_specs=[pl.BlockSpec(pieces.shape, lambda i, *_: (0,) * pieces.ndim)],
            out_specs=pl.BlockSpec(memory_space=pl.ANY),
            scratch_shapes=[pltpu.SemaphoreType.DMA((count,))],
        ),
        compiler_params=pltpu.CompilerParams(vmem_limit_bytes=VMEM_BYTES),
        cost_estimate=pl.CostEstimate(flops=0, bytes_accessed=8 * pieces.size, transcendentals=0),
    )(chosen, pieces)


LANES = 128


def join_kernel(steps, place, ego, arrived, present, wq, wkv, wout, scale, out, top_row, low_row, landed, joined, sems):
    step = pl.program_id(0)
    agents, total, channels = landed.shape
    here = total // steps
    cells = arrived.shape[1]
    pieces = total // cells
    part = pieces // steps

    def copy(i, source):
        a, q = i // pieces, i % pieces
        start = pl.multiple_of(q * cells, 16)
        return pltpu.make_async_copy(arrived.at[source], landed.at[a, pl.ds(start, cells), :], sems.at[i])

    @pl.when(step == 0)
    def _():
        lax.fori_loop(0, agents * pieces, lambda i, _: (copy(i, place[i]).start(), 0)[1], 0)

    def wait(i, _):
        copy(i // part * pieces + step * part + i % part, 0).wait()
        return 0

    lax.fori_loop(0, agents * part, wait, 0)
    heads = channels // HEAD
    scale_col = scale[...].reshape(heads, 1, 1)
    for c in range(here // LANES):
        span = pl.ds(c * LANES, LANES)
        cells_here = ego[span, :]
        queries = dot(wq[...], cells_here, NT)
        factor = lax.rsqrt(head_sums(queries * queries) + unit_eps) * scale_col

        def agent(x):
            kv = dot(wkv[...], x, NT).astype(jnp.bfloat16).astype(jnp.float32)
            keys, values = kv[:channels], kv[channels:]
            score = head_sums(queries * keys) * factor
            return score * lax.rsqrt(head_sums(keys * keys) + unit_eps), values

        scores, values = zip(
            agent(cells_here),
            *(
                agent(landed[a, pl.ds(pl.multiple_of(step * here + c * LANES, LANES), LANES), :])
                for a in range(agents)
            ),
        )
        scores = [scores[0]] + [
            jnp.where(present[a : a + 1, c * LANES : (c + 1) * LANES].reshape(1, 1, LANES) > 0, s, -1e30)
            for a, s in enumerate(scores[1:])
        ]
        top = functools.reduce(jnp.maximum, scores)
        weights = [jnp.exp(s - top) for s in scores]
        inverse = 1.0 / functools.reduce(jnp.add, weights)
        mix = functools.reduce(jnp.add, [by_head(v, w * inverse) for w, v in zip(weights, values)])
        joined[span, :] = dot(mix.astype(jnp.bfloat16), wout[...], TN)
    out[...] = joined[...].astype(jnp.bfloat16)
    rows = here // top_row.shape[0]
    top_row[...] = joined[pl.ds(0, here // rows, stride=rows), :].astype(jnp.bfloat16)
    low_row[...] = joined[pl.ds(rows - 1, here // rows, stride=rows), :].astype(jnp.bfloat16)


def join_agents(pieces, arrived, place, live, wq, wkv, wout, scale):
    count, cols, rows, channels = pieces.shape
    agents = live.shape[0]
    cells = cols * rows
    total = count * cells
    steps = 2
    whole = lambda x: pl.BlockSpec(x.shape, lambda r, *_: (0,) * x.ndim)
    block = lambda n: pl.BlockSpec((n // steps, channels), lambda r, *_: (r, 0))
    weights = (wq.T, wkv.T, wout, scale.reshape(-1, 1))
    present = jnp.repeat(live.astype(jnp.float32), cells, axis=1)
    like = lambda n: jax.ShapeDtypeStruct((n, channels), jnp.bfloat16)
    return pl.pallas_call(
        functools.partial(join_kernel, steps),
        out_shape=[like(total), like(total // rows), like(total // rows)],
        grid_spec=pltpu.PrefetchScalarGridSpec(
            num_scalar_prefetch=1,
            grid=(steps,),
            in_specs=[
                block(total),
                pl.BlockSpec(memory_space=pl.ANY),
                pl.BlockSpec((agents, total // steps), lambda r, *_: (0, r)),
            ]
            + [whole(w) for w in weights],
            out_specs=[block(total), block(total // rows), block(total // rows)],
            scratch_shapes=[
                pltpu.VMEM((agents, total, channels), jnp.bfloat16),
                pltpu.VMEM((total // steps, channels), jnp.float32),
                pltpu.SemaphoreType.DMA((agents * count,)),
            ],
        ),
        compiler_params=pltpu.CompilerParams(vmem_limit_bytes=VMEM_BYTES),
        cost_estimate=pl.CostEstimate(
            flops=total * channels * channels * 40, bytes_accessed=total * channels * 12, transcendentals=total * 20
        ),
    )(
        place.reshape(-1),
        pieces.reshape(total, channels),
        arrived.reshape(-1, cells, channels),
        present,
        *weights,
    )


def norm(x, gain):
    average = jnp.mean(x, axis=-1, keepdims=True)
    centred = x - average
    spread = jnp.mean(centred * centred, axis=-1, keepdims=True)
    return (centred * lax.rsqrt(spread + norm_eps) * gain).astype(jnp.bfloat16)


def spread_rows(ref, rows_of, at, rows):
    count, channels = rows_of.shape
    ref[pl.ds(at, count, stride=rows), :] = rows_of.astype(jnp.float32)
    return ref[: count * rows].reshape(count, rows, channels)


def runs_of(phase, tile_cols, whole_map, pieces):
    run = TILE // PHASES
    out = []
    for t in range(tile_cols):
        first = t * TILE + phase * run - 1
        if pieces is None:
            last = first + run + 2
            blank = jnp.zeros_like(whole_map[:1])
            body = whole_map[max(first, 0) : min(last, tile_cols * TILE)]
            parts = ([blank] if first < 0 else []) + [body] + ([blank] if last > tile_cols * TILE else [])
        else:
            size = run + 2
            one = pieces[0]
            blank = jnp.zeros_like(one[:1])
            if phase == 0:
                left = one[(t - 1) * size : (t - 1) * size + 1] if t else blank
                parts = [left, one[t * size + 1 : (t + 1) * size]]
            else:
                rest = TILE - size
                right = one[(t + 1) * size + 1 : (t + 1) * size + 2] if t + 1 < tile_cols else blank
                parts = [
                    one[t * size + run : (t + 1) * size],
                    pieces[1][t * rest : (t + 1) * rest],
                    one[t * size : t * size + 1],
                    right,
                ]
        out.append(jnp.concatenate(parts, axis=0))
    return out


def taps_of(runs, above, below, taps):
    out = []
    for x, first, last in zip(runs, above, below):
        cols, rows, channels = x.shape
        row = lax.broadcasted_iota(jnp.int32, (rows, channels), 0)[None]
        flat = x.reshape(cols * rows, channels)
        over = jnp.where(row == 0, first, pltpu.roll(flat, 1, 0).reshape(x.shape))
        under = jnp.where(row == rows - 1, last, pltpu.roll(flat, cols * rows - 1, 0).reshape(x.shape))
        total = x[1 : cols - 1]
        for j in range(3):
            span = slice(j, cols - 2 + j)
            total = total + over[span] * taps[j] + x[span] * taps[3 + j] + under[span] * taps[6 + j]
        out.append(total.reshape((cols - 2) * rows, channels))
    return out


def window_kernel(phase, rows, *refs):
    ego, ego_up, ego_down, refs = *refs[:3], refs[3:]
    pieces, refs = [refs[3 * p : 3 * p + 3] for p in range(phase + 1)], refs[3 * phase + 3 :]
    taps, gain_one, wq, wk, wv, wo, scale, gain_two, up, down = refs[:10]
    out, mixed_ref, result_ref, halo = refs[10 + phase :]
    group_size, cols, _, channels = ego.shape
    tile_cols = cols // TILE
    run = TILE // PHASES
    width = 2 * channels
    in_window = rows * WIN
    here = tile_cols * run * rows
    cells = group_size * here
    windows = cells // in_window
    heads = width // HEAD
    f32 = jnp.float32
    for v in range(group_size):
        for half in range(2):
            lanes = slice(half * channels, (half + 1) * channels)
            weights = [taps[i : i + 1, lanes].reshape(1, 1, channels) for i in range(9)]
            if half == 0:
                centre = runs_of(phase, tile_cols, ego[v].astype(f32), None)
                above = runs_of(phase, tile_cols, spread_rows(halo.at[0], ego_up[v, 0], 0, rows), None)
                below = runs_of(phase, tile_cols, spread_rows(halo.at[1], ego_down[v, 0], rows - 1, rows), None)
            else:
                centre, above, below = [], [], []
                for p, (x, first, last) in enumerate(pieces):
                    centre.append(x[v].astype(f32).reshape(-1, rows, channels))
                    above.append(spread_rows(halo.at[2 + 2 * p], first[v], 0, rows))
                    below.append(spread_rows(halo.at[3 + 2 * p], last[v], rows - 1, rows))
                centre, above, below = (runs_of(phase, tile_cols, None, x) for x in (centre, above, below))
            for t, part in enumerate(taps_of(centre, above, below, weights)):
                at = v * here + t * run * rows
                mixed_ref[at : at + run * rows, lanes] = part
    hidden = norm(mixed_ref[...], gain_one[...])
    queries = dot(wq[...], hidden, NT)
    values = dot(wv[...], hidden, NT).astype(jnp.bfloat16)
    keys = dot(hidden, wk[...])
    factor = lax.rsqrt(head_sums(queries * queries) + unit_eps) * scale[...].reshape(heads, 1, 1)
    queries = by_head(queries, factor)
    member = (
        lax.broadcasted_iota(jnp.int32, (width, width), 0) // HEAD
        == lax.broadcasted_iota(jnp.int32, (width, width), 1) // HEAD
    ).astype(f32).astype(jnp.bfloat16)
    square_high, square_low = split(keys * keys)
    keys = keys * lax.rsqrt(dot(square_high, member) + dot(square_low, member) + unit_eps)
    key_high, key_low = split(keys)

    pair = 2 * in_window
    group = 4 * HEAD
    lane = lax.broadcasted_iota(jnp.int32, (width, pair), 1) < in_window
    even = (lax.broadcasted_iota(jnp.int32, (width, pair), 0) // HEAD) % 2 == 0
    blank = jnp.zeros((2 * HEAD, pair), jnp.bfloat16)
    blank_p = jnp.zeros((in_window, 4 * in_window), jnp.bfloat16)
    lane_head = lax.broadcasted_iota(jnp.int32, (HEAD, pair), 1) < in_window
    attended = []
    for p in range(windows // 2):
        straight = queries[:, p * pair : (p + 1) * pair]
        turned = pltpu.roll(straight, in_window, 1)
        blocks = []
        for w in range(2):
            low, high = (straight, turned) if w == 0 else (turned, straight)
            blocks.append(split(jnp.where(even, jnp.where(lane, low, 0.0), jnp.where(lane, 0.0, high))))
        parts = []
        for g in range(width // group):
            channels_of = slice(g * group, (g + 1) * group)
            probs = []
            for w in range(2):
                at = (2 * p + w) * in_window
                k_high = key_high[at : at + in_window, channels_of]
                k_low = key_low[at : at + in_window, channels_of]

                def right(block):
                    block = block[channels_of]
                    return jnp.concatenate(
                        [
                            jnp.concatenate([block[: 2 * HEAD], blank], axis=1),
                            jnp.concatenate([blank, block[2 * HEAD :]], axis=1),
                        ],
                        axis=0,
                    )

                first = dot(jnp.concatenate([k_high, k_low], axis=0), right(blocks[w][0]))
                score = first[:in_window] + first[in_window:] + dot(k_high, right(blocks[w][1]))
                weight = jnp.exp2(score - jnp.max(score, axis=0, keepdims=True))
                weight = weight * (1.0 / jnp.sum(weight, axis=0, keepdims=True))
                weight = weight.astype(jnp.bfloat16)
                probs.append(
                    jnp.concatenate([weight, blank_p] if w == 0 else [blank_p, weight], axis=0)
                )
            v = values[channels_of, p * pair : (p + 1) * pair]
            first, second = dot(v, probs[0]), dot(v, probs[1])
            for h in range(4):
                rows_of = slice(h * HEAD, (h + 1) * HEAD)
                cols_of = slice((h // 2) * pair, (h // 2 + 1) * pair)
                a, b = first[rows_of, cols_of], second[rows_of, cols_of]
                if h % 2 == 0:
                    b = pltpu.roll(b, in_window, 1)
                else:
                    a = pltpu.roll(a, in_window, 1)
                parts.append(jnp.where(lane_head, a, b))
        attended.append(jnp.concatenate(parts, axis=0).astype(jnp.bfloat16))
    attended = jnp.concatenate(attended, axis=1)
    mixed = mixed_ref[...] + dot(attended, wo[...], TN)
    hidden = norm(mixed, gain_two[...])
    inner = dot(hidden, up[...])
    inner = (0.5 * inner * (1.0 + jnp.tanh(0.5 * inner))).astype(jnp.bfloat16)
    result = mixed + dot(inner, down[...])
    for half in range(2):
        result_ref[half] = result[:, half * channels : (half + 1) * channels]
    for v in range(group_size):
        for t in range(tile_cols):
            for i in range(rows):
                at = v * here + t * run * rows + i
                for half in range(2):
                    lanes = slice(half * channels, (half + 1) * channels)
                    line = result_ref[half, pl.ds(at, run, stride=rows), :]
                    out[v, i, t, :, lanes] = line.astype(jnp.bfloat16)


def window_layer(phase, turned, ego_edges, pieces, before, conv_weight, gain_first, window_in, window_out,
                 window_scale, gain_second, hidden_up, hidden_down):
    vehicles, cols, rows, channels = turned.shape
    width = 2 * channels
    tile_cols = cols // TILE
    run = TILE // PHASES
    group = 2
    whole = lambda x: pl.BlockSpec(x.shape, lambda r: (0,) * x.ndim)
    block = lambda *shape: pl.BlockSpec((group, *shape), lambda r: (r,) + (0,) * len(shape))
    weights = (
        conv_weight.reshape(9, width),
        gain_first[None],
        window_in[:, :width].T,
        window_in[:, width : 2 * width],
        window_in[:, 2 * width :].T,
        window_out,
        (window_scale * LOG2E).reshape(-1, 1),
        gain_second[None],
        hidden_up,
        hidden_down,
    )
    pieces = [x.reshape(vehicles, -1, channels) for three in pieces for x in three]
    cells = vehicles * rows * tile_cols * run
    most = cols * rows
    operands = (turned, *ego_edges, *pieces, *weights)
    in_specs = (
        [block(cols, rows, channels)]
        + [block(1, cols, channels)] * 2
        + [block(*x.shape[1:]) for x in pieces]
        + [whole(w) for w in weights]
    )
    aliases = {}
    if before is not None:
        aliases = {len(operands): 0}
        operands += (before,)
        in_specs += [pl.BlockSpec(memory_space=pl.ANY)]
    return pl.pallas_call(
        functools.partial(window_kernel, phase, rows),
        out_shape=jax.ShapeDtypeStruct((vehicles, rows, tile_cols, PHASES, run, width), jnp.bfloat16),
        grid=(vehicles // group,),
        in_specs=in_specs,
        out_specs=pl.BlockSpec(
            (group, rows, tile_cols, None, run, width), lambda r: (r, 0, 0, phase, 0, 0)
        ),
        scratch_shapes=[
            pltpu.VMEM((group * rows * tile_cols * run, width), jnp.float32),
            pltpu.VMEM((2, group * rows * tile_cols * run, channels), jnp.float32),
            pltpu.VMEM((2 * PHASES + 2, most, channels), jnp.float32),
        ],
        input_output_aliases=aliases,
        compiler_params=pltpu.CompilerParams(vmem_limit_bytes=VMEM_BYTES),
        cost_estimate=pl.CostEstimate(
            flops=cells * width * width * 60, bytes_accessed=cells * width * 6, transcendentals=cells * width * 4
        ),
    )(*operands)


def beside(last, first):
    count = lax.axis_size("row")
    above = lax.ppermute(last, "row", [(i, i + 1) for i in range(count - 1)])
    below = lax.ppermute(first, "row", [(i + 1, i) for i in range(count - 1)])
    return above, below


def tables(vehicles_here, tile_cols, senders, shifts, counts):
    agents = senders.shape[1]
    devices = lax.axis_size("veh")
    myself = lax.axis_index("veh")
    pairs = vehicles_here * agents
    capacity = tile_cols * max(1, pairs // devices)
    send_all = senders.reshape(devices, pairs)
    shift_all = shifts.reshape(devices, pairs)
    live_all = (jnp.arange(agents)[None, :] < counts[:, None]).reshape(devices, pairs)
    tiles_all = jnp.where(live_all, tile_cols - jnp.abs(shift_all), 0)
    source_all = send_all // vehicles_here
    same = source_all[:, :, None] == source_all[:, None, :]
    before = jnp.arange(pairs)[None, :] < jnp.arange(pairs)[:, None]
    start_all = jnp.sum(jnp.where(same & before[None], tiles_all[:, None, :], 0), axis=2)
    step = jnp.arange(tile_cols, dtype=jnp.int32)
    tile_of = (
        (send_all % vehicles_here * tile_cols + jnp.maximum(shift_all, 0))[:, :, None] + step
    ).reshape(devices, pairs * tile_cols)
    slot_of = jnp.where(
        ((source_all == myself)[:, :, None]) & (step < tiles_all[:, :, None]),
        start_all[:, :, None] + step,
        -1,
    ).reshape(devices, pairs * tile_cols)
    hit = slot_of[:, None, :] == jnp.arange(capacity)[None, :, None]
    chosen = jnp.sum(jnp.where(hit, tile_of[:, None, :], 0), axis=2).reshape(-1)
    shifted = step + shift_all[myself][:, None]
    inside = (shifted >= 0) & (shifted < tile_cols) & live_all[myself][:, None]
    place = (
        (source_all[myself] * capacity + start_all[myself])[:, None]
        + step
        - jnp.maximum(-shift_all[myself], 0)[:, None]
    )
    place = jnp.where(inside, place, 0)
    by_agent = lambda x: jnp.swapaxes(x.reshape(vehicles_here, agents, tile_cols), 0, 1).reshape(agents, -1)
    return chosen.astype(jnp.int32), by_agent(place.astype(jnp.int32)), by_agent(inside)


def on_device(
    bev_maps,
    senders,
    shifts,
    counts,
    agent_query,
    agent_keyvalue,
    agent_out,
    agent_scale,
    conv_weight,
    gain_first,
    window_in,
    window_out,
    window_scale,
    gain_second,
    hidden_up,
    hidden_down,
):
    vehicles_here, rows, cols, channels = bev_maps.shape
    devices = lax.axis_size("veh")
    chosen, place, live = tables(vehicles_here, cols // TILE, senders, shifts, counts)
    turned, first, second, packed = turn_maps(bev_maps, chosen)
    ego_edges = beside(bev_maps[:, rows - 1 :], bev_maps[:, :1])

    def travel(x):
        x = x.reshape(devices, -1, *x.shape[1:])
        x = lax.all_to_all(x, "veh", 0, 0, tiled=True)
        return x.reshape(-1, *x.shape[2:])

    arrived = [travel(packed)]
    later = pack_tiles(second, chosen)
    arrived[0], later = lax.optimization_barrier((arrived[0], later))
    arrived.append(travel(later))
    result, pieces = None, []
    for phase, own in enumerate((first, second)):
        joined, top, low = join_agents(
            own, arrived[phase], place, live, agent_query, agent_keyvalue, agent_out, agent_scale
        )
        pieces.append((joined, *beside(low, top)))
        result = window_layer(
            phase,
            turned,
            ego_edges,
            pieces,
            result,
            conv_weight,
            gain_first,
            window_in,
            window_out,
            window_scale,
            gain_second,
            hidden_up,
            hidden_down,
        )
    return result.reshape(vehicles_here, rows, cols, 2 * channels)


def solution(mesh):
    split_maps = P("veh", "row", None, None)
    return jax.shard_map(
        on_device,
        mesh=mesh,
        in_specs=(split_maps,) + (P(),) * 15,
        out_specs=split_maps,
        check_vma=False,
    )
```

```python
import functools
import math

import jax
import jax.numpy as jnp
from jax import lax
from jax.experimental import pallas as pl
from jax.experimental.pallas import tpu as pltpu
from jax.sharding import PartitionSpec as P

TILE = 32
WIN = 8
HEAD = 32

norm_eps = 1e-05
unit_eps = 1e-06
LOG2E = math.log2(math.e)
VMEM_BYTES = 48 * 2**20
PHASES = 2

NN = (((1,), (0,)), ((), ()))
NT = (((1,), (1,)), ((), ()))
TN = (((0,), (0,)), ((), ()))


def dot(a, b, dims=NN):
    return lax.dot_general(a, b, dims, preferred_element_type=jnp.float32)


def split(x):
    high = x.astype(jnp.bfloat16)
    return high, (x - high.astype(jnp.float32)).astype(jnp.bfloat16)


def head_sums(x):
    return jnp.sum(x.reshape(x.shape[0] // HEAD, HEAD, x.shape[1]), axis=1, keepdims=True)


def by_head(x, factor):
    return (x.reshape(x.shape[0] // HEAD, HEAD, x.shape[1]) * factor).reshape(x.shape)


def phase_columns(phase):
    run = TILE // PHASES
    return [TILE - 1] + list(range(run + 1)) if phase == 0 else list(range(run + 1, TILE - 1))


def copy_tiles(chosen, pieces, packed, sems):
    def start(i, _):
        pltpu.make_async_copy(pieces.at[chosen[i]], packed.at[i], sems.at[i]).start()
        return 0

    def finish(i, _):
        pltpu.make_async_copy(pieces.at[0], packed.at[i], sems.at[i]).wait()
        return 0

    count = packed.shape[0]
    lax.fori_loop(0, count, start, 0)
    lax.fori_loop(0, count, finish, 0)


def turn_kernel(chosen, maps, turned, first, second, packed, scratch, sems):
    vehicles, rows, cols, channels = maps.shape
    tile_cols = cols // TILE
    run = TILE // PHASES

    def vehicle(v, _):
        for i in range(rows):
            scratch[pl.ds(i, cols, stride=rows), :] = maps[v, i].astype(jnp.float32)
        x = scratch[...].astype(jnp.bfloat16).reshape(cols, rows, channels)
        turned[v] = x
        for t in range(tile_cols):
            at = v * tile_cols + t
            tile = x[t * TILE : (t + 1) * TILE]
            first[at] = jnp.concatenate([tile[TILE - 1 :], tile[: run + 1]], axis=0)
            second[at] = tile[run + 1 : TILE - 1]
        return 0

    lax.fori_loop(0, vehicles, vehicle, 0)
    copy_tiles(chosen, first, packed, sems)


def turn_maps(maps, chosen):
    vehicles, rows, cols, channels = maps.shape
    tiles = vehicles * (cols // TILE)
    count = chosen.shape[0]
    pieces = [(tiles, len(phase_columns(p)), rows, channels) for p in range(PHASES)]
    shapes = [(vehicles, cols, rows, channels), *pieces, (count, *pieces[0][1:])]
    whole = lambda shape: pl.BlockSpec(shape, lambda i, *_: (0,) * len(shape))
    return pl.pallas_call(
        turn_kernel,
        out_shape=[jax.ShapeDtypeStruct(shape, maps.dtype) for shape in shapes],
        grid_spec=pltpu.PrefetchScalarGridSpec(
            num_scalar_prefetch=1,
            grid=(1,),
            in_specs=[whole(maps.shape)],
            out_specs=[whole(shape) for shape in shapes[:3]] + [pl.BlockSpec(memory_space=pl.ANY)],
            scratch_shapes=[
                pltpu.VMEM((rows * cols, channels), jnp.float32),
                pltpu.SemaphoreType.DMA((count,)),
            ],
        ),
        compiler_params=pltpu.CompilerParams(vmem_limit_bytes=VMEM_BYTES),
        cost_estimate=pl.CostEstimate(flops=0, bytes_accessed=10 * maps.size, transcendentals=0),
    )(chosen, maps)


def pack_tiles(pieces, chosen):
    count = chosen.shape[0]
    return pl.pallas_call(
        copy_tiles,
        out_shape=jax.ShapeDtypeStruct((count, *pieces.shape[1:]), pieces.dtype),
        grid_spec=pltpu.PrefetchScalarGridSpec(
            num_scalar_prefetch=1,
            grid=(1,),
            in_specs=[pl.BlockSpec(pieces.shape, lambda i, *_: (0,) * pieces.ndim)],
            out_specs=pl.BlockSpec(memory_space=pl.ANY),
            scratch_shapes=[pltpu.SemaphoreType.DMA((count,))],
        ),
        compiler_params=pltpu.CompilerParams(vmem_limit_bytes=VMEM_BYTES),
        cost_estimate=pl.CostEstimate(flops=0, bytes_accessed=8 * pieces.size, transcendentals=0),
    )(chosen, pieces)


LANES = 128


def join_kernel(steps, place, ego, arrived, present, wq, wkv, wout, scale, out, top_row, low_row, landed, joined, sems):
    step = pl.program_id(0)
    agents, total, channels = landed.shape
    here = total // steps
    cells = arrived.shape[1]
    pieces = total // cells
    part = pieces // steps

    def copy(i, source):
        a, q = i // pieces, i % pieces
        start = pl.multiple_of(q * cells, 16)
        return pltpu.make_async_copy(arrived.at[source], landed.at[a, pl.ds(start, cells), :], sems.at[i])

    @pl.when(step == 0)
    def _():
        lax.fori_loop(0, agents * pieces, lambda i, _: (copy(i, place[i]).start(), 0)[1], 0)

    def wait(i, _):
        copy(i // part * pieces + step * part + i % part, 0).wait()
        return 0

    lax.fori_loop(0, agents * part, wait, 0)
    heads = channels // HEAD
    scale_col = scale[...].reshape(heads, 1, 1)
    for c in range(here // LANES):
        span = pl.ds(c * LANES, LANES)
        cells_here = ego[span, :]
        queries = dot(wq[...], cells_here, NT)
        factor = lax.rsqrt(head_sums(queries * queries) + unit_eps) * scale_col

        def agent(x):
            kv = dot(wkv[...], x, NT).astype(jnp.bfloat16).astype(jnp.float32)
            keys, values = kv[:channels], kv[channels:]
            score = head_sums(queries * keys) * factor
            return score * lax.rsqrt(head_sums(keys * keys) + unit_eps), values

        scores, values = zip(
            agent(cells_here),
            *(
                agent(landed[a, pl.ds(pl.multiple_of(step * here + c * LANES, LANES), LANES), :])
                for a in range(agents)
            ),
        )
        scores = [scores[0]] + [
            jnp.where(present[a : a + 1, c * LANES : (c + 1) * LANES].reshape(1, 1, LANES) > 0, s, -1e30)
            for a, s in enumerate(scores[1:])
        ]
        top = functools.reduce(jnp.maximum, scores)
        weights = [jnp.exp(s - top) for s in scores]
        inverse = 1.0 / functools.reduce(jnp.add, weights)
        mix = functools.reduce(jnp.add, [by_head(v, w * inverse) for w, v in zip(weights, values)])
        joined[span, :] = dot(mix.astype(jnp.bfloat16), wout[...], TN)
    out[...] = joined[...].astype(jnp.bfloat16)
    rows = here // top_row.shape[0]
    top_row[...] = joined[pl.ds(0, here // rows, stride=rows), :].astype(jnp.bfloat16)
    low_row[...] = joined[pl.ds(rows - 1, here // rows, stride=rows), :].astype(jnp.bfloat16)


def join_agents(pieces, arrived, place, live, wq, wkv, wout, scale):
    count, cols, rows, channels = pieces.shape
    agents = live.shape[0]
    cells = cols * rows
    total = count * cells
    steps = 2
    whole = lambda x: pl.BlockSpec(x.shape, lambda r, *_: (0,) * x.ndim)
    block = lambda n: pl.BlockSpec((n // steps, channels), lambda r, *_: (r, 0))
    weights = (wq.T, wkv.T, wout, scale.reshape(-1, 1))
    present = jnp.repeat(live.astype(jnp.float32), cells, axis=1)
    like = lambda n: jax.ShapeDtypeStruct((n, channels), jnp.bfloat16)
    return pl.pallas_call(
        functools.partial(join_kernel, steps),
        out_shape=[like(total), like(total // rows), like(total // rows)],
        grid_spec=pltpu.PrefetchScalarGridSpec(
            num_scalar_prefetch=1,
            grid=(steps,),
            in_specs=[
                block(total),
                pl.BlockSpec(memory_space=pl.ANY),
                pl.BlockSpec((agents, total // steps), lambda r, *_: (0, r)),
            ]
            + [whole(w) for w in weights],
            out_specs=[block(total), block(total // rows), block(total // rows)],
            scratch_shapes=[
                pltpu.VMEM((agents, total, channels), jnp.bfloat16),
                pltpu.VMEM((total // steps, channels), jnp.float32),
                pltpu.SemaphoreType.DMA((agents * count,)),
            ],
        ),
        compiler_params=pltpu.CompilerParams(vmem_limit_bytes=VMEM_BYTES),
        cost_estimate=pl.CostEstimate(
            flops=total * channels * channels * 40, bytes_accessed=total * channels * 12, transcendentals=total * 20
        ),
    )(
        place.reshape(-1),
        pieces.reshape(total, channels),
        arrived.reshape(-1, cells, channels),
        present,
        *weights,
    )


def norm(x, gain):
    average = jnp.mean(x, axis=-1, keepdims=True)
    centred = x - average
    spread = jnp.mean(centred * centred, axis=-1, keepdims=True)
    return (centred * lax.rsqrt(spread + norm_eps) * gain).astype(jnp.bfloat16)


def spread_rows(ref, rows_of, at, rows):
    count, channels = rows_of.shape
    ref[pl.ds(at, count, stride=rows), :] = rows_of.astype(jnp.float32)
    return ref[: count * rows].reshape(count, rows, channels)


def runs_of(phase, tile_cols, whole_map, pieces):
    run = TILE // PHASES
    out = []
    for t in range(tile_cols):
        first = t * TILE + phase * run - 1
        if pieces is None:
            last = first + run + 2
            blank = jnp.zeros_like(whole_map[:1])
            body = whole_map[max(first, 0) : min(last, tile_cols * TILE)]
            parts = ([blank] if first < 0 else []) + [body] + ([blank] if last > tile_cols * TILE else [])
        else:
            size = run + 2
            one = pieces[0]
            blank = jnp.zeros_like(one[:1])
            if phase == 0:
                left = one[(t - 1) * size : (t - 1) * size + 1] if t else blank
                parts = [left, one[t * size + 1 : (t + 1) * size]]
            else:
                rest = TILE - size
                right = one[(t + 1) * size + 1 : (t + 1) * size + 2] if t + 1 < tile_cols else blank
                parts = [
                    one[t * size + run : (t + 1) * size],
                    pieces[1][t * rest : (t + 1) * rest],
                    one[t * size : t * size + 1],
                    right,
                ]
        out.append(jnp.concatenate(parts, axis=0))
    return out


def taps_of(runs, above, below, taps):
    out = []
    for x, first, last in zip(runs, above, below):
        cols, rows, channels = x.shape
        row = lax.broadcasted_iota(jnp.int32, (rows, channels), 0)[None]
        flat = x.reshape(cols * rows, channels)
        over = jnp.where(row == 0, first, pltpu.roll(flat, 1, 0).reshape(x.shape))
        under = jnp.where(row == rows - 1, last, pltpu.roll(flat, cols * rows - 1, 0).reshape(x.shape))
        total = x[1 : cols - 1]
        for j in range(3):
            span = slice(j, cols - 2 + j)
            total = total + over[span] * taps[j] + x[span] * taps[3 + j] + under[span] * taps[6 + j]
        out.append(total.reshape((cols - 2) * rows, channels))
    return out


def window_kernel(phase, rows, *refs):
    ego, ego_up, ego_down, refs = *refs[:3], refs[3:]
    pieces, refs = [refs[3 * p : 3 * p + 3] for p in range(phase + 1)], refs[3 * phase + 3 :]
    taps, gain_one, wq, wk, wv, wo, scale, gain_two, up, down = refs[:10]
    out, mixed_ref, result_ref, halo = refs[10 + phase :]
    group_size, cols, _, channels = ego.shape
    tile_cols = cols // TILE
    run = TILE // PHASES
    width = 2 * channels
    in_window = rows * WIN
    here = tile_cols * run * rows
    cells = group_size * here
    windows = cells // in_window
    heads = width // HEAD
    f32 = jnp.float32
    for v in range(group_size):
        for half in range(2):
            lanes = slice(half * channels, (half + 1) * channels)
            weights = [taps[i : i + 1, lanes].reshape(1, 1, channels) for i in range(9)]
            if half == 0:
                centre = runs_of(phase, tile_cols, ego[v].astype(f32), None)
                above = runs_of(phase, tile_cols, spread_rows(halo.at[0], ego_up[v, 0], 0, rows), None)
                below = runs_of(phase, tile_cols, spread_rows(halo.at[1], ego_down[v, 0], rows - 1, rows), None)
            else:
                centre, above, below = [], [], []
                for p, (x, first, last) in enumerate(pieces):
                    centre.append(x[v].astype(f32).reshape(-1, rows, channels))
                    above.append(spread_rows(halo.at[2 + 2 * p], first[v], 0, rows))
                    below.append(spread_rows(halo.at[3 + 2 * p], last[v], rows - 1, rows))
                centre, above, below = (runs_of(phase, tile_cols, None, x) for x in (centre, above, below))
            for t, part in enumerate(taps_of(centre, above, below, weights)):
                at = v * here + t * run * rows
                mixed_ref[at : at + run * rows, lanes] = part
    hidden = norm(mixed_ref[...], gain_one[...])
    queries = dot(wq[...], hidden, NT)
    values = dot(wv[...], hidden, NT).astype(jnp.bfloat16)
    keys = dot(hidden, wk[...])
    factor = lax.rsqrt(head_sums(queries * queries) + unit_eps) * scale[...].reshape(heads, 1, 1)
    queries = by_head(queries, factor)
    member = (
        lax.broadcasted_iota(jnp.int32, (width, width), 0) // HEAD
        == lax.broadcasted_iota(jnp.int32, (width, width), 1) // HEAD
    ).astype(f32).astype(jnp.bfloat16)
    square_high, square_low = split(keys * keys)
    keys = keys * lax.rsqrt(dot(square_high, member) + dot(square_low, member) + unit_eps)
    key_high, key_low = split(keys)

    pair = 2 * in_window
    group = 4 * HEAD
    lane = lax.broadcasted_iota(jnp.int32, (width, pair), 1) < in_window
    even = (lax.broadcasted_iota(jnp.int32, (width, pair), 0) // HEAD) % 2 == 0
    blank = jnp.zeros((2 * HEAD, pair), jnp.bfloat16)
    blank_p = jnp.zeros((in_window, 4 * in_window), jnp.bfloat16)
    lane_head = lax.broadcasted_iota(jnp.int32, (HEAD, pair), 1) < in_window
    attended = []
    for p in range(windows // 2):
        straight = queries[:, p * pair : (p + 1) * pair]
        turned = pltpu.roll(straight, in_window, 1)
        blocks = []
        for w in range(2):
            low, high = (straight, turned) if w == 0 else (turned, straight)
            blocks.append(split(jnp.where(even, jnp.where(lane, low, 0.0), jnp.where(lane, 0.0, high))))
        parts = []
        for g in range(width // group):
            channels_of = slice(g * group, (g + 1) * group)
            probs = []
            for w in range(2):
                at = (2 * p + w) * in_window
                k_high = key_high[at : at + in_window, channels_of]
                k_low = key_low[at : at + in_window, channels_of]

                def right(block):
                    block = block[channels_of]
                    return jnp.concatenate(
                        [
                            jnp.concatenate([block[: 2 * HEAD], blank], axis=1),
                            jnp.concatenate([blank, block[2 * HEAD :]], axis=1),
                        ],
                        axis=0,
                    )

                first = dot(jnp.concatenate([k_high, k_low], axis=0), right(blocks[w][0]))
                score = first[:in_window] + first[in_window:] + dot(k_high, right(blocks[w][1]))
                weight = jnp.exp2(score - jnp.max(score, axis=0, keepdims=True))
                weight = weight * (1.0 / jnp.sum(weight, axis=0, keepdims=True))
                weight = weight.astype(jnp.bfloat16)
                probs.append(
                    jnp.concatenate([weight, blank_p] if w == 0 else [blank_p, weight], axis=0)
                )
            v = values[channels_of, p * pair : (p + 1) * pair]
            first, second = dot(v, probs[0]), dot(v, probs[1])
            for h in range(4):
                rows_of = slice(h * HEAD, (h + 1) * HEAD)
                cols_of = slice((h // 2) * pair, (h // 2 + 1) * pair)
                a, b = first[rows_of, cols_of], second[rows_of, cols_of]
                if h % 2 == 0:
                    b = pltpu.roll(b, in_window, 1)
                else:
                    a = pltpu.roll(a, in_window, 1)
                parts.append(jnp.where(lane_head, a, b))
        attended.append(jnp.concatenate(parts, axis=0).astype(jnp.bfloat16))
    attended = jnp.concatenate(attended, axis=1)
    mixed = mixed_ref[...] + dot(attended, wo[...], TN)
    hidden = norm(mixed, gain_two[...])
    inner = dot(hidden, up[...])
    inner = (0.5 * inner * (1.0 + jnp.tanh(0.5 * inner))).astype(jnp.bfloat16)
    result = mixed + dot(inner, down[...])
    for half in range(2):
        result_ref[half] = result[:, half * channels : (half + 1) * channels]
    for v in range(group_size):
        for t in range(tile_cols):
            for i in range(rows):
                at = v * here + t * run * rows + i
                for half in range(2):
                    lanes = slice(half * channels, (half + 1) * channels)
                    line = result_ref[half, pl.ds(at, run, stride=rows), :]
                    out[v, i, t, :, lanes] = line.astype(jnp.bfloat16)


def window_layer(phase, turned, ego_edges, pieces, before, conv_weight, gain_first, window_in, window_out,
                 window_scale, gain_second, hidden_up, hidden_down):
    vehicles, cols, rows, channels = turned.shape
    width = 2 * channels
    tile_cols = cols // TILE
    run = TILE // PHASES
    group = 2
    whole = lambda x: pl.BlockSpec(x.shape, lambda r: (0,) * x.ndim)
    block = lambda *shape: pl.BlockSpec((group, *shape), lambda r: (r,) + (0,) * len(shape))
    weights = (
        conv_weight.reshape(9, width),
        gain_first[None],
        window_in[:, :width].T,
        window_in[:, width : 2 * width],
        window_in[:, 2 * width :].T,
        window_out,
        (window_scale * LOG2E).reshape(-1, 1),
        gain_second[None],
        hidden_up,
        hidden_down,
    )
    pieces = [x.reshape(vehicles, -1, channels) for three in pieces for x in three]
    cells = vehicles * rows * tile_cols * run
    most = cols * rows
    operands = (turned, *ego_edges, *pieces, *weights)
    in_specs = (
        [block(cols, rows, channels)]
        + [block(1, cols, channels)] * 2
        + [block(*x.shape[1:]) for x in pieces]
        + [whole(w) for w in weights]
    )
    aliases = {}
    if before is not None:
        aliases = {len(operands): 0}
        operands += (before,)
        in_specs += [pl.BlockSpec(memory_space=pl.ANY)]
    return pl.pallas_call(
        functools.partial(window_kernel, phase, rows),
        out_shape=jax.ShapeDtypeStruct((vehicles, rows, tile_cols, PHASES, run, width), jnp.bfloat16),
        grid=(vehicles // group,),
        in_specs=in_specs,
        out_specs=pl.BlockSpec(
            (group, rows, tile_cols, None, run, width), lambda r: (r, 0, 0, phase, 0, 0)
        ),
        scratch_shapes=[
            pltpu.VMEM((group * rows * tile_cols * run, width), jnp.float32),
            pltpu.VMEM((2, group * rows * tile_cols * run, channels), jnp.float32),
            pltpu.VMEM((2 * PHASES + 2, most, channels), jnp.float32),
        ],
        input_output_aliases=aliases,
        compiler_params=pltpu.CompilerParams(vmem_limit_bytes=VMEM_BYTES),
        cost_estimate=pl.CostEstimate(
            flops=cells * width * width * 60, bytes_accessed=cells * width * 6, transcendentals=cells * width * 4
        ),
    )(*operands)


def beside(last, first):
    count = lax.axis_size("row")
    above = lax.ppermute(last, "row", [(i, i + 1) for i in range(count - 1)])
    below = lax.ppermute(first, "row", [(i + 1, i) for i in range(count - 1)])
    return above, below


def tables(vehicles_here, tile_cols, senders, shifts, counts):
    agents = senders.shape[1]
    devices = lax.axis_size("veh")
    myself = lax.axis_index("veh")
    pairs = vehicles_here * agents
    capacity = tile_cols * max(1, pairs // devices)
    send_all = senders.reshape(devices, pairs)
    shift_all = shifts.reshape(devices, pairs)
    live_all = (jnp.arange(agents)[None, :] < counts[:, None]).reshape(devices, pairs)
    tiles_all = jnp.where(live_all, tile_cols - jnp.abs(shift_all), 0)
    source_all = send_all // vehicles_here
    same = source_all[:, :, None] == source_all[:, None, :]
    before = jnp.arange(pairs)[None, :] < jnp.arange(pairs)[:, None]
    start_all = jnp.sum(jnp.where(same & before[None], tiles_all[:, None, :], 0), axis=2)
    step = jnp.arange(tile_cols, dtype=jnp.int32)
    tile_of = (
        (send_all % vehicles_here * tile_cols + jnp.maximum(shift_all, 0))[:, :, None] + step
    ).reshape(devices, pairs * tile_cols)
    slot_of = jnp.where(
        ((source_all == myself)[:, :, None]) & (step < tiles_all[:, :, None]),
        start_all[:, :, None] + step,
        -1,
    ).reshape(devices, pairs * tile_cols)
    hit = slot_of[:, None, :] == jnp.arange(capacity)[None, :, None]
    chosen = jnp.sum(jnp.where(hit, tile_of[:, None, :], 0), axis=2).reshape(-1)
    shifted = step + shift_all[myself][:, None]
    inside = (shifted >= 0) & (shifted < tile_cols) & live_all[myself][:, None]
    place = (
        (source_all[myself] * capacity + start_all[myself])[:, None]
        + step
        - jnp.maximum(-shift_all[myself], 0)[:, None]
    )
    place = jnp.where(inside, place, 0)
    by_agent = lambda x: jnp.swapaxes(x.reshape(vehicles_here, agents, tile_cols), 0, 1).reshape(agents, -1)
    return chosen.astype(jnp.int32), by_agent(place.astype(jnp.int32)), by_agent(inside)


def on_device(
    bev_maps,
    senders,
    shifts,
    counts,
    agent_query,
    agent_keyvalue,
    agent_out,
    agent_scale,
    conv_weight,
    gain_first,
    window_in,
    window_out,
    window_scale,
    gain_second,
    hidden_up,
    hidden_down,
):
    vehicles_here, rows, cols, channels = bev_maps.shape
    devices = lax.axis_size("veh")
    chosen, place, live = tables(vehicles_here, cols // TILE, senders, shifts, counts)
    turned, first, second, packed = turn_maps(bev_maps, chosen)
    ego_edges = beside(bev_maps[:, rows - 1 :], bev_maps[:, :1])

    def travel(x):
        x = x.reshape(devices, -1, *x.shape[1:])
        x = lax.all_to_all(x, "veh", 0, 0, tiled=True)
        return x.reshape(-1, *x.shape[2:])

    arrived = [travel(packed)]
    later = pack_tiles(second, chosen)
    arrived[0], later = lax.optimization_barrier((arrived[0], later))
    arrived.append(travel(later))
    result, pieces = None, []
    for phase, own in enumerate((first, second)):
        if phase:
            place, result = lax.optimization_barrier((place, result))
        joined, top, low = join_agents(
            own, arrived[phase], place, live, agent_query, agent_keyvalue, agent_out, agent_scale
        )
        pieces.append((joined, *beside(low, top)))
        result = window_layer(
            phase,
            turned,
            ego_edges,
            pieces,
            result,
            conv_weight,
            gain_first,
            window_in,
            window_out,
            window_scale,
            gain_second,
            hidden_up,
            hidden_down,
        )
    return result.reshape(vehicles_here, rows, cols, 2 * channels)


def solution(mesh):
    split_maps = P("veh", "row", None, None)
    return jax.shard_map(
        on_device,
        mesh=mesh,
        in_specs=(split_maps,) + (P(),) * 15,
        out_specs=split_maps,
        check_vma=False,
    )
```

```python
import functools
import math

import jax
import jax.numpy as jnp
from jax import lax
from jax.experimental import pallas as pl
from jax.experimental.pallas import tpu as pltpu
from jax.sharding import PartitionSpec as P

TILE = 32
WIN = 8
HEAD = 32

norm_eps = 1e-05
unit_eps = 1e-06
LOG2E = math.log2(math.e)
VMEM_BYTES = 24 * 2**20
PHASES = 2

NN = (((1,), (0,)), ((), ()))
NT = (((1,), (1,)), ((), ()))
TN = (((0,), (0,)), ((), ()))


def dot(a, b, dims=NN):
    return lax.dot_general(a, b, dims, preferred_element_type=jnp.float32)


def split(x):
    high = x.astype(jnp.bfloat16)
    return high, (x - high.astype(jnp.float32)).astype(jnp.bfloat16)


def head_sums(x):
    return jnp.sum(x.reshape(x.shape[0] // HEAD, HEAD, x.shape[1]), axis=1, keepdims=True)


def by_head(x, factor):
    return (x.reshape(x.shape[0] // HEAD, HEAD, x.shape[1]) * factor).reshape(x.shape)


def phase_columns(phase):
    run = TILE // PHASES
    return [TILE - 1] + list(range(run + 1)) if phase == 0 else list(range(run + 1, TILE - 1))


def half_size():
    return max(1, lax.axis_size("veh") // 2)


def turn_kernel(maps, turned, first, second, scratch):
    rows, cols, channels = maps.shape[1:]
    run = TILE // PHASES
    for i in range(rows):
        scratch[pl.ds(i, cols, stride=rows), :] = maps[0, i].astype(jnp.float32)
    x = scratch[...].astype(jnp.bfloat16).reshape(cols, rows, channels)
    turned[0] = x
    for t in range(cols // TILE):
        tile = x[t * TILE : (t + 1) * TILE]
        first[t] = jnp.concatenate([tile[TILE - 1 :], tile[: run + 1]], axis=0)
        second[t] = tile[run + 1 : TILE - 1]


def turn_maps(maps):
    vehicles, rows, cols, channels = maps.shape
    tile_cols = cols // TILE
    pieces = [(tile_cols, len(phase_columns(p)), rows, channels) for p in range(PHASES)]
    blocks = [(1, cols, rows, channels), *pieces]
    block = lambda shape: pl.BlockSpec(shape, lambda v: (v, 0, 0, 0))
    return pl.pallas_call(
        turn_kernel,
        out_shape=[jax.ShapeDtypeStruct((vehicles * n[0], *n[1:]), maps.dtype) for n in blocks],
        grid=(vehicles,),
        in_specs=[block((1, rows, cols, channels))],
        out_specs=[block(n) for n in blocks],
        scratch_shapes=[pltpu.VMEM((rows * cols, channels), jnp.float32)],
        compiler_params=pltpu.CompilerParams(vmem_limit_bytes=VMEM_BYTES),
        cost_estimate=pl.CostEstimate(flops=0, bytes_accessed=10 * maps.size, transcendentals=0),
    )(maps)


def send_kernel(sizes, senders, shifts, counts, ids, *refs):
    vehicles, agents, tile_cols, group, capacity, sources = sizes
    bufs, messages, sems = refs[:sources], refs[sources:-1], refs[-1]
    me = ids[0]
    base = me // group * group
    filled = []
    for k in range(1, group):
        target = base + (me - base + k) % group
        for b in range(sources):

            def pair(i, n):
                r, a = target * vehicles + i // agents, i % agents
                sender, shift = senders[r, a], shifts[r, a]
                tiles = tile_cols - jnp.abs(shift)
                fits = (a < counts[r]) & (sender // vehicles == ids[b + 1]) & (n + tiles <= capacity)
                tile = sender % vehicles * tile_cols + jnp.maximum(shift, 0)
                for t in range(tile_cols):

                    @pl.when(fits & (t < tiles))
                    def _():
                        slot = b * capacity + n + t
                        pltpu.make_async_copy(
                            bufs[b].at[tile + t], messages[k - 1].at[slot], sems.at[k - 1, slot]
                        ).start()

                return n + jnp.where(fits, tiles, 0)

            filled.append((k, b, lax.fori_loop(0, vehicles * agents, pair, 0)))
    for k, b, n in filled:

        def finish(i, _):
            slot = b * capacity + i
            pltpu.make_async_copy(bufs[b].at[0], messages[k - 1].at[slot], sems.at[k - 1, slot]).wait()
            return 0

        lax.fori_loop(0, n, finish, 0)


def messages_for(pairs, tile_cols, sources):
    senders = pairs[0]
    devices = lax.axis_size("veh")
    vehicles, agents = senders.shape[0] // devices, senders.shape[1]
    group = half_size()
    capacity = tile_cols * max(1, vehicles * agents // devices)
    ids = jnp.stack([lax.axis_index("veh")] + [d for d, _ in sources]).astype(jnp.int32)
    shape = (len(sources) * capacity, *sources[0][1].shape[1:])
    return pl.pallas_call(
        functools.partial(
            send_kernel, (vehicles, agents, tile_cols, group, capacity, len(sources))
        ),
        out_shape=[jax.ShapeDtypeStruct(shape, sources[0][1].dtype)] * (group - 1),
        grid_spec=pltpu.PrefetchScalarGridSpec(
            num_scalar_prefetch=4,
            grid=(1,),
            in_specs=[pl.BlockSpec(memory_space=pl.ANY)] * len(sources),
            out_specs=[pl.BlockSpec(memory_space=pl.ANY)] * (group - 1),
            scratch_shapes=[pltpu.SemaphoreType.DMA((group - 1, shape[0]))],
        ),
        compiler_params=pltpu.CompilerParams(vmem_limit_bytes=VMEM_BYTES),
        cost_estimate=pl.CostEstimate(
            flops=0, bytes_accessed=4 * (group - 1) * math.prod(shape), transcendentals=0
        ),
    )(*pairs, ids, *(x for _, x in sources))


def place_kernel(sizes, senders, shifts, counts, ids, place, live, sent):
    vehicles, agents, tile_cols, group, capacity = sizes
    me = ids[0]
    tiles_held = vehicles * tile_cols
    rank = me % group

    def clear(i, _):
        sent[i] = 0
        return 0

    lax.fori_loop(0, sent.shape[0], clear, 0)

    def pair(i, _):
        v, a = i // agents, i % agents
        r = me * vehicles + v
        sender, shift = senders[r, a], shifts[r, a]
        alive = a < counts[r]
        source = sender // vehicles
        n = sent[source]
        k = (rank - source % group + group) % group
        apart = jnp.where(source // group == me // group, 0, 1)
        slot = jnp.where(
            k == 0,
            apart * tiles_held + sender % vehicles * tile_cols + jnp.maximum(shift, 0),
            2 * tiles_held + ((k - 1) * 2 + apart) * capacity + n,
        )
        first = jnp.maximum(-shift, 0)
        for t in range(tile_cols):
            inside = alive & (t + shift >= 0) & (t + shift < tile_cols)
            at = a * tiles_held + v * tile_cols + t
            place[at] = jnp.where(inside, slot + t - first, 0)
            live[at] = jnp.where(inside, 1, 0)
        sent[source] = n + jnp.where(alive, tile_cols - jnp.abs(shift), 0)
        return 0

    lax.fori_loop(0, vehicles * agents, pair, 0)


def places_of(pairs, tile_cols):
    senders = pairs[0]
    devices = lax.axis_size("veh")
    vehicles, agents = senders.shape[0] // devices, senders.shape[1]
    capacity = tile_cols * max(1, vehicles * agents // devices)
    count = agents * vehicles * tile_cols
    ids = lax.axis_index("veh").astype(jnp.int32).reshape(1)
    place, live = pl.pallas_call(
        functools.partial(place_kernel, (vehicles, agents, tile_cols, half_size(), capacity)),
        out_shape=[jax.ShapeDtypeStruct((count,), jnp.int32)] * 2,
        in_specs=[pl.BlockSpec(memory_space=pltpu.SMEM)] * 4,
        out_specs=[pl.BlockSpec(memory_space=pltpu.SMEM)] * 2,
        scratch_shapes=[pltpu.SMEM((devices,), jnp.int32)],
        compiler_params=pltpu.CompilerParams(vmem_limit_bytes=VMEM_BYTES),
    )(*pairs, ids)
    return place, live.reshape(agents, -1)


LANES = 128


def join_kernel(steps, starts, place, ego, *refs):
    bufs, refs = refs[: len(starts)], refs[len(starts) :]
    present, wq, wkv, wout, scale, out, top_row, low_row, landed, joined, sems = refs
    step = pl.program_id(0)
    agents, total, channels = landed.shape
    here = total // steps
    cells = bufs[0].shape[1]
    pieces = total // cells
    part = pieces // steps

    def copy(i, source):
        a, q = i // pieces, i % pieces
        start = pl.multiple_of(q * cells, 16)
        return pltpu.make_async_copy(source, landed.at[a, pl.ds(start, cells), :], sems.at[i])

    def fetch(i, _):
        at = place[i]
        for buf, parts in zip(bufs, starts):
            for first, size, offset in parts:

                @pl.when((at >= first) & (at < first + size))
                def _(buf=buf, first=first, offset=offset):
                    copy(i, buf.at[at - first + offset]).start()

        return 0

    @pl.when(step == 0)
    def _():
        lax.fori_loop(0, agents * pieces, fetch, 0)

    def wait(i, _):
        copy(i // part * pieces + step * part + i % part, bufs[0].at[0]).wait()
        return 0

    lax.fori_loop(0, agents * part, wait, 0)
    heads = channels // HEAD
    scale_col = scale[...].reshape(heads, 1, 1)
    for c in range(here // LANES):
        span = pl.ds(c * LANES, LANES)
        cells_here = ego[span, :]
        queries = dot(wq[...], cells_here, NT)
        factor = lax.rsqrt(head_sums(queries * queries) + unit_eps) * scale_col

        def agent(x):
            kv = dot(wkv[...], x, NT).astype(jnp.bfloat16).astype(jnp.float32)
            keys, values = kv[:channels], kv[channels:]
            score = head_sums(queries * keys) * factor
            return score * lax.rsqrt(head_sums(keys * keys) + unit_eps), values

        scores, values = zip(
            agent(cells_here),
            *(
                agent(landed[a, pl.ds(pl.multiple_of(step * here + c * LANES, LANES), LANES), :])
                for a in range(agents)
            ),
        )
        scores = [scores[0]] + [
            jnp.where(present[a : a + 1, c * LANES : (c + 1) * LANES].reshape(1, 1, LANES) > 0, s, -1e30)
            for a, s in enumerate(scores[1:])
        ]
        top = functools.reduce(jnp.maximum, scores)
        weights = [jnp.exp(s - top) for s in scores]
        inverse = 1.0 / functools.reduce(jnp.add, weights)
        mix = functools.reduce(jnp.add, [by_head(v, w * inverse) for w, v in zip(weights, values)])
        joined[span, :] = dot(mix.astype(jnp.bfloat16), wout[...], TN)
    out[...] = joined[...].astype(jnp.bfloat16)
    rows = here // top_row.shape[0]
    top_row[...] = joined[pl.ds(0, here // rows, stride=rows), :].astype(jnp.bfloat16)
    low_row[...] = joined[pl.ds(rows - 1, here // rows, stride=rows), :].astype(jnp.bfloat16)


def join_agents(pieces, arrived, starts, place, live, wq, wkv, wout, scale):
    count, cols, rows, channels = pieces.shape
    agents = live.shape[0]
    cells = cols * rows
    total = count * cells
    steps = 2
    whole = lambda x: pl.BlockSpec(x.shape, lambda r, *_: (0,) * x.ndim)
    block = lambda n: pl.BlockSpec((n // steps, channels), lambda r, *_: (r, 0))
    weights = (wq.T, wkv.T, wout, scale.reshape(-1, 1))
    present = jnp.repeat(live.astype(jnp.float32), cells, axis=1)
    like = lambda n: jax.ShapeDtypeStruct((n, channels), jnp.bfloat16)
    return pl.pallas_call(
        functools.partial(join_kernel, steps, starts),
        out_shape=[like(total), like(total // rows), like(total // rows)],
        grid_spec=pltpu.PrefetchScalarGridSpec(
            num_scalar_prefetch=1,
            grid=(steps,),
            in_specs=[
                block(total),
                *[pl.BlockSpec(memory_space=pl.ANY)] * len(arrived),
                pl.BlockSpec((agents, total // steps), lambda r, *_: (0, r)),
            ]
            + [whole(w) for w in weights],
            out_specs=[block(total), block(total // rows), block(total // rows)],
            scratch_shapes=[
                pltpu.VMEM((agents, total, channels), jnp.bfloat16),
                pltpu.VMEM((total // steps, channels), jnp.float32),
                pltpu.SemaphoreType.DMA((agents * count,)),
            ],
        ),
        compiler_params=pltpu.CompilerParams(vmem_limit_bytes=VMEM_BYTES),
        cost_estimate=pl.CostEstimate(
            flops=total * channels * channels * 40, bytes_accessed=total * channels * 12, transcendentals=total * 20
        ),
    )(
        place,
        pieces.reshape(total, channels),
        *(x.reshape(-1, cells, channels) for x in arrived),
        present,
        *weights,
    )


def norm(x, gain):
    average = jnp.mean(x, axis=-1, keepdims=True)
    centred = x - average
    spread = jnp.mean(centred * centred, axis=-1, keepdims=True)
    return (centred * lax.rsqrt(spread + norm_eps) * gain).astype(jnp.bfloat16)


def spread_rows(ref, rows_of, at, rows):
    count, channels = rows_of.shape
    ref[pl.ds(at, count, stride=rows), :] = rows_of.astype(jnp.float32)
    return ref[: count * rows].reshape(count, rows, channels)


def runs_of(phase, tile_cols, whole_map, pieces):
    run = TILE // PHASES
    out = []
    for t in range(tile_cols):
        first = t * TILE + phase * run - 1
        if pieces is None:
            last = first + run + 2
            blank = jnp.zeros_like(whole_map[:1])
            body = whole_map[max(first, 0) : min(last, tile_cols * TILE)]
            parts = ([blank] if first < 0 else []) + [body] + ([blank] if last > tile_cols * TILE else [])
        else:
            size = run + 2
            one = pieces[0]
            blank = jnp.zeros_like(one[:1])
            if phase == 0:
                left = one[(t - 1) * size : (t - 1) * size + 1] if t else blank
                parts = [left, one[t * size + 1 : (t + 1) * size]]
            else:
                rest = TILE - size
                right = one[(t + 1) * size + 1 : (t + 1) * size + 2] if t + 1 < tile_cols else blank
                parts = [
                    one[t * size + run : (t + 1) * size],
                    pieces[1][t * rest : (t + 1) * rest],
                    one[t * size : t * size + 1],
                    right,
                ]
        out.append(jnp.concatenate(parts, axis=0))
    return out


def taps_of(runs, above, below, taps):
    out = []
    for x, first, last in zip(runs, above, below):
        cols, rows, channels = x.shape
        row = lax.broadcasted_iota(jnp.int32, (rows, channels), 0)[None]
        flat = x.reshape(cols * rows, channels)
        over = jnp.where(row == 0, first, pltpu.roll(flat, 1, 0).reshape(x.shape))
        under = jnp.where(row == rows - 1, last, pltpu.roll(flat, cols * rows - 1, 0).reshape(x.shape))
        total = x[1 : cols - 1]
        for j in range(3):
            span = slice(j, cols - 2 + j)
            total = total + over[span] * taps[j] + x[span] * taps[3 + j] + under[span] * taps[6 + j]
        out.append(total.reshape((cols - 2) * rows, channels))
    return out


def window_kernel(phase, rows, *refs):
    ego, ego_up, ego_down, refs = *refs[:3], refs[3:]
    pieces, refs = [refs[3 * p : 3 * p + 3] for p in range(phase + 1)], refs[3 * phase + 3 :]
    taps, gain_one, wq, wk, wv, wo, scale, gain_two, up, down = refs[:10]
    out, mixed_ref, result_ref, halo = refs[10 + phase :]
    group_size, cols, _, channels = ego.shape
    tile_cols = cols // TILE
    run = TILE // PHASES
    width = 2 * channels
    in_window = rows * WIN
    here = tile_cols * run * rows
    cells = group_size * here
    windows = cells // in_window
    heads = width // HEAD
    f32 = jnp.float32
    for v in range(group_size):
        for half in range(2):
            lanes = slice(half * channels, (half + 1) * channels)
            weights = [taps[i : i + 1, lanes].reshape(1, 1, channels) for i in range(9)]
            if half == 0:
                centre = runs_of(phase, tile_cols, ego[v].astype(f32), None)
                above = runs_of(phase, tile_cols, spread_rows(halo.at[0], ego_up[v, 0], 0, rows), None)
                below = runs_of(phase, tile_cols, spread_rows(halo.at[1], ego_down[v, 0], rows - 1, rows), None)
            else:
                centre, above, below = [], [], []
                for p, (x, first, last) in enumerate(pieces):
                    centre.append(x[v].astype(f32).reshape(-1, rows, channels))
                    above.append(spread_rows(halo.at[2 + 2 * p], first[v], 0, rows))
                    below.append(spread_rows(halo.at[3 + 2 * p], last[v], rows - 1, rows))
                centre, above, below = (runs_of(phase, tile_cols, None, x) for x in (centre, above, below))
            for t, part in enumerate(taps_of(centre, above, below, weights)):
                at = v * here + t * run * rows
                mixed_ref[at : at + run * rows, lanes] = part
    hidden = norm(mixed_ref[...], gain_one[...])
    queries = dot(wq[...], hidden, NT)
    values = dot(wv[...], hidden, NT).astype(jnp.bfloat16)
    keys = dot(hidden, wk[...])
    factor = lax.rsqrt(head_sums(queries * queries) + unit_eps) * scale[...].reshape(heads, 1, 1)
    queries = by_head(queries, factor)
    member = (
        lax.broadcasted_iota(jnp.int32, (width, width), 0) // HEAD
        == lax.broadcasted_iota(jnp.int32, (width, width), 1) // HEAD
    ).astype(f32).astype(jnp.bfloat16)
    square_high, square_low = split(keys * keys)
    keys = keys * lax.rsqrt(dot(square_high, member) + dot(square_low, member) + unit_eps)
    key_high, key_low = split(keys)

    pair = 2 * in_window
    group = 4 * HEAD
    lane = lax.broadcasted_iota(jnp.int32, (width, pair), 1) < in_window
    even = (lax.broadcasted_iota(jnp.int32, (width, pair), 0) // HEAD) % 2 == 0
    blank = jnp.zeros((2 * HEAD, pair), jnp.bfloat16)
    blank_p = jnp.zeros((in_window, 4 * in_window), jnp.bfloat16)
    lane_head = lax.broadcasted_iota(jnp.int32, (HEAD, pair), 1) < in_window
    attended = []
    for p in range(windows // 2):
        straight = queries[:, p * pair : (p + 1) * pair]
        turned = pltpu.roll(straight, in_window, 1)
        blocks = []
        for w in range(2):
            low, high = (straight, turned) if w == 0 else (turned, straight)
            blocks.append(split(jnp.where(even, jnp.where(lane, low, 0.0), jnp.where(lane, 0.0, high))))
        parts = []
        for g in range(width // group):
            channels_of = slice(g * group, (g + 1) * group)
            probs = []
            for w in range(2):
                at = (2 * p + w) * in_window
                k_high = key_high[at : at + in_window, channels_of]
                k_low = key_low[at : at + in_window, channels_of]

                def right(block):
                    block = block[channels_of]
                    return jnp.concatenate(
                        [
                            jnp.concatenate([block[: 2 * HEAD], blank], axis=1),
                            jnp.concatenate([blank, block[2 * HEAD :]], axis=1),
                        ],
                        axis=0,
                    )

                first = dot(jnp.concatenate([k_high, k_low], axis=0), right(blocks[w][0]))
                score = first[:in_window] + first[in_window:] + dot(k_high, right(blocks[w][1]))
                weight = jnp.exp2(score - jnp.max(score, axis=0, keepdims=True))
                weight = weight * (1.0 / jnp.sum(weight, axis=0, keepdims=True))
                weight = weight.astype(jnp.bfloat16)
                probs.append(
                    jnp.concatenate([weight, blank_p] if w == 0 else [blank_p, weight], axis=0)
                )
            v = values[channels_of, p * pair : (p + 1) * pair]
            first, second = dot(v, probs[0]), dot(v, probs[1])
            for h in range(4):
                rows_of = slice(h * HEAD, (h + 1) * HEAD)
                cols_of = slice((h // 2) * pair, (h // 2 + 1) * pair)
                a, b = first[rows_of, cols_of], second[rows_of, cols_of]
                if h % 2 == 0:
                    b = pltpu.roll(b, in_window, 1)
                else:
                    a = pltpu.roll(a, in_window, 1)
                parts.append(jnp.where(lane_head, a, b))
        attended.append(jnp.concatenate(parts, axis=0).astype(jnp.bfloat16))
    attended = jnp.concatenate(attended, axis=1)
    mixed = mixed_ref[...] + dot(attended, wo[...], TN)
    hidden = norm(mixed, gain_two[...])
    inner = dot(hidden, up[...])
    inner = (0.5 * inner * (1.0 + jnp.tanh(0.5 * inner))).astype(jnp.bfloat16)
    result = mixed + dot(inner, down[...])
    for half in range(2):
        result_ref[half] = result[:, half * channels : (half + 1) * channels]
    for v in range(group_size):
        for t in range(tile_cols):
            for i in range(rows):
                at = v * here + t * run * rows + i
                for half in range(2):
                    lanes = slice(half * channels, (half + 1) * channels)
                    line = result_ref[half, pl.ds(at, run, stride=rows), :]
                    out[v, i, t, :, lanes] = line.astype(jnp.bfloat16)


def window_layer(phase, turned, ego_edges, pieces, before, conv_weight, gain_first, window_in, window_out,
                 window_scale, gain_second, hidden_up, hidden_down):
    vehicles, cols, rows, channels = turned.shape
    width = 2 * channels
    tile_cols = cols // TILE
    run = TILE // PHASES
    group = 2
    whole = lambda x: pl.BlockSpec(x.shape, lambda r: (0,) * x.ndim)
    block = lambda *shape: pl.BlockSpec((group, *shape), lambda r: (r,) + (0,) * len(shape))
    weights = (
        conv_weight.reshape(9, width),
        gain_first[None],
        window_in[:, :width].T,
        window_in[:, width : 2 * width],
        window_in[:, 2 * width :].T,
        window_out,
        (window_scale * LOG2E).reshape(-1, 1),
        gain_second[None],
        hidden_up,
        hidden_down,
    )
    pieces = [x.reshape(vehicles, -1, channels) for three in pieces for x in three]
    cells = vehicles * rows * tile_cols * run
    most = cols * rows
    operands = (turned, *ego_edges, *pieces, *weights)
    in_specs = (
        [block(cols, rows, channels)]
        + [block(1, cols, channels)] * 2
        + [block(*x.shape[1:]) for x in pieces]
        + [whole(w) for w in weights]
    )
    aliases = {}
    if before is not None:
        aliases = {len(operands): 0}
        operands += (before,)
        in_specs += [pl.BlockSpec(memory_space=pl.ANY)]
    return pl.pallas_call(
        functools.partial(window_kernel, phase, rows),
        out_shape=jax.ShapeDtypeStruct((vehicles, rows, tile_cols, PHASES, run, width), jnp.bfloat16),
        grid=(vehicles // group,),
        in_specs=in_specs,
        out_specs=pl.BlockSpec(
            (group, rows, tile_cols, None, run, width), lambda r: (r, 0, 0, phase, 0, 0)
        ),
        scratch_shapes=[
            pltpu.VMEM((group * rows * tile_cols * run, width), jnp.float32),
            pltpu.VMEM((2, group * rows * tile_cols * run, channels), jnp.float32),
            pltpu.VMEM((2 * PHASES + 2, most, channels), jnp.float32),
        ],
        input_output_aliases=aliases,
        compiler_params=pltpu.CompilerParams(vmem_limit_bytes=VMEM_BYTES),
        cost_estimate=pl.CostEstimate(
            flops=cells * width * width * 60, bytes_accessed=cells * width * 6, transcendentals=cells * width * 4
        ),
    )(*operands)


def beside(last, first):
    count = lax.axis_size("row")
    above = lax.ppermute(last, "row", [(i, i + 1) for i in range(count - 1)])
    below = lax.ppermute(first, "row", [(i + 1, i) for i in range(count - 1)])
    return above, below


def on_device(
    bev_maps,
    senders,
    shifts,
    counts,
    agent_query,
    agent_keyvalue,
    agent_out,
    agent_scale,
    conv_weight,
    gain_first,
    window_in,
    window_out,
    window_scale,
    gain_second,
    hidden_up,
    hidden_down,
):
    vehicles_here, rows, cols, channels = bev_maps.shape
    devices = lax.axis_size("veh")
    tile_cols = cols // TILE
    tiles = vehicles_here * tile_cols
    myself = lax.axis_index("veh")
    group = half_size()
    partner = (myself + group) % devices
    capacity = tile_cols * max(1, vehicles_here * senders.shape[1] // devices)
    pairs = (senders, shifts, counts)

    turned, first, second = turn_maps(bev_maps)

    def swap(x):
        return lax.ppermute(x, "veh", [(i, (i + group) % devices) for i in range(devices)])

    def send(messages):
        return [
            lax.ppermute(
                x, "veh", [(i, i // group * group + (i + k + 1) % group) for i in range(devices)]
            )
            for k, x in enumerate(messages)
        ]

    far = swap(first)
    near_tiles = send(messages_for(pairs, tile_cols, [(myself, first)]))
    place, live = places_of(pairs, tile_cols)
    ego_edges = beside(bev_maps[:, rows - 1 :], bev_maps[:, :1])
    far, second = lax.optimization_barrier((far, second))
    far_tiles = send(messages_for(pairs, tile_cols, [(partner, far)]))
    later = swap(second)
    later_tiles = send(messages_for(pairs, tile_cols, [(myself, second), (partner, later)]))
    arrived = [[first, far, *near_tiles, *far_tiles], [second, later, *later_tiles]]
    slots = lambda n: 2 * tiles + n * capacity
    whole_maps = [((0, tiles, 0),), ((tiles, tiles, 0),)]
    starts = [
        whole_maps
        + [((slots(2 * k), capacity, 0),) for k in range(group - 1)]
        + [((slots(2 * k + 1), capacity, 0),) for k in range(group - 1)],
        whole_maps + [((slots(2 * k), 2 * capacity, 0),) for k in range(group - 1)],
    ]
    result, pieces = None, []
    for phase, own in enumerate((first, second)):
        if phase:
            place, result = lax.optimization_barrier((place, result))
        joined, top, low = join_agents(
            own, arrived[phase], starts[phase], place, live, agent_query, agent_keyvalue, agent_out, agent_scale
        )
        pieces.append((joined, *beside(low, top)))
        result = window_layer(
            phase,
            turned,
            ego_edges,
            pieces,
            result,
            conv_weight,
            gain_first,
            window_in,
            window_out,
            window_scale,
            gain_second,
            hidden_up,
            hidden_down,
        )
    return result.reshape(vehicles_here, rows, cols, 2 * channels)


def solution(mesh):
    split_maps = P("veh", "row", None, None)
    return jax.shard_map(
        on_device,
        mesh=mesh,
        in_specs=(split_maps,) + (P(),) * 15,
        out_specs=split_maps,
        check_vma=False,
    )
```

```python
import functools
import math

import jax
import jax.numpy as jnp
from jax import lax
from jax.experimental import pallas as pl
from jax.experimental.pallas import tpu as pltpu
from jax.sharding import PartitionSpec as P

TILE = 32
WIN = 8
HEAD = 32

norm_eps = 1e-05
unit_eps = 1e-06
LOG2E = math.log2(math.e)
VMEM_BYTES = 24 * 2**20
WINDOW_VMEM_BYTES = 60 * 2**20
PHASES = 2

NN = (((1,), (0,)), ((), ()))
NT = (((1,), (1,)), ((), ()))
TN = (((0,), (0,)), ((), ()))


def dot(a, b, dims=NN):
    return lax.dot_general(a, b, dims, preferred_element_type=jnp.float32)


def split(x):
    high = x.astype(jnp.bfloat16)
    return high, (x - high.astype(jnp.float32)).astype(jnp.bfloat16)


def head_sums(x):
    return jnp.sum(x.reshape(x.shape[0] // HEAD, HEAD, x.shape[1]), axis=1, keepdims=True)


def by_head(x, factor):
    return (x.reshape(x.shape[0] // HEAD, HEAD, x.shape[1]) * factor).reshape(x.shape)


def phase_columns(phase):
    run = TILE // PHASES
    return [TILE - 1] + list(range(run + 1)) if phase == 0 else list(range(run + 1, TILE - 1))


def half_size():
    return max(1, lax.axis_size("veh") // 2)


def turn_kernel(maps, turned, first, second, scratch):
    rows, cols, channels = maps.shape[1:]
    run = TILE // PHASES
    for i in range(rows):
        scratch[pl.ds(i, cols, stride=rows), :] = maps[0, i].astype(jnp.float32)
    x = scratch[...].astype(jnp.bfloat16).reshape(cols, rows, channels)
    turned[0] = x
    for t in range(cols // TILE):
        tile = x[t * TILE : (t + 1) * TILE]
        first[t] = jnp.concatenate([tile[TILE - 1 :], tile[: run + 1]], axis=0)
        second[t] = tile[run + 1 : TILE - 1]


def turn_maps(maps):
    vehicles, rows, cols, channels = maps.shape
    tile_cols = cols // TILE
    pieces = [(tile_cols, len(phase_columns(p)), rows, channels) for p in range(PHASES)]
    blocks = [(1, cols, rows, channels), *pieces]
    block = lambda shape: pl.BlockSpec(shape, lambda v: (v, 0, 0, 0))
    return pl.pallas_call(
        turn_kernel,
        out_shape=[jax.ShapeDtypeStruct((vehicles * n[0], *n[1:]), maps.dtype) for n in blocks],
        grid=(vehicles,),
        in_specs=[block((1, rows, cols, channels))],
        out_specs=[block(n) for n in blocks],
        scratch_shapes=[pltpu.VMEM((rows * cols, channels), jnp.float32)],
        compiler_params=pltpu.CompilerParams(vmem_limit_bytes=VMEM_BYTES),
        cost_estimate=pl.CostEstimate(flops=0, bytes_accessed=10 * maps.size, transcendentals=0),
    )(maps)


def plan_kernel(sizes, senders, shifts, counts, ids, chosen, filled, place, live, sent):
    vehicles, agents, tile_cols, group, capacity = sizes
    me, partner = ids[0], ids[1]
    tiles_held = vehicles * tile_cols
    rank = me % group
    pairs = vehicles * agents

    def clear(i, _):
        sent[i] = 0
        return 0

    lax.fori_loop(0, sent.shape[0], clear, 0)

    def target(k, _):
        first = (me - rank + (rank + k + 1) % group) * vehicles

        def pair(i, n):
            r, a = first + i // agents, i % agents
            sender, shift = senders[r, a], shifts[r, a]
            tiles = tile_cols - jnp.abs(shift)
            source = sender // vehicles
            far = jnp.where(source == partner, 1, 0)
            filled_here = jnp.where(far == 1, n[1], n[0])
            fits = (a < counts[r]) & ((source == me) | (far == 1)) & (filled_here + tiles <= capacity)

            @pl.when(fits)
            def _():
                at = (2 * k + far) * capacity + filled_here
                tile = sender % vehicles * tile_cols + jnp.maximum(shift, 0)
                for t in range(tile_cols):

                    @pl.when(t < tiles)
                    def _():
                        chosen[at + t] = tile + t

            more = jnp.where(fits, tiles, 0)
            return n[0] + more * (1 - far), n[1] + more * far

        near, far = lax.fori_loop(0, pairs, pair, (0, 0))
        filled[2 * k] = near
        filled[2 * k + 1] = far
        return 0

    lax.fori_loop(0, group - 1, target, 0)

    def pair(i, _):
        v, a = i // agents, i % agents
        r = me * vehicles + v
        sender, shift = senders[r, a], shifts[r, a]
        alive = a < counts[r]
        source = sender // vehicles
        n = sent[source]
        k = (rank - source % group + group) % group
        apart = jnp.where(source // group == me // group, 0, 1)
        slot = jnp.where(
            k == 0,
            apart * tiles_held + sender % vehicles * tile_cols + jnp.maximum(shift, 0),
            2 * tiles_held + ((k - 1) * 2 + apart) * capacity + n,
        )
        first = jnp.maximum(-shift, 0)
        for t in range(tile_cols):
            inside = alive & (t + shift >= 0) & (t + shift < tile_cols)
            at = a * tiles_held + v * tile_cols + t
            place[at] = jnp.where(inside, slot + t - first, 0)
            live[at] = jnp.where(inside, 1, 0)
        sent[source] = n + jnp.where(alive, tile_cols - jnp.abs(shift), 0)
        return 0

    lax.fori_loop(0, pairs, pair, 0)


def plan_of(senders, shifts, counts, tile_cols, capacity):
    devices = lax.axis_size("veh")
    group = half_size()
    vehicles, agents = senders.shape[0] // devices, senders.shape[1]
    me = lax.axis_index("veh").astype(jnp.int32)
    ids = jnp.stack([me, (me + group) % devices])
    sizes = [(group - 1) * 2 * capacity, (group - 1) * 2] + [agents * vehicles * tile_cols] * 2
    smem = pl.BlockSpec(memory_space=pltpu.SMEM)
    return pl.pallas_call(
        functools.partial(plan_kernel, (vehicles, agents, tile_cols, group, capacity)),
        out_shape=[jax.ShapeDtypeStruct((n,), jnp.int32) for n in sizes],
        in_specs=[smem] * 4,
        out_specs=[smem] * 4,
        scratch_shapes=[pltpu.SMEM((devices,), jnp.int32)],
        compiler_params=pltpu.CompilerParams(vmem_limit_bytes=VMEM_BYTES),
        cost_estimate=pl.CostEstimate(flops=0, bytes_accessed=20 * 2**20, transcendentals=0),
    )(senders, shifts, counts, ids)


def send_kernel(sources, capacity, chosen, filled, *refs):
    bufs, messages, sems = refs[: len(sources)], refs[len(sources) : -1], refs[-1]
    copies = []
    for k, message in enumerate(messages):
        for b, source in enumerate(sources):

            def copy(i, tile, k=k, b=b, message=message):
                slot = b * capacity + i
                return pltpu.make_async_copy(bufs[b].at[tile], message.at[slot], sems.at[k, slot])

            copies.append((2 * k + source, copy))
    for at, copy in copies:
        lax.fori_loop(
            0, filled[at], lambda i, _: (copy(i, chosen[at * capacity + i]).start(), 0)[1], 0
        )
    for at, copy in copies:
        lax.fori_loop(0, filled[at], lambda i, _: (copy(i, 0).wait(), 0)[1], 0)


def messages_for(chosen, filled, capacity, sources):
    first = next(iter(sources.values()))
    count = filled.shape[0] // 2
    shape = (len(sources) * capacity, *first.shape[1:])
    anywhere = pl.BlockSpec(memory_space=pl.ANY)
    return pl.pallas_call(
        functools.partial(send_kernel, tuple(sources), capacity),
        out_shape=[jax.ShapeDtypeStruct(shape, first.dtype)] * count,
        grid_spec=pltpu.PrefetchScalarGridSpec(
            num_scalar_prefetch=2,
            grid=(1,),
            in_specs=[anywhere] * len(sources),
            out_specs=[anywhere] * count,
            scratch_shapes=[pltpu.SemaphoreType.DMA((count, shape[0]))],
        ),
        compiler_params=pltpu.CompilerParams(vmem_limit_bytes=VMEM_BYTES),
        cost_estimate=pl.CostEstimate(
            flops=0, bytes_accessed=4 * count * math.prod(shape), transcendentals=0
        ),
    )(chosen, filled, *sources.values())


LANES = 128


def join_kernel(steps, starts, place, ego, *refs):
    bufs, refs = refs[: len(starts)], refs[len(starts) :]
    present, wq, wkv, wout, scale, out, top_row, low_row, landed, joined, sems = refs
    step = pl.program_id(0)
    agents, total, channels = landed.shape
    here = total // steps
    cells = bufs[0].shape[1]
    pieces = total // cells
    part = pieces // steps

    def copy(i, source):
        a, q = i // pieces, i % pieces
        start = pl.multiple_of(q * cells, 16)
        return pltpu.make_async_copy(source, landed.at[a, pl.ds(start, cells), :], sems.at[i])

    def fetch(i, _):
        at = place[i]
        for buf, parts in zip(bufs, starts):
            for first, size, offset in parts:

                @pl.when((at >= first) & (at < first + size))
                def _(buf=buf, first=first, offset=offset):
                    copy(i, buf.at[at - first + offset]).start()

        return 0

    @pl.when(step == 0)
    def _():
        lax.fori_loop(0, agents * pieces, fetch, 0)

    def wait(i, _):
        copy(i // part * pieces + step * part + i % part, bufs[0].at[0]).wait()
        return 0

    lax.fori_loop(0, agents * part, wait, 0)
    heads = channels // HEAD
    scale_col = scale[...].reshape(heads, 1, 1)
    for c in range(here // LANES):
        span = pl.ds(c * LANES, LANES)
        cells_here = ego[span, :]
        queries = dot(wq[...], cells_here, NT)
        factor = lax.rsqrt(head_sums(queries * queries) + unit_eps) * scale_col

        def agent(x):
            kv = dot(wkv[...], x, NT).astype(jnp.bfloat16).astype(jnp.float32)
            keys, values = kv[:channels], kv[channels:]
            score = head_sums(queries * keys) * factor
            return score * lax.rsqrt(head_sums(keys * keys) + unit_eps), values

        scores, values = zip(
            agent(cells_here),
            *(
                agent(landed[a, pl.ds(pl.multiple_of(step * here + c * LANES, LANES), LANES), :])
                for a in range(agents)
            ),
        )
        scores = [scores[0]] + [
            jnp.where(present[a : a + 1, c * LANES : (c + 1) * LANES].reshape(1, 1, LANES) > 0, s, -1e30)
            for a, s in enumerate(scores[1:])
        ]
        top = functools.reduce(jnp.maximum, scores)
        weights = [jnp.exp(s - top) for s in scores]
        inverse = 1.0 / functools.reduce(jnp.add, weights)
        mix = functools.reduce(jnp.add, [by_head(v, w * inverse) for w, v in zip(weights, values)])
        joined[span, :] = dot(mix.astype(jnp.bfloat16), wout[...], TN)
    out[...] = joined[...].astype(jnp.bfloat16)
    rows = here // top_row.shape[0]
    top_row[...] = joined[pl.ds(0, here // rows, stride=rows), :].astype(jnp.bfloat16)
    low_row[...] = joined[pl.ds(rows - 1, here // rows, stride=rows), :].astype(jnp.bfloat16)


def join_agents(pieces, arrived, starts, place, live, wq, wkv, wout, scale):
    count, cols, rows, channels = pieces.shape
    agents = live.shape[0]
    cells = cols * rows
    total = count * cells
    steps = 2
    whole = lambda x: pl.BlockSpec(x.shape, lambda r, *_: (0,) * x.ndim)
    block = lambda n: pl.BlockSpec((n // steps, channels), lambda r, *_: (r, 0))
    weights = (wq.T, wkv.T, wout, scale.reshape(-1, 1))
    present = jnp.repeat(live.astype(jnp.float32), cells, axis=1)
    like = lambda n: jax.ShapeDtypeStruct((n, channels), jnp.bfloat16)
    return pl.pallas_call(
        functools.partial(join_kernel, steps, starts),
        out_shape=[like(total), like(total // rows), like(total // rows)],
        grid_spec=pltpu.PrefetchScalarGridSpec(
            num_scalar_prefetch=1,
            grid=(steps,),
            in_specs=[
                block(total),
                *[pl.BlockSpec(memory_space=pl.ANY)] * len(arrived),
                pl.BlockSpec((agents, total // steps), lambda r, *_: (0, r)),
            ]
            + [whole(w) for w in weights],
            out_specs=[block(total), block(total // rows), block(total // rows)],
            scratch_shapes=[
                pltpu.VMEM((agents, total, channels), jnp.bfloat16),
                pltpu.VMEM((total // steps, channels), jnp.float32),
                pltpu.SemaphoreType.DMA((agents * count,)),
            ],
        ),
        compiler_params=pltpu.CompilerParams(vmem_limit_bytes=VMEM_BYTES),
        cost_estimate=pl.CostEstimate(
            flops=total * channels * channels * 40, bytes_accessed=total * channels * 12, transcendentals=total * 20
        ),
    )(
        place,
        pieces.reshape(total, channels),
        *(x.reshape(-1, cells, channels) for x in arrived),
        present,
        *weights,
    )


def norm(x, gain):
    average = jnp.mean(x, axis=-1, keepdims=True)
    centred = x - average
    spread = jnp.mean(centred * centred, axis=-1, keepdims=True)
    return (centred * lax.rsqrt(spread + norm_eps) * gain).astype(jnp.bfloat16)


def spread_rows(ref, rows_of, at, rows):
    count, channels = rows_of.shape
    ref[pl.ds(at, count, stride=rows), :] = rows_of.astype(jnp.float32)
    return ref[: count * rows].reshape(count, rows, channels)


def runs_of(phase, tile_cols, whole_map, pieces):
    run = TILE // PHASES
    out = []
    for t in range(tile_cols):
        first = t * TILE + phase * run - 1
        if pieces is None:
            last = first + run + 2
            blank = jnp.zeros_like(whole_map[:1])
            body = whole_map[max(first, 0) : min(last, tile_cols * TILE)]
            parts = ([blank] if first < 0 else []) + [body] + ([blank] if last > tile_cols * TILE else [])
        else:
            size = run + 2
            one = pieces[0]
            blank = jnp.zeros_like(one[:1])
            if phase == 0:
                left = one[(t - 1) * size : (t - 1) * size + 1] if t else blank
                parts = [left, one[t * size + 1 : (t + 1) * size]]
            else:
                rest = TILE - size
                right = one[(t + 1) * size + 1 : (t + 1) * size + 2] if t + 1 < tile_cols else blank
                parts = [
                    one[t * size + run : (t + 1) * size],
                    pieces[1][t * rest : (t + 1) * rest],
                    one[t * size : t * size + 1],
                    right,
                ]
        out.append(jnp.concatenate(parts, axis=0))
    return out


def taps_of(runs, above, below, taps):
    out = []
    for x, first, last in zip(runs, above, below):
        cols, rows, channels = x.shape
        row = lax.broadcasted_iota(jnp.int32, (rows, channels), 0)[None]
        flat = x.reshape(cols * rows, channels)
        over = jnp.where(row == 0, first, pltpu.roll(flat, 1, 0).reshape(x.shape))
        under = jnp.where(row == rows - 1, last, pltpu.roll(flat, cols * rows - 1, 0).reshape(x.shape))
        total = x[1 : cols - 1]
        for j in range(3):
            span = slice(j, cols - 2 + j)
            total = total + over[span] * taps[j] + x[span] * taps[3 + j] + under[span] * taps[6 + j]
        out.append(total.reshape((cols - 2) * rows, channels))
    return out


def window_kernel(phase, rows, *refs):
    ego, ego_up, ego_down, refs = *refs[:3], refs[3:]
    pieces, refs = [refs[3 * p : 3 * p + 3] for p in range(phase + 1)], refs[3 * phase + 3 :]
    taps, gain_one, wq, wk, wv, wo, scale, gain_two, up, down = refs[:10]
    out, mixed_ref, result_ref, halo = refs[10 + phase :]
    group_size, cols, _, channels = ego.shape
    tile_cols = cols // TILE
    run = TILE // PHASES
    width = 2 * channels
    in_window = rows * WIN
    here = tile_cols * run * rows
    cells = group_size * here
    windows = cells // in_window
    heads = width // HEAD
    f32 = jnp.float32
    for v in range(group_size):
        for half in range(2):
            lanes = slice(half * channels, (half + 1) * channels)
            weights = [taps[i : i + 1, lanes].reshape(1, 1, channels) for i in range(9)]
            if half == 0:
                centre = runs_of(phase, tile_cols, ego[v].astype(f32), None)
                above = runs_of(phase, tile_cols, spread_rows(halo.at[0], ego_up[v, 0], 0, rows), None)
                below = runs_of(phase, tile_cols, spread_rows(halo.at[1], ego_down[v, 0], rows - 1, rows), None)
            else:
                centre, above, below = [], [], []
                for p, (x, first, last) in enumerate(pieces):
                    centre.append(x[v].astype(f32).reshape(-1, rows, channels))
                    above.append(spread_rows(halo.at[2 + 2 * p], first[v], 0, rows))
                    below.append(spread_rows(halo.at[3 + 2 * p], last[v], rows - 1, rows))
                centre, above, below = (runs_of(phase, tile_cols, None, x) for x in (centre, above, below))
            for t, part in enumerate(taps_of(centre, above, below, weights)):
                at = v * here + t * run * rows
                mixed_ref[at : at + run * rows, lanes] = part
    hidden = norm(mixed_ref[...], gain_one[...])
    queries = dot(wq[...], hidden, NT)
    values = dot(wv[...], hidden, NT).astype(jnp.bfloat16)
    keys = dot(hidden, wk[...])
    factor = lax.rsqrt(head_sums(queries * queries) + unit_eps) * scale[...].reshape(heads, 1, 1)
    queries = by_head(queries, factor)
    member = (
        lax.broadcasted_iota(jnp.int32, (width, width), 0) // HEAD
        == lax.broadcasted_iota(jnp.int32, (width, width), 1) // HEAD
    ).astype(f32).astype(jnp.bfloat16)
    square_high, square_low = split(keys * keys)
    keys = keys * lax.rsqrt(dot(square_high, member) + dot(square_low, member) + unit_eps)
    key_high, key_low = split(keys)

    pair = 2 * in_window
    group = 4 * HEAD
    lane = lax.broadcasted_iota(jnp.int32, (width, pair), 1) < in_window
    even = (lax.broadcasted_iota(jnp.int32, (width, pair), 0) // HEAD) % 2 == 0
    blank = jnp.zeros((2 * HEAD, pair), jnp.bfloat16)
    blank_p = jnp.zeros((in_window, 4 * in_window), jnp.bfloat16)
    lane_head = lax.broadcasted_iota(jnp.int32, (HEAD, pair), 1) < in_window
    attended = []
    for p in range(windows // 2):
        straight = queries[:, p * pair : (p + 1) * pair]
        turned = pltpu.roll(straight, in_window, 1)
        blocks = []
        for w in range(2):
            low, high = (straight, turned) if w == 0 else (turned, straight)
            blocks.append(split(jnp.where(even, jnp.where(lane, low, 0.0), jnp.where(lane, 0.0, high))))
        parts = []
        for g in range(width // group):
            channels_of = slice(g * group, (g + 1) * group)
            probs = []
            for w in range(2):
                at = (2 * p + w) * in_window
                k_high = key_high[at : at + in_window, channels_of]
                k_low = key_low[at : at + in_window, channels_of]

                def right(block):
                    block = block[channels_of]
                    return jnp.concatenate(
                        [
                            jnp.concatenate([block[: 2 * HEAD], blank], axis=1),
                            jnp.concatenate([blank, block[2 * HEAD :]], axis=1),
                        ],
                        axis=0,
                    )

                first = dot(jnp.concatenate([k_high, k_low], axis=0), right(blocks[w][0]))
                score = first[:in_window] + first[in_window:] + dot(k_high, right(blocks[w][1]))
                weight = jnp.exp2(score - jnp.max(score, axis=0, keepdims=True))
                weight = weight * (1.0 / jnp.sum(weight, axis=0, keepdims=True))
                weight = weight.astype(jnp.bfloat16)
                probs.append(
                    jnp.concatenate([weight, blank_p] if w == 0 else [blank_p, weight], axis=0)
                )
            v = values[channels_of, p * pair : (p + 1) * pair]
            first, second = dot(v, probs[0]), dot(v, probs[1])
            for h in range(4):
                rows_of = slice(h * HEAD, (h + 1) * HEAD)
                cols_of = slice((h // 2) * pair, (h // 2 + 1) * pair)
                a, b = first[rows_of, cols_of], second[rows_of, cols_of]
                if h % 2 == 0:
                    b = pltpu.roll(b, in_window, 1)
                else:
                    a = pltpu.roll(a, in_window, 1)
                parts.append(jnp.where(lane_head, a, b))
        attended.append(jnp.concatenate(parts, axis=0).astype(jnp.bfloat16))
    attended = jnp.concatenate(attended, axis=1)
    mixed = mixed_ref[...] + dot(attended, wo[...], TN)
    hidden = norm(mixed, gain_two[...])
    inner = dot(hidden, up[...])
    inner = (0.5 * inner * (1.0 + jnp.tanh(0.5 * inner))).astype(jnp.bfloat16)
    result = mixed + dot(inner, down[...])
    for half in range(2):
        result_ref[half] = result[:, half * channels : (half + 1) * channels]
    for v in range(group_size):
        for t in range(tile_cols):
            for i in range(rows):
                at = v * here + t * run * rows + i
                for half in range(2):
                    lanes = slice(half * channels, (half + 1) * channels)
                    line = result_ref[half, pl.ds(at, run, stride=rows), :]
                    out[v, i, t, :, lanes] = line.astype(jnp.bfloat16)


def window_layer(phase, turned, ego_edges, pieces, before, conv_weight, gain_first, window_in, window_out,
                 window_scale, gain_second, hidden_up, hidden_down):
    vehicles, cols, rows, channels = turned.shape
    width = 2 * channels
    tile_cols = cols // TILE
    run = TILE // PHASES
    group = 2
    whole = lambda x: pl.BlockSpec(x.shape, lambda r: (0,) * x.ndim)
    block = lambda *shape: pl.BlockSpec((group, *shape), lambda r: (r,) + (0,) * len(shape))
    weights = (
        conv_weight.reshape(9, width),
        gain_first[None],
        window_in[:, :width].T,
        window_in[:, width : 2 * width],
        window_in[:, 2 * width :].T,
        window_out,
        (window_scale * LOG2E).reshape(-1, 1),
        gain_second[None],
        hidden_up,
        hidden_down,
    )
    pieces = [x.reshape(vehicles, -1, channels) for three in pieces for x in three]
    cells = vehicles * rows * tile_cols * run
    most = cols * rows
    operands = (turned, *ego_edges, *pieces, *weights)
    in_specs = (
        [block(cols, rows, channels)]
        + [block(1, cols, channels)] * 2
        + [block(*x.shape[1:]) for x in pieces]
        + [whole(w) for w in weights]
    )
    aliases = {}
    if before is not None:
        aliases = {len(operands): 0}
        operands += (before,)
        in_specs += [pl.BlockSpec(memory_space=pl.ANY)]
    return pl.pallas_call(
        functools.partial(window_kernel, phase, rows),
        out_shape=jax.ShapeDtypeStruct((vehicles, rows, tile_cols, PHASES, run, width), jnp.bfloat16),
        grid=(vehicles // group,),
        in_specs=in_specs,
        out_specs=pl.BlockSpec(
            (group, rows, tile_cols, None, run, width), lambda r: (r, 0, 0, phase, 0, 0)
        ),
        scratch_shapes=[
            pltpu.VMEM((group * rows * tile_cols * run, width), jnp.float32),
            pltpu.VMEM((2, group * rows * tile_cols * run, channels), jnp.float32),
            pltpu.VMEM((2 * PHASES + 2, most, channels), jnp.float32),
        ],
        input_output_aliases=aliases,
        compiler_params=pltpu.CompilerParams(vmem_limit_bytes=WINDOW_VMEM_BYTES),
        cost_estimate=pl.CostEstimate(
            flops=cells * width * width * 60, bytes_accessed=cells * width * 6, transcendentals=cells * width * 4
        ),
    )(*operands)


def beside(last, first):
    count = lax.axis_size("row")
    above = lax.ppermute(last, "row", [(i, i + 1) for i in range(count - 1)])
    below = lax.ppermute(first, "row", [(i + 1, i) for i in range(count - 1)])
    return above, below


def on_device(
    bev_maps,
    senders,
    shifts,
    counts,
    agent_query,
    agent_keyvalue,
    agent_out,
    agent_scale,
    conv_weight,
    gain_first,
    window_in,
    window_out,
    window_scale,
    gain_second,
    hidden_up,
    hidden_down,
):
    vehicles_here, rows, cols, channels = bev_maps.shape
    devices = lax.axis_size("veh")
    tile_cols = cols // TILE
    tiles = vehicles_here * tile_cols
    group = half_size()
    capacity = tile_cols * max(1, vehicles_here * senders.shape[1] // devices)
    turned, first, second = turn_maps(bev_maps)

    def swap(x):
        return lax.ppermute(x, "veh", [(i, (i + group) % devices) for i in range(devices)])

    def send(messages):
        return [
            lax.ppermute(
                x, "veh", [(i, i // group * group + (i + k + 1) % group) for i in range(devices)]
            )
            for k, x in enumerate(messages)
        ]

    far = swap(first)
    chosen, filled, place, live = plan_of(senders, shifts, counts, tile_cols, capacity)
    live = live.reshape(senders.shape[1], -1)
    near_tiles = send(messages_for(chosen, filled, capacity, {0: first}))
    ego_edges = beside(bev_maps[:, rows - 1 :], bev_maps[:, :1])
    far, second = lax.optimization_barrier((far, second))
    far_tiles = send(messages_for(chosen, filled, capacity, {1: far}))
    later = swap(second)
    later_tiles = send(messages_for(chosen, filled, capacity, {0: second, 1: later}))
    arrived = [[first, far, *near_tiles, *far_tiles], [second, later, *later_tiles]]
    slots = lambda n: 2 * tiles + n * capacity
    whole_maps = [((0, tiles, 0),), ((tiles, tiles, 0),)]
    starts = [
        whole_maps
        + [((slots(2 * k), capacity, 0),) for k in range(group - 1)]
        + [((slots(2 * k + 1), capacity, 0),) for k in range(group - 1)],
        whole_maps + [((slots(2 * k), 2 * capacity, 0),) for k in range(group - 1)],
    ]
    result, pieces = None, []
    for phase, own in enumerate((first, second)):
        if phase:
            place, result = lax.optimization_barrier((place, result))
        joined, top, low = join_agents(
            own, arrived[phase], starts[phase], place, live, agent_query, agent_keyvalue, agent_out, agent_scale
        )
        pieces.append((joined, *beside(low, top)))
        result = window_layer(
            phase,
            turned,
            ego_edges,
            pieces,
            result,
            conv_weight,
            gain_first,
            window_in,
            window_out,
            window_scale,
            gain_second,
            hidden_up,
            hidden_down,
        )
    return result.reshape(vehicles_here, rows, cols, 2 * channels)


def solution(mesh):
    split_maps = P("veh", "row", None, None)
    return jax.shard_map(
        on_device,
        mesh=mesh,
        in_specs=(split_maps,) + (P(),) * 15,
        out_specs=split_maps,
        check_vma=False,
    )
```

```python
import functools
import math

import jax
import jax.numpy as jnp
from jax import lax
from jax.experimental import pallas as pl
from jax.experimental.pallas import tpu as pltpu
from jax.sharding import PartitionSpec as P

TILE = 32
WIN = 8
HEAD = 32
ENTRY_BITS = 10

norm_eps = 1e-05
unit_eps = 1e-06
LOG2E = math.log2(math.e)
VMEM_BYTES = 24 * 2**20
WINDOW_VMEM_BYTES = 60 * 2**20
PHASES = 2

NN = (((1,), (0,)), ((), ()))
NT = (((1,), (1,)), ((), ()))
TN = (((0,), (0,)), ((), ()))


def dot(a, b, dims=NN):
    return lax.dot_general(a, b, dims, preferred_element_type=jnp.float32)


def split(x):
    high = x.astype(jnp.bfloat16)
    return high, (x - high.astype(jnp.float32)).astype(jnp.bfloat16)


def head_sums(x):
    return jnp.sum(x.reshape(x.shape[0] // HEAD, HEAD, x.shape[1]), axis=1, keepdims=True)


def by_head(x, factor):
    return (x.reshape(x.shape[0] // HEAD, HEAD, x.shape[1]) * factor).reshape(x.shape)


def phase_columns(phase):
    run = TILE // PHASES
    return [TILE - 1] + list(range(run + 1)) if phase == 0 else list(range(run + 1, TILE - 1))


def half_size():
    return max(1, lax.axis_size("veh") // 2)


def turn_kernel(maps, turned, first, second, scratch):
    rows, cols, channels = maps.shape[1:]
    run = TILE // PHASES
    for i in range(rows):
        scratch[pl.ds(i, cols, stride=rows), :] = maps[0, i].astype(jnp.float32)
    x = scratch[...].astype(jnp.bfloat16).reshape(cols, rows, channels)
    turned[0] = x
    for t in range(cols // TILE):
        tile = x[t * TILE : (t + 1) * TILE]
        first[t] = jnp.concatenate([tile[TILE - 1 :], tile[: run + 1]], axis=0)
        second[t] = tile[run + 1 : TILE - 1]


def turn_maps(maps):
    vehicles, rows, cols, channels = maps.shape
    tile_cols = cols // TILE
    pieces = [(tile_cols, len(phase_columns(p)), rows, channels) for p in range(PHASES)]
    blocks = [(1, cols, rows, channels), *pieces]
    block = lambda shape: pl.BlockSpec(shape, lambda v: (v, 0, 0, 0))
    return pl.pallas_call(
        turn_kernel,
        out_shape=[jax.ShapeDtypeStruct((vehicles * n[0], *n[1:]), maps.dtype) for n in blocks],
        grid=(vehicles,),
        in_specs=[block((1, rows, cols, channels))],
        out_specs=[block(n) for n in blocks],
        scratch_shapes=[pltpu.VMEM((rows * cols, channels), jnp.float32)],
        compiler_params=pltpu.CompilerParams(vmem_limit_bytes=VMEM_BYTES),
        cost_estimate=pl.CostEstimate(flops=0, bytes_accessed=10 * maps.size, transcendentals=0),
    )(maps)


def plan_kernel(sizes, senders, shifts, counts, ids, chosen, filled, entries, listed, sizes_of, live, blank, sent):
    vehicles, agents, tile_cols, group, capacity = sizes
    me, partner = ids[0], ids[1]
    tiles_held = vehicles * tile_cols
    rank = me % group
    pairs = vehicles * agents

    def clear(i, _):
        sent[i] = 0
        return 0

    def clear_list(i, _):
        listed[i] = 0
        return 0

    lax.fori_loop(0, sent.shape[0], clear, 0)
    lax.fori_loop(0, listed.shape[0], clear_list, 0)
    last = blank.shape[0] - 1
    blank[last] = 0

    def target(k, _):
        first = (me - rank + (rank + k + 1) % group) * vehicles

        def pair(i, n):
            r, a = first + i // agents, i % agents
            sender, shift = senders[r, a], shifts[r, a]
            tiles = tile_cols - jnp.abs(shift)
            source = sender // vehicles
            far = jnp.where(source == partner, 1, 0)
            filled_here = jnp.where(far == 1, n[1], n[0])
            fits = (a < counts[r]) & ((source == me) | (far == 1)) & (filled_here + tiles <= capacity)

            @pl.when(fits)
            def _():
                at = (2 * k + far) * capacity + filled_here
                tile = sender % vehicles * tile_cols + jnp.maximum(shift, 0)
                for t in range(tile_cols):

                    @pl.when(t < tiles)
                    def _():
                        chosen[at + t] = tile + t

            more = jnp.where(fits, tiles, 0)
            return n[0] + more * (1 - far), n[1] + more * far

        near, far = lax.fori_loop(0, pairs, pair, (0, 0))
        filled[2 * k] = near
        filled[2 * k + 1] = far
        return 0

    lax.fori_loop(0, group - 1, target, 0)

    def pair(i, _):
        v, a = i // agents, i % agents
        r = me * vehicles + v
        sender, shift = senders[r, a], shifts[r, a]
        alive = a < counts[r]
        source = sender // vehicles
        n = sent[source]
        k = (rank - source % group + group) % group
        apart = jnp.where(source // group == me // group, 0, 1)
        slot = jnp.where(k == 0, sender % vehicles * tile_cols + jnp.maximum(shift, 0), n)
        origin = jnp.where(k == 0, 0, 2 * k) + apart
        tiles = jnp.where(alive, tile_cols - jnp.abs(shift), 0)
        base = a * tiles_held + v * tile_cols
        first = jnp.maximum(-shift, 0)

        @pl.when(tiles > 0)
        def _():
            here = origin * tile_cols + tiles - 1
            entries[here * pairs + listed[here]] = ((base + first) << ENTRY_BITS) + slot
            listed[here] = listed[here] + 1

        sizes_of[a * vehicles + v] = tiles
        for t in range(tile_cols):
            inside = (t >= first) & (t < first + tiles)
            live[base + t] = jnp.where(inside, 1, 0)

            @pl.when(jnp.logical_not(inside))
            def _():
                blank[blank[last]] = base + t
                blank[last] = blank[last] + 1

        sent[source] = n + tiles
        return 0

    lax.fori_loop(0, pairs, pair, 0)


def plan_of(senders, shifts, counts, tile_cols, capacity):
    devices = lax.axis_size("veh")
    group = half_size()
    vehicles, agents = senders.shape[0] // devices, senders.shape[1]
    me = lax.axis_index("veh").astype(jnp.int32)
    ids = jnp.stack([me, (me + group) % devices])
    pairs = agents * vehicles
    places = 2 * group * tile_cols
    sizes = [(group - 1) * 2 * capacity, (group - 1) * 2, places * pairs, places, pairs]
    sizes += [pairs * tile_cols, pairs * tile_cols + 1]
    smem = pl.BlockSpec(memory_space=pltpu.SMEM)
    return pl.pallas_call(
        functools.partial(plan_kernel, (vehicles, agents, tile_cols, group, capacity)),
        out_shape=[jax.ShapeDtypeStruct((n,), jnp.int32) for n in sizes],
        in_specs=[smem] * 4,
        out_specs=[smem] * 7,
        scratch_shapes=[pltpu.SMEM((devices,), jnp.int32)],
        compiler_params=pltpu.CompilerParams(vmem_limit_bytes=VMEM_BYTES),
        cost_estimate=pl.CostEstimate(flops=0, bytes_accessed=20 * 2**20, transcendentals=0),
    )(senders, shifts, counts, ids)


def send_kernel(sources, capacity, chosen, filled, *refs):
    bufs, messages, sems = refs[: len(sources)], refs[len(sources) : -1], refs[-1]
    copies = []
    for k, message in enumerate(messages):
        for b, source in enumerate(sources):

            def copy(i, tile, k=k, b=b, message=message):
                slot = b * capacity + i
                return pltpu.make_async_copy(bufs[b].at[tile], message.at[slot], sems.at[k, slot])

            copies.append((2 * k + source, copy))
    for at, copy in copies:
        lax.fori_loop(
            0, filled[at], lambda i, _: (copy(i, chosen[at * capacity + i]).start(), 0)[1], 0
        )
    for at, copy in copies:
        lax.fori_loop(0, filled[at], lambda i, _: (copy(i, 0).wait(), 0)[1], 0)


def messages_for(chosen, filled, capacity, sources):
    first = next(iter(sources.values()))
    count = filled.shape[0] // 2
    shape = (len(sources) * capacity, *first.shape[1:])
    anywhere = pl.BlockSpec(memory_space=pl.ANY)
    return pl.pallas_call(
        functools.partial(send_kernel, tuple(sources), capacity),
        out_shape=[jax.ShapeDtypeStruct(shape, first.dtype)] * count,
        grid_spec=pltpu.PrefetchScalarGridSpec(
            num_scalar_prefetch=2,
            grid=(1,),
            in_specs=[anywhere] * len(sources),
            out_specs=[anywhere] * count,
            scratch_shapes=[pltpu.SemaphoreType.DMA((count, shape[0]))],
        ),
        compiler_params=pltpu.CompilerParams(vmem_limit_bytes=VMEM_BYTES),
        cost_estimate=pl.CostEstimate(
            flops=0, bytes_accessed=4 * count * math.prod(shape), transcendentals=0
        ),
    )(chosen, filled, *sources.values())


LANES = 256


def join_kernel(origins, tile_cols, entries, listed, sizes_of, blank, ego, *refs):
    buffers = 1 + max(b for b, _ in origins)
    bufs, refs = refs[:buffers], refs[buffers:]
    present, wq, wkv, wout, scale, out, top_row, low_row, landed, joined, sems = refs
    count, cells, channels = landed.shape
    agents = present.shape[0]
    pieces = count // agents
    vehicles = pieces // tile_cols
    total = pieces * cells
    pairs = agents * vehicles

    def copy(source, at, size, pair):
        return pltpu.make_async_copy(source, landed.at[pl.ds(at, size)], sems.at[pair])

    for origin, (b, offset) in enumerate(origins):
        for size in range(tile_cols, 0, -1):
            place = origin * tile_cols + size - 1

            def fetch(i, _, b=b, offset=offset, size=size, place=place):
                entry = entries[place * pairs + i]
                at, tile = entry >> ENTRY_BITS, entry & ((1 << ENTRY_BITS) - 1)
                copy(bufs[b].at[pl.ds(tile + offset, size)], at, size, at // tile_cols).start()
                return 0

            lax.fori_loop(0, listed[place], fetch, 0)

    def clear(i, _):
        landed[blank[i]] = jnp.zeros((cells, channels), landed.dtype)
        return 0

    lax.fori_loop(0, blank[blank.shape[0] - 1], clear, 0)
    arrived = 0
    heads = channels // HEAD
    scale_col = scale[...].reshape(heads, 1, 1)
    landed_cells = landed.reshape(agents, total, channels)
    for c in range(total // LANES):
        while arrived * tile_cols * cells < (c + 1) * LANES:
            for a in range(agents):
                for size in range(1, tile_cols + 1):
                    pair = a * vehicles + arrived

                    @pl.when(sizes_of[pair] == size)
                    def _(size=size, pair=pair):
                        copy(bufs[0].at[pl.ds(0, size)], pair * tile_cols, size, pair).wait()

            arrived += 1
        span = pl.ds(c * LANES, LANES)
        cells_here = ego[span, :]
        queries = dot(wq[...], cells_here, NT)
        factor = lax.rsqrt(head_sums(queries * queries) + unit_eps) * scale_col

        def agent(x):
            kv = dot(wkv[...], x, NT).astype(jnp.bfloat16).astype(jnp.float32)
            keys, values = kv[:channels], kv[channels:]
            score = head_sums(queries * keys) * factor
            return score * lax.rsqrt(head_sums(keys * keys) + unit_eps), values

        scores, values = zip(
            agent(cells_here),
            *(
                agent(landed_cells[a, span, :])
                for a in range(agents)
            ),
        )
        scores = [scores[0]] + [
            jnp.where(present[a : a + 1, c * LANES : (c + 1) * LANES].reshape(1, 1, LANES) > 0, s, -1e30)
            for a, s in enumerate(scores[1:])
        ]
        top = functools.reduce(jnp.maximum, scores)
        weights = [jnp.exp(s - top) for s in scores]
        inverse = 1.0 / functools.reduce(jnp.add, weights)
        mix = functools.reduce(jnp.add, [by_head(v, w * inverse) for w, v in zip(weights, values)])
        joined[span, :] = dot(mix.astype(jnp.bfloat16), wout[...], TN)
    out[...] = joined[...].astype(jnp.bfloat16)
    rows = total // top_row.shape[0]
    top_row[...] = joined[pl.ds(0, total // rows, stride=rows), :].astype(jnp.bfloat16)
    low_row[...] = joined[pl.ds(rows - 1, total // rows, stride=rows), :].astype(jnp.bfloat16)


def join_agents(pieces, arrived, origins, tile_cols, plan, live, wq, wkv, wout, scale):
    count, cols, rows, channels = pieces.shape
    agents = live.shape[0]
    cells = cols * rows
    total = count * cells
    whole = lambda shape: pl.BlockSpec(shape, lambda r, *_: (0,) * len(shape))
    weights = (wq.T, wkv.T, wout, scale.reshape(-1, 1))
    present = jnp.repeat(live.astype(jnp.float32), cells, axis=1)
    shapes = [(n, channels) for n in (total, total // rows, total // rows)]
    return pl.pallas_call(
        functools.partial(join_kernel, origins, tile_cols),
        out_shape=[jax.ShapeDtypeStruct(shape, jnp.bfloat16) for shape in shapes],
        grid_spec=pltpu.PrefetchScalarGridSpec(
            num_scalar_prefetch=4,
            grid=(1,),
            in_specs=[
                whole((total, channels)),
                *[pl.BlockSpec(memory_space=pl.ANY)] * len(arrived),
                whole(present.shape),
            ]
            + [whole(w.shape) for w in weights],
            out_specs=[whole(shape) for shape in shapes],
            scratch_shapes=[
                pltpu.VMEM((agents * count, cells, channels), jnp.bfloat16),
                pltpu.VMEM((total, channels), jnp.float32),
                pltpu.SemaphoreType.DMA((agents * count // tile_cols,)),
            ],
        ),
        compiler_params=pltpu.CompilerParams(vmem_limit_bytes=VMEM_BYTES),
        cost_estimate=pl.CostEstimate(
            flops=total * channels * channels * 40, bytes_accessed=total * channels * 12, transcendentals=total * 20
        ),
    )(
        *plan,
        pieces.reshape(total, channels),
        *(x.reshape(-1, cells, channels) for x in arrived),
        present,
        *weights,
    )


def norm(x, gain):
    average = jnp.mean(x, axis=-1, keepdims=True)
    centred = x - average
    spread = jnp.mean(centred * centred, axis=-1, keepdims=True)
    return (centred * lax.rsqrt(spread + norm_eps) * gain).astype(jnp.bfloat16)


def spread_rows(ref, rows_of, at, rows):
    count, channels = rows_of.shape
    ref[pl.ds(at, count, stride=rows), :] = rows_of.astype(jnp.float32)
    return ref[: count * rows].reshape(count, rows, channels)


def runs_of(phase, tile_cols, whole_map, pieces):
    run = TILE // PHASES
    out = []
    for t in range(tile_cols):
        first = t * TILE + phase * run - 1
        if pieces is None:
            last = first + run + 2
            blank = jnp.zeros_like(whole_map[:1])
            body = whole_map[max(first, 0) : min(last, tile_cols * TILE)]
            parts = ([blank] if first < 0 else []) + [body] + ([blank] if last > tile_cols * TILE else [])
        else:
            size = run + 2
            one = pieces[0]
            blank = jnp.zeros_like(one[:1])
            if phase == 0:
                left = one[(t - 1) * size : (t - 1) * size + 1] if t else blank
                parts = [left, one[t * size + 1 : (t + 1) * size]]
            else:
                rest = TILE - size
                right = one[(t + 1) * size + 1 : (t + 1) * size + 2] if t + 1 < tile_cols else blank
                parts = [
                    one[t * size + run : (t + 1) * size],
                    pieces[1][t * rest : (t + 1) * rest],
                    one[t * size : t * size + 1],
                    right,
                ]
        out.append(jnp.concatenate(parts, axis=0))
    return out


def taps_of(runs, above, below, taps):
    out = []
    for x, first, last in zip(runs, above, below):
        cols, rows, channels = x.shape
        row = lax.broadcasted_iota(jnp.int32, (rows, channels), 0)[None]
        flat = x.reshape(cols * rows, channels)
        over = jnp.where(row == 0, first, pltpu.roll(flat, 1, 0).reshape(x.shape))
        under = jnp.where(row == rows - 1, last, pltpu.roll(flat, cols * rows - 1, 0).reshape(x.shape))
        total = x[1 : cols - 1]
        for j in range(3):
            span = slice(j, cols - 2 + j)
            total = total + over[span] * taps[j] + x[span] * taps[3 + j] + under[span] * taps[6 + j]
        out.append(total.reshape((cols - 2) * rows, channels))
    return out


def window_kernel(phase, rows, *refs):
    ego, ego_up, ego_down, refs = *refs[:3], refs[3:]
    pieces, refs = [refs[3 * p : 3 * p + 3] for p in range(phase + 1)], refs[3 * phase + 3 :]
    taps, gain_one, wq, wk, wv, wo, scale, gain_two, up, down = refs[:10]
    out, mixed_ref, result_ref, halo = refs[10 + phase :]
    group_size, cols, _, channels = ego.shape
    tile_cols = cols // TILE
    run = TILE // PHASES
    width = 2 * channels
    in_window = rows * WIN
    here = tile_cols * run * rows
    cells = group_size * here
    windows = cells // in_window
    heads = width // HEAD
    f32 = jnp.float32
    for v in range(group_size):
        for half in range(2):
            lanes = slice(half * channels, (half + 1) * channels)
            weights = [taps[i : i + 1, lanes].reshape(1, 1, channels) for i in range(9)]
            if half == 0:
                centre = runs_of(phase, tile_cols, ego[v].astype(f32), None)
                above = runs_of(phase, tile_cols, spread_rows(halo.at[0], ego_up[v, 0], 0, rows), None)
                below = runs_of(phase, tile_cols, spread_rows(halo.at[1], ego_down[v, 0], rows - 1, rows), None)
            else:
                centre, above, below = [], [], []
                for p, (x, first, last) in enumerate(pieces):
                    centre.append(x[v].astype(f32).reshape(-1, rows, channels))
                    above.append(spread_rows(halo.at[2 + 2 * p], first[v], 0, rows))
                    below.append(spread_rows(halo.at[3 + 2 * p], last[v], rows - 1, rows))
                centre, above, below = (runs_of(phase, tile_cols, None, x) for x in (centre, above, below))
            for t, part in enumerate(taps_of(centre, above, below, weights)):
                at = v * here + t * run * rows
                mixed_ref[at : at + run * rows, lanes] = part
    hidden = norm(mixed_ref[...], gain_one[...])
    queries = dot(wq[...], hidden, NT)
    values = dot(wv[...], hidden, NT).astype(jnp.bfloat16)
    keys = dot(hidden, wk[...])
    factor = lax.rsqrt(head_sums(queries * queries) + unit_eps) * scale[...].reshape(heads, 1, 1)
    queries = by_head(queries, factor)
    member = (
        lax.broadcasted_iota(jnp.int32, (width, width), 0) // HEAD
        == lax.broadcasted_iota(jnp.int32, (width, width), 1) // HEAD
    ).astype(f32).astype(jnp.bfloat16)
    square_high, square_low = split(keys * keys)
    keys = keys * lax.rsqrt(dot(square_high, member) + dot(square_low, member) + unit_eps)
    key_high, key_low = split(keys)

    pair = 2 * in_window
    group = 4 * HEAD
    lane = lax.broadcasted_iota(jnp.int32, (width, pair), 1) < in_window
    even = (lax.broadcasted_iota(jnp.int32, (width, pair), 0) // HEAD) % 2 == 0
    blank = jnp.zeros((2 * HEAD, pair), jnp.bfloat16)
    blank_p = jnp.zeros((in_window, 4 * in_window), jnp.bfloat16)
    lane_head = lax.broadcasted_iota(jnp.int32, (HEAD, pair), 1) < in_window
    rights = []
    for p in range(windows // 2):
        straight = queries[:, p * pair : (p + 1) * pair]
        turned = pltpu.roll(straight, in_window, 1)
        for w in range(2):
            low, high = (straight, turned) if w == 0 else (turned, straight)
            rights.append(split(jnp.where(even, jnp.where(lane, low, 0.0), jnp.where(lane, 0.0, high))))

    def right(block, g):
        block = block[g * group : (g + 1) * group]
        return jnp.concatenate(
            [
                jnp.concatenate([block[: 2 * HEAD], blank], axis=1),
                jnp.concatenate([blank, block[2 * HEAD :]], axis=1),
            ],
            axis=0,
        )

    groups = width // group
    scores = []
    for w in range(windows):
        for g in range(groups):
            span = slice(w * in_window, (w + 1) * in_window), slice(g * group, (g + 1) * group)
            both = dot(jnp.concatenate([key_high[span], key_low[span]], axis=0), right(rights[w][0], g))
            scores.append(both[:in_window] + both[in_window:] + dot(key_high[span], right(rights[w][1], g)))
    probs = []
    for score in scores:
        weight = jnp.exp2(score - jnp.max(score, axis=0, keepdims=True))
        probs.append((weight * (1.0 / jnp.sum(weight, axis=0, keepdims=True))).astype(jnp.bfloat16))
    attended = []
    for p in range(windows // 2):
        parts = []
        for g in range(groups):
            v = values[g * group : (g + 1) * group, p * pair : (p + 1) * pair]
            first = dot(v, jnp.concatenate([probs[2 * p * groups + g], blank_p], axis=0))
            second = dot(v, jnp.concatenate([blank_p, probs[(2 * p + 1) * groups + g]], axis=0))
            for h in range(4):
                rows_of = slice(h * HEAD, (h + 1) * HEAD)
                cols_of = slice((h // 2) * pair, (h // 2 + 1) * pair)
                a, b = first[rows_of, cols_of], second[rows_of, cols_of]
                if h % 2 == 0:
                    b = pltpu.roll(b, in_window, 1)
                else:
                    a = pltpu.roll(a, in_window, 1)
                parts.append(jnp.where(lane_head, a, b))
        attended.append(jnp.concatenate(parts, axis=0).astype(jnp.bfloat16))
    attended = jnp.concatenate(attended, axis=1)
    mixed = mixed_ref[...] + dot(attended, wo[...], TN)
    hidden = norm(mixed, gain_two[...])
    inner = dot(hidden, up[...])
    inner = (0.5 * inner * (1.0 + jnp.tanh(0.5 * inner))).astype(jnp.bfloat16)
    result = mixed + dot(inner, down[...])
    for half in range(2):
        result_ref[half] = result[:, half * channels : (half + 1) * channels]
    for v in range(group_size):
        for t in range(tile_cols):
            for i in range(rows):
                at = v * here + t * run * rows + i
                for half in range(2):
                    lanes = slice(half * channels, (half + 1) * channels)
                    line = result_ref[half, pl.ds(at, run, stride=rows), :]
                    out[v, i, t, :, lanes] = line.astype(jnp.bfloat16)


def window_layer(phase, turned, ego_edges, pieces, before, conv_weight, gain_first, window_in, window_out,
                 window_scale, gain_second, hidden_up, hidden_down):
    vehicles, cols, rows, channels = turned.shape
    width = 2 * channels
    tile_cols = cols // TILE
    run = TILE // PHASES
    group = 4
    whole = lambda x: pl.BlockSpec(x.shape, lambda r: (0,) * x.ndim)
    block = lambda *shape: pl.BlockSpec((group, *shape), lambda r: (r,) + (0,) * len(shape))
    weights = (
        conv_weight.reshape(9, width),
        gain_first[None],
        window_in[:, :width].T,
        window_in[:, width : 2 * width],
        window_in[:, 2 * width :].T,
        window_out,
        (window_scale * LOG2E).reshape(-1, 1),
        gain_second[None],
        hidden_up,
        hidden_down,
    )
    pieces = [x.reshape(vehicles, -1, channels) for three in pieces for x in three]
    cells = vehicles * rows * tile_cols * run
    most = cols * rows
    operands = (turned, *ego_edges, *pieces, *weights)
    in_specs = (
        [block(cols, rows, channels)]
        + [block(1, cols, channels)] * 2
        + [block(*x.shape[1:]) for x in pieces]
        + [whole(w) for w in weights]
    )
    aliases = {}
    if before is not None:
        aliases = {len(operands): 0}
        operands += (before,)
        in_specs += [pl.BlockSpec(memory_space=pl.ANY)]
    return pl.pallas_call(
        functools.partial(window_kernel, phase, rows),
        out_shape=jax.ShapeDtypeStruct((vehicles, rows, tile_cols, PHASES, run, width), jnp.bfloat16),
        grid=(vehicles // group,),
        in_specs=in_specs,
        out_specs=pl.BlockSpec(
            (group, rows, tile_cols, None, run, width), lambda r: (r, 0, 0, phase, 0, 0)
        ),
        scratch_shapes=[
            pltpu.VMEM((group * rows * tile_cols * run, width), jnp.float32),
            pltpu.VMEM((2, group * rows * tile_cols * run, channels), jnp.float32),
            pltpu.VMEM((2 * PHASES + 2, most, channels), jnp.float32),
        ],
        input_output_aliases=aliases,
        compiler_params=pltpu.CompilerParams(vmem_limit_bytes=WINDOW_VMEM_BYTES),
        cost_estimate=pl.CostEstimate(
            flops=cells * width * width * 60, bytes_accessed=cells * width * 6, transcendentals=cells * width * 4
        ),
    )(*operands)


def beside(last, first):
    count = lax.axis_size("row")
    above = lax.ppermute(last, "row", [(i, i + 1) for i in range(count - 1)])
    below = lax.ppermute(first, "row", [(i + 1, i) for i in range(count - 1)])
    return above, below


def on_device(
    bev_maps,
    senders,
    shifts,
    counts,
    agent_query,
    agent_keyvalue,
    agent_out,
    agent_scale,
    conv_weight,
    gain_first,
    window_in,
    window_out,
    window_scale,
    gain_second,
    hidden_up,
    hidden_down,
):
    vehicles_here, rows, cols, channels = bev_maps.shape
    devices = lax.axis_size("veh")
    tile_cols = cols // TILE
    group = half_size()
    capacity = tile_cols * max(1, vehicles_here * senders.shape[1] // devices)
    turned, first, second = turn_maps(bev_maps)

    def swap(x):
        return lax.ppermute(x, "veh", [(i, (i + group) % devices) for i in range(devices)])

    def send(messages):
        return [
            lax.ppermute(
                x, "veh", [(i, i // group * group + (i + k + 1) % group) for i in range(devices)]
            )
            for k, x in enumerate(messages)
        ]

    far = swap(first)
    chosen, filled, *plan = plan_of(senders, shifts, counts, tile_cols, capacity)
    entries, listed, sizes_of, live, blank = plan
    plan = (entries, listed, sizes_of, blank)
    live = live.reshape(senders.shape[1], -1)
    near_tiles = send(messages_for(chosen, filled, capacity, {0: first}))
    ego_edges = beside(bev_maps[:, rows - 1 :], bev_maps[:, :1])
    far, second = lax.optimization_barrier((far, second))
    far_tiles = send(messages_for(chosen, filled, capacity, {1: far}))
    later = swap(second)
    later_tiles = send(messages_for(chosen, filled, capacity, {0: second, 1: later}))
    arrived = [[first, far, *near_tiles, *far_tiles], [second, later, *later_tiles]]
    origins = [
        [(0, 0), (1, 0)] + [(2 + k + part * (group - 1), 0) for k in range(group - 1) for part in (0, 1)],
        [(0, 0), (1, 0)] + [(2 + k, part * capacity) for k in range(group - 1) for part in (0, 1)],
    ]
    result, pieces = None, []
    for phase, own in enumerate((first, second)):
        if phase:
            plan, result = lax.optimization_barrier((plan, result))
        joined, top, low = join_agents(
            own, arrived[phase], origins[phase], tile_cols, plan, live, agent_query, agent_keyvalue, agent_out, agent_scale
        )
        pieces.append((joined, *beside(low, top)))
        result = window_layer(
            phase,
            turned,
            ego_edges,
            pieces,
            result,
            conv_weight,
            gain_first,
            window_in,
            window_out,
            window_scale,
            gain_second,
            hidden_up,
            hidden_down,
        )
    return result.reshape(vehicles_here, rows, cols, 2 * channels)


def solution(mesh):
    split_maps = P("veh", "row", None, None)
    return jax.shard_map(
        on_device,
        mesh=mesh,
        in_specs=(split_maps,) + (P(),) * 15,
        out_specs=split_maps,
        check_vma=False,
    )
```

```python
import functools
import math

import jax
import jax.numpy as jnp
from jax import lax
from jax.experimental import pallas as pl
from jax.experimental.pallas import tpu as pltpu
from jax.sharding import PartitionSpec as P

TILE = 32
WIN = 8
HEAD = 32
ENTRY_BITS = 10

norm_eps = 1e-05
unit_eps = 1e-06
LOG2E = math.log2(math.e)
VMEM_BYTES = 24 * 2**20
COST = pl.CostEstimate(flops=0, bytes_accessed=2**16, transcendentals=0)
WINDOW_VMEM_BYTES = 60 * 2**20
PHASES = 2

NN = (((1,), (0,)), ((), ()))
NT = (((1,), (1,)), ((), ()))
TN = (((0,), (0,)), ((), ()))


def dot(a, b, dims=NN):
    return lax.dot_general(a, b, dims, preferred_element_type=jnp.float32)


def split(x):
    high = x.astype(jnp.bfloat16)
    return high, (x - high.astype(jnp.float32)).astype(jnp.bfloat16)


def head_sums(x):
    return jnp.sum(x.reshape(x.shape[0] // HEAD, HEAD, x.shape[1]), axis=1, keepdims=True)


def by_head(x, factor):
    return (x.reshape(x.shape[0] // HEAD, HEAD, x.shape[1]) * factor).reshape(x.shape)


def phase_columns(phase):
    run = TILE // PHASES
    return [TILE - 1] + list(range(run + 1)) if phase == 0 else list(range(run + 1, TILE - 1))


def half_size():
    return max(1, lax.axis_size("veh") // 2)


def turn_kernel(maps, turned, first, second, scratch):
    rows, cols, channels = maps.shape[1:]
    run = TILE // PHASES
    for i in range(rows):
        scratch[pl.ds(i, cols, stride=rows), :] = maps[0, i].astype(jnp.float32)
    x = scratch[...].astype(jnp.bfloat16).reshape(cols, rows, channels)
    turned[0] = x
    for t in range(cols // TILE):
        tile = x[t * TILE : (t + 1) * TILE]
        first[t] = jnp.concatenate([tile[TILE - 1 :], tile[: run + 1]], axis=0)
        second[t] = tile[run + 1 : TILE - 1]


def turn_maps(maps):
    vehicles, rows, cols, channels = maps.shape
    tile_cols = cols // TILE
    pieces = [(tile_cols, len(phase_columns(p)), rows, channels) for p in range(PHASES)]
    blocks = [(1, cols, rows, channels), *pieces]
    block = lambda shape: pl.BlockSpec(shape, lambda v: (v, 0, 0, 0))
    return pl.pallas_call(
        turn_kernel,
        out_shape=[jax.ShapeDtypeStruct((vehicles * n[0], *n[1:]), maps.dtype) for n in blocks],
        grid=(vehicles,),
        in_specs=[block((1, rows, cols, channels))],
        out_specs=[block(n) for n in blocks],
        scratch_shapes=[pltpu.VMEM((rows * cols, channels), jnp.float32)],
        compiler_params=pltpu.CompilerParams(vmem_limit_bytes=VMEM_BYTES),
        cost_estimate=COST,
    )(maps)


def plan_kernel(sizes, senders, shifts, counts, ids, chosen, filled, entries, listed, sizes_of, live, blank, sent):
    vehicles, agents, tile_cols, group, capacity = sizes
    me, partner = ids[0], ids[1]
    tiles_held = vehicles * tile_cols
    rank = me % group
    pairs = vehicles * agents

    def clear(i, _):
        sent[i] = 0
        return 0

    def clear_list(i, _):
        listed[i] = 0
        return 0

    lax.fori_loop(0, sent.shape[0], clear, 0)
    lax.fori_loop(0, listed.shape[0], clear_list, 0)
    last = blank.shape[0] - 1
    blank[last] = 0

    def target(k, _):
        first = (me - rank + (rank + k + 1) % group) * vehicles

        def pair(i, n):
            r, a = first + i // agents, i % agents
            sender, shift = senders[r, a], shifts[r, a]
            tiles = tile_cols - jnp.abs(shift)
            source = sender // vehicles
            far = jnp.where(source == partner, 1, 0)
            filled_here = jnp.where(far == 1, n[1], n[0])
            fits = (a < counts[r]) & ((source == me) | (far == 1)) & (filled_here + tiles <= capacity)

            @pl.when(fits)
            def _():
                at = (2 * k + far) * capacity + filled_here
                tile = sender % vehicles * tile_cols + jnp.maximum(shift, 0)
                for t in range(tile_cols):

                    @pl.when(t < tiles)
                    def _():
                        chosen[at + t] = tile + t

            more = jnp.where(fits, tiles, 0)
            return n[0] + more * (1 - far), n[1] + more * far

        near, far = lax.fori_loop(0, pairs, pair, (0, 0))
        filled[2 * k] = near
        filled[2 * k + 1] = far
        return 0

    lax.fori_loop(0, group - 1, target, 0)

    def pair(i, _):
        v, a = i // agents, i % agents
        r = me * vehicles + v
        sender, shift = senders[r, a], shifts[r, a]
        alive = a < counts[r]
        source = sender // vehicles
        n = sent[source]
        k = (rank - source % group + group) % group
        apart = jnp.where(source // group == me // group, 0, 1)
        slot = jnp.where(k == 0, sender % vehicles * tile_cols + jnp.maximum(shift, 0), n)
        origin = jnp.where(k == 0, 0, 2 * k) + apart
        tiles = jnp.where(alive, tile_cols - jnp.abs(shift), 0)
        base = a * tiles_held + v * tile_cols
        first = jnp.maximum(-shift, 0)

        @pl.when(tiles > 0)
        def _():
            here = origin * tile_cols + tiles - 1
            entries[here * pairs + listed[here]] = ((base + first) << ENTRY_BITS) + slot
            listed[here] = listed[here] + 1

        sizes_of[a * vehicles + v] = tiles
        for t in range(tile_cols):
            inside = (t >= first) & (t < first + tiles)
            live[base + t] = jnp.where(inside, 1, 0)

            @pl.when(jnp.logical_not(inside))
            def _():
                blank[blank[last]] = base + t
                blank[last] = blank[last] + 1

        sent[source] = n + tiles
        return 0

    lax.fori_loop(0, pairs, pair, 0)


def plan_of(senders, shifts, counts, tile_cols, capacity):
    devices = lax.axis_size("veh")
    group = half_size()
    vehicles, agents = senders.shape[0] // devices, senders.shape[1]
    me = lax.axis_index("veh").astype(jnp.int32)
    ids = jnp.stack([me, (me + group) % devices])
    pairs = agents * vehicles
    places = 2 * group * tile_cols
    sizes = [(group - 1) * 2 * capacity, (group - 1) * 2, places * pairs, places, pairs]
    sizes += [pairs * tile_cols, pairs * tile_cols + 1]
    smem = pl.BlockSpec(memory_space=pltpu.SMEM)
    return pl.pallas_call(
        functools.partial(plan_kernel, (vehicles, agents, tile_cols, group, capacity)),
        out_shape=[jax.ShapeDtypeStruct((n,), jnp.int32) for n in sizes],
        in_specs=[smem] * 4,
        out_specs=[smem] * 7,
        scratch_shapes=[pltpu.SMEM((devices,), jnp.int32)],
        compiler_params=pltpu.CompilerParams(vmem_limit_bytes=VMEM_BYTES),
        cost_estimate=COST,
    )(senders, shifts, counts, ids)


def send_kernel(sources, capacity, chosen, filled, *refs):
    bufs, messages, sems = refs[: len(sources)], refs[len(sources) : -1], refs[-1]
    copies = []
    for k, message in enumerate(messages):
        for b, source in enumerate(sources):

            def copy(i, tile, k=k, b=b, message=message):
                slot = b * capacity + i
                return pltpu.make_async_copy(bufs[b].at[tile], message.at[slot], sems.at[k, slot])

            copies.append((2 * k + source, copy))
    for at, copy in copies:
        lax.fori_loop(
            0, filled[at], lambda i, _: (copy(i, chosen[at * capacity + i]).start(), 0)[1], 0
        )
    for at, copy in copies:
        lax.fori_loop(0, filled[at], lambda i, _: (copy(i, 0).wait(), 0)[1], 0)


def messages_for(chosen, filled, capacity, sources):
    first = next(iter(sources.values()))
    count = filled.shape[0] // 2
    shape = (len(sources) * capacity, *first.shape[1:])
    anywhere = pl.BlockSpec(memory_space=pl.ANY)
    return pl.pallas_call(
        functools.partial(send_kernel, tuple(sources), capacity),
        out_shape=[jax.ShapeDtypeStruct(shape, first.dtype)] * count,
        grid_spec=pltpu.PrefetchScalarGridSpec(
            num_scalar_prefetch=2,
            grid=(1,),
            in_specs=[anywhere] * len(sources),
            out_specs=[anywhere] * count,
            scratch_shapes=[pltpu.SemaphoreType.DMA((count, shape[0]))],
        ),
        compiler_params=pltpu.CompilerParams(vmem_limit_bytes=VMEM_BYTES),
        cost_estimate=COST,
    )(chosen, filled, *sources.values())


LANES = 256


def join_kernel(origins, tile_cols, entries, listed, sizes_of, blank, ego, *refs):
    buffers = 1 + max(b for b, _ in origins)
    bufs, refs = refs[:buffers], refs[buffers:]
    present, wq, wkv, wout, scale, out, top_row, low_row, landed, joined, sems = refs
    count, cells, channels = landed.shape
    agents = present.shape[0]
    pieces = count // agents
    vehicles = pieces // tile_cols
    total = pieces * cells
    pairs = agents * vehicles

    def copy(source, at, size, pair):
        return pltpu.make_async_copy(source, landed.at[pl.ds(at, size)], sems.at[pair])

    for origin, (b, offset) in enumerate(origins):
        for size in range(tile_cols, 0, -1):
            place = origin * tile_cols + size - 1

            def fetch(i, _, b=b, offset=offset, size=size, place=place):
                entry = entries[place * pairs + i]
                at, tile = entry >> ENTRY_BITS, entry & ((1 << ENTRY_BITS) - 1)
                copy(bufs[b].at[pl.ds(tile + offset, size)], at, size, at // tile_cols).start()
                return 0

            lax.fori_loop(0, listed[place], fetch, 0)

    def clear(i, _):
        landed[blank[i]] = jnp.zeros((cells, channels), landed.dtype)
        return 0

    lax.fori_loop(0, blank[blank.shape[0] - 1], clear, 0)
    arrived = 0
    heads = channels // HEAD
    scale_col = scale[...].reshape(heads, 1, 1)
    landed_cells = landed.reshape(agents, total, channels)
    for c in range(total // LANES):
        while arrived * tile_cols * cells < (c + 1) * LANES:
            for a in range(agents):
                for size in range(1, tile_cols + 1):
                    pair = a * vehicles + arrived

                    @pl.when(sizes_of[pair] == size)
                    def _(size=size, pair=pair):
                        copy(bufs[0].at[pl.ds(0, size)], pair * tile_cols, size, pair).wait()

            arrived += 1
        span = pl.ds(c * LANES, LANES)
        cells_here = ego[span, :]
        queries = dot(wq[...], cells_here, NT)
        factor = lax.rsqrt(head_sums(queries * queries) + unit_eps) * scale_col

        def agent(x):
            kv = dot(wkv[...], x, NT).astype(jnp.bfloat16).astype(jnp.float32)
            keys, values = kv[:channels], kv[channels:]
            score = head_sums(queries * keys) * factor
            return score * lax.rsqrt(head_sums(keys * keys) + unit_eps), values

        scores, values = zip(
            agent(cells_here),
            *(
                agent(landed_cells[a, span, :])
                for a in range(agents)
            ),
        )
        scores = [scores[0]] + [
            jnp.where(present[a : a + 1, c * LANES : (c + 1) * LANES].reshape(1, 1, LANES) > 0, s, -1e30)
            for a, s in enumerate(scores[1:])
        ]
        top = functools.reduce(jnp.maximum, scores)
        weights = [jnp.exp(s - top) for s in scores]
        inverse = 1.0 / functools.reduce(jnp.add, weights)
        mix = functools.reduce(jnp.add, [by_head(v, w * inverse) for w, v in zip(weights, values)])
        joined[span, :] = dot(mix.astype(jnp.bfloat16), wout[...], TN)
    out[...] = joined[...].astype(jnp.bfloat16)
    edge = top_row.shape[1]
    rows = total // (vehicles * edge)
    for v in range(vehicles):
        start = v * edge * rows
        top_row[v] = joined[pl.ds(start, edge, stride=rows), :].astype(jnp.bfloat16)
        low_row[v] = joined[pl.ds(start + rows - 1, edge, stride=rows), :].astype(jnp.bfloat16)


def join_weights(wq, wkv, wout, scale):
    return wq.T, wkv.T, wout, scale.reshape(-1, 1)


def present_cells(live, phase, rows):
    return jnp.repeat(live.astype(jnp.float32), len(phase_columns(phase)) * rows, axis=1)


def join_agents(pieces, arrived, origins, tile_cols, plan, present, weights):
    count, cols, rows, channels = pieces.shape
    agents = present.shape[0]
    cells = cols * rows
    total = count * cells
    whole = lambda shape: pl.BlockSpec(shape, lambda r, *_: (0,) * len(shape))
    shapes = [(total, channels)] + [(count // tile_cols, tile_cols * cols, channels)] * 2
    return pl.pallas_call(
        functools.partial(join_kernel, origins, tile_cols),
        out_shape=[jax.ShapeDtypeStruct(shape, jnp.bfloat16) for shape in shapes],
        grid_spec=pltpu.PrefetchScalarGridSpec(
            num_scalar_prefetch=4,
            grid=(1,),
            in_specs=[
                whole((total, channels)),
                *[pl.BlockSpec(memory_space=pl.ANY)] * len(arrived),
                whole(present.shape),
            ]
            + [whole(w.shape) for w in weights],
            out_specs=[whole(shape) for shape in shapes],
            scratch_shapes=[
                pltpu.VMEM((agents * count, cells, channels), jnp.bfloat16),
                pltpu.VMEM((total, channels), jnp.float32),
                pltpu.SemaphoreType.DMA((agents * count // tile_cols,)),
            ],
        ),
        compiler_params=pltpu.CompilerParams(vmem_limit_bytes=VMEM_BYTES),
        cost_estimate=COST,
    )(
        *plan,
        pieces.reshape(total, channels),
        *(x.reshape(-1, cells, channels) for x in arrived),
        present,
        *weights,
    )


def norm(x, gain):
    average = jnp.mean(x, axis=-1, keepdims=True)
    centred = x - average
    spread = jnp.mean(centred * centred, axis=-1, keepdims=True)
    return (centred * lax.rsqrt(spread + norm_eps) * gain).astype(jnp.bfloat16)


def spread_rows(ref, rows_of, at, rows):
    count, channels = rows_of.shape
    ref[pl.ds(at, count, stride=rows), :] = rows_of.astype(jnp.float32)
    return ref[: count * rows].reshape(count, rows, channels)


def runs_of(phase, tile_cols, whole_map, pieces):
    run = TILE // PHASES
    out = []
    for t in range(tile_cols):
        first = t * TILE + phase * run - 1
        if pieces is None:
            last = first + run + 2
            blank = jnp.zeros_like(whole_map[:1])
            body = whole_map[max(first, 0) : min(last, tile_cols * TILE)]
            parts = ([blank] if first < 0 else []) + [body] + ([blank] if last > tile_cols * TILE else [])
        else:
            size = run + 2
            one = pieces[0]
            blank = jnp.zeros_like(one[:1])
            if phase == 0:
                left = one[(t - 1) * size : (t - 1) * size + 1] if t else blank
                parts = [left, one[t * size + 1 : (t + 1) * size]]
            else:
                rest = TILE - size
                right = one[(t + 1) * size + 1 : (t + 1) * size + 2] if t + 1 < tile_cols else blank
                parts = [
                    one[t * size + run : (t + 1) * size],
                    pieces[1][t * rest : (t + 1) * rest],
                    one[t * size : t * size + 1],
                    right,
                ]
        out.append(jnp.concatenate(parts, axis=0))
    return out


def taps_of(runs, above, below, taps):
    out = []
    for x, first, last in zip(runs, above, below):
        cols, rows, channels = x.shape
        row = lax.broadcasted_iota(jnp.int32, (rows, channels), 0)[None]
        flat = x.reshape(cols * rows, channels)
        over = jnp.where(row == 0, first, pltpu.roll(flat, 1, 0).reshape(x.shape))
        under = jnp.where(row == rows - 1, last, pltpu.roll(flat, cols * rows - 1, 0).reshape(x.shape))
        total = x[1 : cols - 1]
        for j in range(3):
            span = slice(j, cols - 2 + j)
            total = total + over[span] * taps[j] + x[span] * taps[3 + j] + under[span] * taps[6 + j]
        out.append(total.reshape((cols - 2) * rows, channels))
    return out


def window_kernel(phase, rows, *refs):
    ego, ego_up, ego_down, refs = *refs[:3], refs[3:]
    pieces, refs = [refs[3 * p : 3 * p + 3] for p in range(phase + 1)], refs[3 * phase + 3 :]
    taps, gain_one, wq, wk, wv, wo, scale, gain_two, up, down = refs[:10]
    out, mixed_ref, result_ref, halo = refs[10 + phase :]
    group_size, cols, _, channels = ego.shape
    tile_cols = cols // TILE
    run = TILE // PHASES
    width = 2 * channels
    in_window = rows * WIN
    here = tile_cols * run * rows
    cells = group_size * here
    windows = cells // in_window
    heads = width // HEAD
    f32 = jnp.float32
    for v in range(group_size):
        for half in range(2):
            lanes = slice(half * channels, (half + 1) * channels)
            weights = [taps[i : i + 1, lanes].reshape(1, 1, channels) for i in range(9)]
            if half == 0:
                centre = runs_of(phase, tile_cols, ego[v].astype(f32), None)
                above = runs_of(phase, tile_cols, spread_rows(halo.at[0], ego_up[v, 0], 0, rows), None)
                below = runs_of(phase, tile_cols, spread_rows(halo.at[1], ego_down[v, 0], rows - 1, rows), None)
            else:
                centre, above, below = [], [], []
                for p, (x, first, last) in enumerate(pieces):
                    centre.append(x[v].astype(f32).reshape(-1, rows, channels))
                    above.append(spread_rows(halo.at[2 + 2 * p], first[v], 0, rows))
                    below.append(spread_rows(halo.at[3 + 2 * p], last[v], rows - 1, rows))
                centre, above, below = (runs_of(phase, tile_cols, None, x) for x in (centre, above, below))
            for t, part in enumerate(taps_of(centre, above, below, weights)):
                at = v * here + t * run * rows
                mixed_ref[at : at + run * rows, lanes] = part
    hidden = norm(mixed_ref[...], gain_one[...])
    queries = dot(wq[...], hidden, NT)
    values = dot(wv[...], hidden, NT).astype(jnp.bfloat16)
    keys = dot(hidden, wk[...])
    factor = lax.rsqrt(head_sums(queries * queries) + unit_eps) * scale[...].reshape(heads, 1, 1)
    queries = by_head(queries, factor)
    member = (
        lax.broadcasted_iota(jnp.int32, (width, width), 0) // HEAD
        == lax.broadcasted_iota(jnp.int32, (width, width), 1) // HEAD
    ).astype(f32).astype(jnp.bfloat16)
    square_high, square_low = split(keys * keys)
    keys = keys * lax.rsqrt(dot(square_high, member) + dot(square_low, member) + unit_eps)
    key_high, key_low = split(keys)

    pair = 2 * in_window
    group = 4 * HEAD
    lane = lax.broadcasted_iota(jnp.int32, (width, pair), 1) < in_window
    even = (lax.broadcasted_iota(jnp.int32, (width, pair), 0) // HEAD) % 2 == 0
    blank = jnp.zeros((2 * HEAD, pair), jnp.bfloat16)
    blank_p = jnp.zeros((in_window, 4 * in_window), jnp.bfloat16)
    lane_head = lax.broadcasted_iota(jnp.int32, (HEAD, pair), 1) < in_window
    rights = []
    for p in range(windows // 2):
        straight = queries[:, p * pair : (p + 1) * pair]
        turned = pltpu.roll(straight, in_window, 1)
        for w in range(2):
            low, high = (straight, turned) if w == 0 else (turned, straight)
            rights.append(split(jnp.where(even, jnp.where(lane, low, 0.0), jnp.where(lane, 0.0, high))))

    def right(block, g):
        block = block[g * group : (g + 1) * group]
        return jnp.concatenate(
            [
                jnp.concatenate([block[: 2 * HEAD], blank], axis=1),
                jnp.concatenate([blank, block[2 * HEAD :]], axis=1),
            ],
            axis=0,
        )

    groups = width // group
    scores = []
    for w in range(windows):
        for g in range(groups):
            span = slice(w * in_window, (w + 1) * in_window), slice(g * group, (g + 1) * group)
            both = dot(jnp.concatenate([key_high[span], key_low[span]], axis=0), right(rights[w][0], g))
            scores.append(both[:in_window] + both[in_window:] + dot(key_high[span], right(rights[w][1], g)))
    probs = []
    for score in scores:
        weight = jnp.exp2(score - jnp.max(score, axis=0, keepdims=True))
        probs.append((weight * (1.0 / jnp.sum(weight, axis=0, keepdims=True))).astype(jnp.bfloat16))
    attended = []
    for p in range(windows // 2):
        parts = []
        for g in range(groups):
            v = values[g * group : (g + 1) * group, p * pair : (p + 1) * pair]
            first = dot(v, jnp.concatenate([probs[2 * p * groups + g], blank_p], axis=0))
            second = dot(v, jnp.concatenate([blank_p, probs[(2 * p + 1) * groups + g]], axis=0))
            for h in range(4):
                rows_of = slice(h * HEAD, (h + 1) * HEAD)
                cols_of = slice((h // 2) * pair, (h // 2 + 1) * pair)
                a, b = first[rows_of, cols_of], second[rows_of, cols_of]
                if h % 2 == 0:
                    b = pltpu.roll(b, in_window, 1)
                else:
                    a = pltpu.roll(a, in_window, 1)
                parts.append(jnp.where(lane_head, a, b))
        attended.append(jnp.concatenate(parts, axis=0).astype(jnp.bfloat16))
    attended = jnp.concatenate(attended, axis=1)
    mixed = mixed_ref[...] + dot(attended, wo[...], TN)
    hidden = norm(mixed, gain_two[...])
    inner = dot(hidden, up[...])
    inner = (0.5 * inner * (1.0 + jnp.tanh(0.5 * inner))).astype(jnp.bfloat16)
    result = mixed + dot(inner, down[...])
    for half in range(2):
        result_ref[half] = result[:, half * channels : (half + 1) * channels]
    for v in range(group_size):
        for t in range(tile_cols):
            for i in range(rows):
                at = v * here + t * run * rows + i
                for half in range(2):
                    lanes = slice(half * channels, (half + 1) * channels)
                    line = result_ref[half, pl.ds(at, run, stride=rows), :]
                    out[v, i, t, :, lanes] = line.astype(jnp.bfloat16)


def window_weights(conv_weight, gain_first, window_in, window_out, window_scale, gain_second, hidden_up, hidden_down):
    width = conv_weight.shape[-1]
    return (
        conv_weight.reshape(9, width),
        gain_first[None],
        window_in[:, :width].T,
        window_in[:, width : 2 * width],
        window_in[:, 2 * width :].T,
        window_out,
        (window_scale * LOG2E).reshape(-1, 1),
        gain_second[None],
        hidden_up,
        hidden_down,
    )


def window_layer(phase, turned, ego_edges, pieces, before, weights):
    vehicles, cols, rows, channels = turned.shape
    width = 2 * channels
    tile_cols = cols // TILE
    run = TILE // PHASES
    group = 4
    whole = lambda x: pl.BlockSpec(x.shape, lambda r: (0,) * x.ndim)
    block = lambda *shape: pl.BlockSpec((group, *shape), lambda r: (r,) + (0,) * len(shape))
    pieces = [x.reshape(vehicles, -1, channels) for three in pieces for x in three]
    cells = vehicles * rows * tile_cols * run
    most = cols * rows
    operands = (turned, *ego_edges, *pieces, *weights)
    in_specs = (
        [block(cols, rows, channels)]
        + [block(1, cols, channels)] * 2
        + [block(*x.shape[1:]) for x in pieces]
        + [whole(w) for w in weights]
    )
    aliases = {}
    if before is not None:
        aliases = {len(operands): 0}
        operands += (before,)
        in_specs += [pl.BlockSpec(memory_space=pl.ANY)]
    return pl.pallas_call(
        functools.partial(window_kernel, phase, rows),
        out_shape=jax.ShapeDtypeStruct((vehicles, rows, tile_cols, PHASES, run, width), jnp.bfloat16),
        grid=(vehicles // group,),
        in_specs=in_specs,
        out_specs=pl.BlockSpec(
            (group, rows, tile_cols, None, run, width), lambda r: (r, 0, 0, phase, 0, 0)
        ),
        scratch_shapes=[
            pltpu.VMEM((group * rows * tile_cols * run, width), jnp.float32),
            pltpu.VMEM((2, group * rows * tile_cols * run, channels), jnp.float32),
            pltpu.VMEM((2 * PHASES + 2, most, channels), jnp.float32),
        ],
        input_output_aliases=aliases,
        compiler_params=pltpu.CompilerParams(vmem_limit_bytes=WINDOW_VMEM_BYTES),
        cost_estimate=COST,
    )(*operands)


def beside(last, first):
    count = lax.axis_size("row")
    above = lax.ppermute(last, "row", [(i, i + 1) for i in range(count - 1)])
    below = lax.ppermute(first, "row", [(i + 1, i) for i in range(count - 1)])
    return above, below


def on_device(
    bev_maps,
    senders,
    shifts,
    counts,
    agent_query,
    agent_keyvalue,
    agent_out,
    agent_scale,
    conv_weight,
    gain_first,
    window_in,
    window_out,
    window_scale,
    gain_second,
    hidden_up,
    hidden_down,
):
    vehicles_here, rows, cols, channels = bev_maps.shape
    devices = lax.axis_size("veh")
    tile_cols = cols // TILE
    group = half_size()
    capacity = tile_cols * max(1, vehicles_here * senders.shape[1] // devices)
    turned, first, second = turn_maps(bev_maps)

    def swap(x):
        return lax.ppermute(x, "veh", [(i, (i + group) % devices) for i in range(devices)])

    def send(messages):
        return [
            lax.ppermute(
                x, "veh", [(i, i // group * group + (i + k + 1) % group) for i in range(devices)]
            )
            for k, x in enumerate(messages)
        ]

    far = swap(first)
    chosen, filled, *plan = plan_of(senders, shifts, counts, tile_cols, capacity)
    entries, listed, sizes_of, live, blank = plan
    plan = (entries, listed, sizes_of, blank)
    live = live.reshape(senders.shape[1], -1)
    near_tiles = send(messages_for(chosen, filled, capacity, {0: first}))
    ego_edges = beside(bev_maps[:, rows - 1 :], bev_maps[:, :1])
    join_all = join_weights(agent_query, agent_keyvalue, agent_out, agent_scale)
    present = [present_cells(live, p, rows) for p in range(PHASES)]
    window_all = window_weights(
        conv_weight, gain_first, window_in, window_out, window_scale, gain_second, hidden_up, hidden_down
    )
    far, near_tiles, second, join_all, present, window_all, ego_edges = lax.optimization_barrier(
        (far, near_tiles, second, join_all, present, window_all, ego_edges)
    )
    far_tiles = send(messages_for(chosen, filled, capacity, {1: far}))
    later = swap(second)
    later_messages = messages_for(chosen, filled, capacity, {0: second, 1: later})
    plan, later_messages = lax.optimization_barrier((plan, later_messages))
    later_tiles = send(later_messages)
    arrived = [[first, far, *near_tiles, *far_tiles], [second, later, *later_tiles]]
    origins = [
        [(0, 0), (1, 0)] + [(2 + k + part * (group - 1), 0) for k in range(group - 1) for part in (0, 1)],
        [(0, 0), (1, 0)] + [(2 + k, part * capacity) for k in range(group - 1) for part in (0, 1)],
    ]
    result, pieces = None, []
    for phase, own in enumerate((first, second)):
        if phase:
            plan, result = lax.optimization_barrier((plan, result))
        joined, top, low = join_agents(
            own, arrived[phase], origins[phase], tile_cols, plan, present[phase], join_all
        )
        pieces.append((joined, *beside(low, top)))
        result = window_layer(phase, turned, ego_edges, pieces, result, window_all)
    return result.reshape(vehicles_here, rows, cols, 2 * channels)


def solution(mesh):
    split_maps = P("veh", "row", None, None)
    return jax.shard_map(
        on_device,
        mesh=mesh,
        in_specs=(split_maps,) + (P(),) * 15,
        out_specs=split_maps,
        check_vma=False,
    )
```

```python
import functools
import math

import jax
import jax.numpy as jnp
from jax import lax
from jax.experimental import pallas as pl
from jax.experimental.pallas import tpu as pltpu
from jax.sharding import PartitionSpec as P

TILE = 32
WIN = 8
HEAD = 32
ENTRY_BITS = 10

norm_eps = 1e-05
unit_eps = 1e-06
LOG2E = math.log2(math.e)
VMEM_BYTES = 24 * 2**20
WINDOW_VMEM_BYTES = 40 * 2**20
PHASES = 2

NN = (((1,), (0,)), ((), ()))
NT = (((1,), (1,)), ((), ()))
TN = (((0,), (0,)), ((), ()))


def dot(a, b, dims=NN):
    return lax.dot_general(a, b, dims, preferred_element_type=jnp.float32)


def split(x):
    high = x.astype(jnp.bfloat16)
    return high, (x - high.astype(jnp.float32)).astype(jnp.bfloat16)


def head_sums(x):
    return jnp.sum(x.reshape(x.shape[0] // HEAD, HEAD, x.shape[1]), axis=1, keepdims=True)


def by_head(x, factor):
    return (x.reshape(x.shape[0] // HEAD, HEAD, x.shape[1]) * factor).reshape(x.shape)


def phase_columns(phase):
    run = TILE // PHASES
    return [TILE - 1] + list(range(run + 1)) if phase == 0 else list(range(run + 1, TILE - 1))


def half_size():
    return max(1, lax.axis_size("veh") // 2)


def turn_kernel(maps, turned, first, second, scratch):
    rows, cols, channels = maps.shape[1:]
    run = TILE // PHASES
    for i in range(rows):
        scratch[pl.ds(i, cols, stride=rows), :] = maps[0, i].astype(jnp.float32)
    x = scratch[...].astype(jnp.bfloat16).reshape(cols, rows, channels)
    turned[0] = x
    for t in range(cols // TILE):
        tile = x[t * TILE : (t + 1) * TILE]
        first[t] = jnp.concatenate([tile[TILE - 1 :], tile[: run + 1]], axis=0)
        second[t] = tile[run + 1 : TILE - 1]


def turn_maps(maps):
    vehicles, rows, cols, channels = maps.shape
    tile_cols = cols // TILE
    pieces = [(tile_cols, len(phase_columns(p)), rows, channels) for p in range(PHASES)]
    blocks = [(1, cols, rows, channels), *pieces]
    block = lambda shape: pl.BlockSpec(shape, lambda v: (v, 0, 0, 0))
    return pl.pallas_call(
        turn_kernel,
        out_shape=[jax.ShapeDtypeStruct((vehicles * n[0], *n[1:]), maps.dtype) for n in blocks],
        grid=(vehicles,),
        in_specs=[block((1, rows, cols, channels))],
        out_specs=[block(n) for n in blocks],
        scratch_shapes=[pltpu.VMEM((rows * cols, channels), jnp.float32)],
        compiler_params=pltpu.CompilerParams(vmem_limit_bytes=VMEM_BYTES),
        cost_estimate=pl.CostEstimate(flops=0, bytes_accessed=10 * maps.size, transcendentals=0),
    )(maps)


def plan_kernel(sizes, senders, shifts, counts, ids, chosen, filled, entries, listed, sizes_of, live, blank, sent):
    vehicles, agents, tile_cols, group, capacity = sizes
    me, partner = ids[0], ids[1]
    tiles_held = vehicles * tile_cols
    rank = me % group
    pairs = vehicles * agents

    def clear(i, _):
        sent[i] = 0
        return 0

    def clear_list(i, _):
        listed[i] = 0
        return 0

    spare = chosen.shape[0] - 1
    lax.fori_loop(0, sent.shape[0], clear, 0)
    lax.fori_loop(0, listed.shape[0], clear_list, 0)
    last = blank.shape[0] - 1
    nowhere = listed.shape[0] - 1

    def target(k, _):
        first = (me - rank + (rank + k + 1) % group) * vehicles

        def pair(i, n):
            r, a = first + i // agents, i % agents
            sender, shift = senders[r, a], shifts[r, a]
            tiles = tile_cols - jnp.abs(shift)
            source = sender // vehicles
            far = jnp.where(source == partner, 1, 0)
            filled_here = jnp.where(far == 1, n[1], n[0])
            fits = (a < counts[r]) & ((source == me) | (far == 1)) & (filled_here + tiles <= capacity)

            at = (2 * k + far) * capacity + filled_here
            tile = sender % vehicles * tile_cols + jnp.maximum(shift, 0)
            for t in range(tile_cols):
                chosen[jnp.where(fits & (t < tiles), at + t, spare)] = tile + t
            more = jnp.where(fits, tiles, 0)
            return n[0] + more * (1 - far), n[1] + more * far

        near, far = lax.fori_loop(0, pairs, pair, (0, 0))
        filled[2 * k] = near
        filled[2 * k + 1] = far
        return 0

    lax.fori_loop(0, group - 1, target, 0)

    def pair(i, bare):
        v, a = i // agents, i % agents
        r = me * vehicles + v
        sender, shift = senders[r, a], shifts[r, a]
        alive = a < counts[r]
        source = sender // vehicles
        n = sent[source]
        k = (rank - source % group + group) % group
        apart = jnp.where(source // group == me // group, 0, 1)
        slot = jnp.where(k == 0, sender % vehicles * tile_cols + jnp.maximum(shift, 0), n)
        origin = jnp.where(k == 0, 0, 2 * k) + apart
        tiles = jnp.where(alive, tile_cols - jnp.abs(shift), 0)
        base = a * tiles_held + v * tile_cols
        first = jnp.maximum(-shift, 0)

        here = jnp.where(tiles > 0, origin * tile_cols + tiles - 1, nowhere)
        entries[here * pairs + listed[here]] = ((base + first) << ENTRY_BITS) + slot
        listed[here] = listed[here] + 1
        sizes_of[a * vehicles + v] = tiles
        for t in range(tile_cols):
            inside = (t >= first) & (t < first + tiles)
            live[base + t] = jnp.where(inside, 1, 0)

            blank[jnp.where(inside, last, bare)] = base + t
            bare = bare + jnp.where(inside, 0, 1)

        sent[source] = n + tiles
        return bare

    blank[last] = lax.fori_loop(0, pairs, pair, 0)


def plan_of(senders, shifts, counts, tile_cols, capacity):
    devices = lax.axis_size("veh")
    group = half_size()
    vehicles, agents = senders.shape[0] // devices, senders.shape[1]
    me = lax.axis_index("veh").astype(jnp.int32)
    ids = jnp.stack([me, (me + group) % devices])
    pairs = agents * vehicles
    places = 2 * group * tile_cols
    sizes = [(group - 1) * 2 * capacity + 1, (group - 1) * 2, (places + 1) * pairs, places + 1, pairs]
    sizes += [pairs * tile_cols, pairs * tile_cols + 1]
    smem = pl.BlockSpec(memory_space=pltpu.SMEM)
    return pl.pallas_call(
        functools.partial(plan_kernel, (vehicles, agents, tile_cols, group, capacity)),
        out_shape=[jax.ShapeDtypeStruct((n,), jnp.int32) for n in sizes],
        in_specs=[smem] * 4,
        out_specs=[smem] * 7,
        scratch_shapes=[pltpu.SMEM((devices,), jnp.int32)],
        compiler_params=pltpu.CompilerParams(vmem_limit_bytes=VMEM_BYTES),
        cost_estimate=pl.CostEstimate(flops=0, bytes_accessed=20 * 2**20, transcendentals=0),
    )(senders, shifts, counts, ids)


def send_kernel(sources, capacity, chosen, filled, *refs):
    bufs, messages, sems = refs[: len(sources)], refs[len(sources) : -1], refs[-1]
    copies = []
    for k, message in enumerate(messages):
        for b, source in enumerate(sources):

            def copy(i, tile, k=k, b=b, message=message):
                slot = b * capacity + i
                return pltpu.make_async_copy(bufs[b].at[tile], message.at[slot], sems.at[k, slot])

            copies.append((2 * k + source, copy))
    for at, copy in copies:
        lax.fori_loop(
            0, filled[at], lambda i, _: (copy(i, chosen[at * capacity + i]).start(), 0)[1], 0
        )
    for at, copy in copies:
        lax.fori_loop(0, filled[at], lambda i, _: (copy(i, 0).wait(), 0)[1], 0)


def messages_for(chosen, filled, capacity, sources):
    first = next(iter(sources.values()))
    count = filled.shape[0] // 2
    shape = (len(sources) * capacity, *first.shape[1:])
    anywhere = pl.BlockSpec(memory_space=pl.ANY)
    return pl.pallas_call(
        functools.partial(send_kernel, tuple(sources), capacity),
        out_shape=[jax.ShapeDtypeStruct(shape, first.dtype)] * count,
        grid_spec=pltpu.PrefetchScalarGridSpec(
            num_scalar_prefetch=2,
            grid=(1,),
            in_specs=[anywhere] * len(sources),
            out_specs=[anywhere] * count,
            scratch_shapes=[pltpu.SemaphoreType.DMA((count, shape[0]))],
        ),
        compiler_params=pltpu.CompilerParams(vmem_limit_bytes=VMEM_BYTES),
        cost_estimate=pl.CostEstimate(
            flops=0, bytes_accessed=4 * count * math.prod(shape), transcendentals=0
        ),
    )(chosen, filled, *sources.values())


LANES = 256


def join_kernel(origins, tile_cols, entries, listed, sizes_of, blank, ego, *refs):
    buffers = 1 + max(b for b, _ in origins)
    bufs, refs = refs[:buffers], refs[buffers:]
    present, wq, wkv, wout, scale, out, top_row, low_row, landed, joined, sems = refs
    count, cells, channels = landed.shape
    agents = present.shape[0]
    pieces = count // agents
    vehicles = pieces // tile_cols
    total = pieces * cells
    pairs = agents * vehicles

    def copy(source, at, size, pair):
        return pltpu.make_async_copy(source, landed.at[pl.ds(at, size)], sems.at[pair])

    for origin, (b, offset) in enumerate(origins):
        for size in range(tile_cols, 0, -1):
            place = origin * tile_cols + size - 1

            def fetch(i, _, b=b, offset=offset, size=size, place=place):
                entry = entries[place * pairs + i]
                at, tile = entry >> ENTRY_BITS, entry & ((1 << ENTRY_BITS) - 1)
                copy(bufs[b].at[pl.ds(tile + offset, size)], at, size, at // tile_cols).start()
                return 0

            lax.fori_loop(0, listed[place], fetch, 0)

    def clear(i, _):
        landed[blank[i]] = jnp.zeros((cells, channels), landed.dtype)
        return 0

    lax.fori_loop(0, blank[blank.shape[0] - 1], clear, 0)
    arrived = 0
    heads = channels // HEAD
    scale_col = scale[...].reshape(heads, 1, 1)
    landed_cells = landed.reshape(agents, total, channels)
    for c in range(total // LANES):
        while arrived * tile_cols * cells < (c + 1) * LANES:
            for a in range(agents):
                for size in range(1, tile_cols + 1):
                    pair = a * vehicles + arrived

                    @pl.when(sizes_of[pair] == size)
                    def _(size=size, pair=pair):
                        copy(bufs[0].at[pl.ds(0, size)], pair * tile_cols, size, pair).wait()

            arrived += 1
        span = pl.ds(c * LANES, LANES)
        cells_here = ego[span, :]
        queries = dot(wq[...], cells_here, NT)
        factor = lax.rsqrt(head_sums(queries * queries) + unit_eps) * scale_col

        def agent(x):
            kv = dot(wkv[...], x, NT).astype(jnp.bfloat16).astype(jnp.float32)
            keys, values = kv[:channels], kv[channels:]
            score = head_sums(queries * keys) * factor
            return score * lax.rsqrt(head_sums(keys * keys) + unit_eps), values

        scores, values = zip(
            agent(cells_here),
            *(
                agent(landed_cells[a, span, :])
                for a in range(agents)
            ),
        )
        scores = [scores[0]] + [
            jnp.where(present[a : a + 1, c * LANES : (c + 1) * LANES].reshape(1, 1, LANES) > 0, s, -1e30)
            for a, s in enumerate(scores[1:])
        ]
        top = functools.reduce(jnp.maximum, scores)
        weights = [jnp.exp(s - top) for s in scores]
        inverse = 1.0 / functools.reduce(jnp.add, weights)
        mix = functools.reduce(jnp.add, [by_head(v, w * inverse) for w, v in zip(weights, values)])
        joined[span, :] = dot(mix.astype(jnp.bfloat16), wout[...], TN)
    out[...] = joined[...].astype(jnp.bfloat16)
    edge = top_row.shape[1]
    rows = total // (vehicles * edge)
    for v in range(vehicles):
        start = v * edge * rows
        top_row[v] = joined[pl.ds(start, edge, stride=rows), :].astype(jnp.bfloat16)
        low_row[v] = joined[pl.ds(start + rows - 1, edge, stride=rows), :].astype(jnp.bfloat16)


def join_weights(wq, wkv, wout, scale):
    return wq.T, wkv.T, wout, scale.reshape(-1, 1)


def present_cells(live, phase, rows):
    return jnp.repeat(live.astype(jnp.float32), len(phase_columns(phase)) * rows, axis=1)


def join_agents(pieces, arrived, origins, tile_cols, plan, present, weights):
    count, cols, rows, channels = pieces.shape
    agents = present.shape[0]
    cells = cols * rows
    total = count * cells
    whole = lambda shape: pl.BlockSpec(shape, lambda r, *_: (0,) * len(shape))
    shapes = [(total, channels)] + [(count // tile_cols, tile_cols * cols, channels)] * 2
    return pl.pallas_call(
        functools.partial(join_kernel, origins, tile_cols),
        out_shape=[jax.ShapeDtypeStruct(shape, jnp.bfloat16) for shape in shapes],
        grid_spec=pltpu.PrefetchScalarGridSpec(
            num_scalar_prefetch=4,
            grid=(1,),
            in_specs=[
                whole((total, channels)),
                *[pl.BlockSpec(memory_space=pl.ANY)] * len(arrived),
                whole(present.shape),
            ]
            + [whole(w.shape) for w in weights],
            out_specs=[whole(shape) for shape in shapes],
            scratch_shapes=[
                pltpu.VMEM((agents * count, cells, channels), jnp.bfloat16),
                pltpu.VMEM((total, channels), jnp.float32),
                pltpu.SemaphoreType.DMA((agents * count // tile_cols,)),
            ],
        ),
        compiler_params=pltpu.CompilerParams(vmem_limit_bytes=VMEM_BYTES),
        cost_estimate=pl.CostEstimate(
            flops=total * channels * channels * 40, bytes_accessed=total * channels * 12, transcendentals=total * 20
        ),
    )(
        *plan,
        pieces.reshape(total, channels),
        *(x.reshape(-1, cells, channels) for x in arrived),
        present,
        *weights,
    )


def norm(x, gain):
    average = jnp.mean(x, axis=-1, keepdims=True)
    centred = x - average
    spread = jnp.mean(centred * centred, axis=-1, keepdims=True)
    return (centred * lax.rsqrt(spread + norm_eps) * gain).astype(jnp.bfloat16)


def spread_rows(ref, rows_of, at, rows):
    count, channels = rows_of.shape
    ref[pl.ds(at, count, stride=rows), :] = rows_of.astype(jnp.float32)
    return ref[: count * rows].reshape(count, rows, channels)


def runs_of(phase, tile_cols, whole_map, pieces):
    run = TILE // PHASES
    out = []
    for t in range(tile_cols):
        first = t * TILE + phase * run - 1
        if pieces is None:
            last = first + run + 2
            blank = jnp.zeros_like(whole_map[:1])
            body = whole_map[max(first, 0) : min(last, tile_cols * TILE)]
            parts = ([blank] if first < 0 else []) + [body] + ([blank] if last > tile_cols * TILE else [])
        else:
            size = run + 2
            one = pieces[0]
            blank = jnp.zeros_like(one[:1])
            if phase == 0:
                left = one[(t - 1) * size : (t - 1) * size + 1] if t else blank
                parts = [left, one[t * size + 1 : (t + 1) * size]]
            else:
                rest = TILE - size
                right = one[(t + 1) * size + 1 : (t + 1) * size + 2] if t + 1 < tile_cols else blank
                parts = [
                    one[t * size + run : (t + 1) * size],
                    pieces[1][t * rest : (t + 1) * rest],
                    one[t * size : t * size + 1],
                    right,
                ]
        out.append(jnp.concatenate(parts, axis=0))
    return out


def taps_of(runs, above, below, taps):
    out = []
    for x, first, last in zip(runs, above, below):
        cols, rows, channels = x.shape
        row = lax.broadcasted_iota(jnp.int32, (rows, channels), 0)[None]
        flat = x.reshape(cols * rows, channels)
        over = jnp.where(row == 0, first, pltpu.roll(flat, 1, 0).reshape(x.shape))
        under = jnp.where(row == rows - 1, last, pltpu.roll(flat, cols * rows - 1, 0).reshape(x.shape))
        total = x[1 : cols - 1]
        for j in range(3):
            span = slice(j, cols - 2 + j)
            total = total + over[span] * taps[j] + x[span] * taps[3 + j] + under[span] * taps[6 + j]
        out.append(total.reshape((cols - 2) * rows, channels))
    return out


def window_kernel(phase, rows, *refs):
    ego, ego_up, ego_down, refs = *refs[:3], refs[3:]
    pieces, refs = [refs[3 * p : 3 * p + 3] for p in range(phase + 1)], refs[3 * phase + 3 :]
    taps, gain_one, wq, wk, wv, wo, scale, gain_two, up, down = refs[:10]
    out, mixed_ref, result_ref, halo = refs[10 + phase :]
    group_size, cols, _, channels = ego.shape
    tile_cols = cols // TILE
    run = TILE // PHASES
    width = 2 * channels
    in_window = rows * WIN
    here = tile_cols * run * rows
    cells = group_size * here
    windows = cells // in_window
    heads = width // HEAD
    f32 = jnp.float32
    for v in range(group_size):
        for half in range(2):
            lanes = slice(half * channels, (half + 1) * channels)
            weights = [taps[i : i + 1, lanes].reshape(1, 1, channels) for i in range(9)]
            if half == 0:
                centre = runs_of(phase, tile_cols, ego[v].astype(f32), None)
                above = runs_of(phase, tile_cols, spread_rows(halo.at[0], ego_up[v, 0], 0, rows), None)
                below = runs_of(phase, tile_cols, spread_rows(halo.at[1], ego_down[v, 0], rows - 1, rows), None)
            else:
                centre, above, below = [], [], []
                for p, (x, first, last) in enumerate(pieces):
                    centre.append(x[v].astype(f32).reshape(-1, rows, channels))
                    above.append(spread_rows(halo.at[2 + 2 * p], first[v], 0, rows))
                    below.append(spread_rows(halo.at[3 + 2 * p], last[v], rows - 1, rows))
                centre, above, below = (runs_of(phase, tile_cols, None, x) for x in (centre, above, below))
            for t, part in enumerate(taps_of(centre, above, below, weights)):
                at = v * here + t * run * rows
                mixed_ref[at : at + run * rows, lanes] = part
    hidden = norm(mixed_ref[...], gain_one[...])
    queries = dot(wq[...], hidden, NT)
    values = dot(wv[...], hidden, NT).astype(jnp.bfloat16)
    keys = dot(hidden, wk[...])
    factor = lax.rsqrt(head_sums(queries * queries) + unit_eps) * scale[...].reshape(heads, 1, 1)
    queries = by_head(queries, factor)
    member = (
        lax.broadcasted_iota(jnp.int32, (width, width), 0) // HEAD
        == lax.broadcasted_iota(jnp.int32, (width, width), 1) // HEAD
    ).astype(f32).astype(jnp.bfloat16)
    square_high, square_low = split(keys * keys)
    keys = keys * lax.rsqrt(dot(square_high, member) + dot(square_low, member) + unit_eps)
    key_high, key_low = split(keys)

    pair = 2 * in_window
    group = 4 * HEAD
    lane = lax.broadcasted_iota(jnp.int32, (width, pair), 1) < in_window
    even = (lax.broadcasted_iota(jnp.int32, (width, pair), 0) // HEAD) % 2 == 0
    blank = jnp.zeros((2 * HEAD, pair), jnp.bfloat16)
    blank_p = jnp.zeros((in_window, 4 * in_window), jnp.bfloat16)
    lane_head = lax.broadcasted_iota(jnp.int32, (HEAD, pair), 1) < in_window
    rights = []
    for p in range(windows // 2):
        straight = queries[:, p * pair : (p + 1) * pair]
        turned = pltpu.roll(straight, in_window, 1)
        for w in range(2):
            low, high = (straight, turned) if w == 0 else (turned, straight)
            rights.append(split(jnp.where(even, jnp.where(lane, low, 0.0), jnp.where(lane, 0.0, high))))

    def right(block, g):
        block = block[g * group : (g + 1) * group]
        return jnp.concatenate(
            [
                jnp.concatenate([block[: 2 * HEAD], blank], axis=1),
                jnp.concatenate([blank, block[2 * HEAD :]], axis=1),
            ],
            axis=0,
        )

    groups = width // group
    scores = []
    for w in range(windows):
        for g in range(groups):
            span = slice(w * in_window, (w + 1) * in_window), slice(g * group, (g + 1) * group)
            both = dot(jnp.concatenate([key_high[span], key_low[span]], axis=0), right(rights[w][0], g))
            scores.append(both[:in_window] + both[in_window:] + dot(key_high[span], right(rights[w][1], g)))
    probs = []
    for score in scores:
        weight = jnp.exp2(score - jnp.max(score, axis=0, keepdims=True))
        probs.append((weight * (1.0 / jnp.sum(weight, axis=0, keepdims=True))).astype(jnp.bfloat16))
    attended = []
    for p in range(windows // 2):
        parts = []
        for g in range(groups):
            v = values[g * group : (g + 1) * group, p * pair : (p + 1) * pair]
            first = dot(v, jnp.concatenate([probs[2 * p * groups + g], blank_p], axis=0))
            second = dot(v, jnp.concatenate([blank_p, probs[(2 * p + 1) * groups + g]], axis=0))
            for h in range(4):
                rows_of = slice(h * HEAD, (h + 1) * HEAD)
                cols_of = slice((h // 2) * pair, (h // 2 + 1) * pair)
                a, b = first[rows_of, cols_of], second[rows_of, cols_of]
                if h % 2 == 0:
                    b = pltpu.roll(b, in_window, 1)
                else:
                    a = pltpu.roll(a, in_window, 1)
                parts.append(jnp.where(lane_head, a, b))
        attended.append(jnp.concatenate(parts, axis=0).astype(jnp.bfloat16))
    attended = jnp.concatenate(attended, axis=1)
    mixed = mixed_ref[...] + dot(attended, wo[...], TN)
    hidden = norm(mixed, gain_two[...])
    inner = dot(hidden, up[...])
    inner = (0.5 * inner * (1.0 + jnp.tanh(0.5 * inner))).astype(jnp.bfloat16)
    result = mixed + dot(inner, down[...])
    for half in range(2):
        result_ref[half] = result[:, half * channels : (half + 1) * channels]
    for v in range(group_size):
        for t in range(tile_cols):
            for i in range(rows):
                at = v * here + t * run * rows + i
                for half in range(2):
                    lanes = slice(half * channels, (half + 1) * channels)
                    line = result_ref[half, pl.ds(at, run, stride=rows), :]
                    out[v, i, t, :, lanes] = line.astype(jnp.bfloat16)


def window_weights(conv_weight, gain_first, window_in, window_out, window_scale, gain_second, hidden_up, hidden_down):
    width = conv_weight.shape[-1]
    return (
        conv_weight.reshape(9, width),
        gain_first[None],
        window_in[:, :width].T,
        window_in[:, width : 2 * width],
        window_in[:, 2 * width :].T,
        window_out,
        (window_scale * LOG2E).reshape(-1, 1),
        gain_second[None],
        hidden_up,
        hidden_down,
    )


def window_layer(phase, turned, ego_edges, pieces, before, weights):
    vehicles, cols, rows, channels = turned.shape
    width = 2 * channels
    tile_cols = cols // TILE
    run = TILE // PHASES
    group = 4
    whole = lambda x: pl.BlockSpec(x.shape, lambda r: (0,) * x.ndim)
    block = lambda *shape: pl.BlockSpec((group, *shape), lambda r: (r,) + (0,) * len(shape))
    pieces = [x.reshape(vehicles, -1, channels) for three in pieces for x in three]
    cells = vehicles * rows * tile_cols * run
    most = cols * rows
    operands = (turned, *ego_edges, *pieces, *weights)
    in_specs = (
        [block(cols, rows, channels)]
        + [block(1, cols, channels)] * 2
        + [block(*x.shape[1:]) for x in pieces]
        + [whole(w) for w in weights]
    )
    aliases = {}
    if before is not None:
        aliases = {len(operands): 0}
        operands += (before,)
        in_specs += [pl.BlockSpec(memory_space=pl.ANY)]
    return pl.pallas_call(
        functools.partial(window_kernel, phase, rows),
        out_shape=jax.ShapeDtypeStruct((vehicles, rows, tile_cols, PHASES, run, width), jnp.bfloat16),
        grid=(vehicles // group,),
        in_specs=in_specs,
        out_specs=pl.BlockSpec(
            (group, rows, tile_cols, None, run, width), lambda r: (r, 0, 0, phase, 0, 0)
        ),
        scratch_shapes=[
            pltpu.VMEM((group * rows * tile_cols * run, width), jnp.float32),
            pltpu.VMEM((2, group * rows * tile_cols * run, channels), jnp.float32),
            pltpu.VMEM((2 * PHASES + 2, most, channels), jnp.float32),
        ],
        input_output_aliases=aliases,
        compiler_params=pltpu.CompilerParams(vmem_limit_bytes=WINDOW_VMEM_BYTES),
        cost_estimate=pl.CostEstimate(
            flops=cells * width * width * 60, bytes_accessed=cells * width * 6, transcendentals=cells * width * 4
        ),
    )(*operands)


def beside(last, first):
    count = lax.axis_size("row")
    above = lax.ppermute(last, "row", [(i, i + 1) for i in range(count - 1)])
    below = lax.ppermute(first, "row", [(i + 1, i) for i in range(count - 1)])
    return above, below


def on_device(
    bev_maps,
    senders,
    shifts,
    counts,
    agent_query,
    agent_keyvalue,
    agent_out,
    agent_scale,
    conv_weight,
    gain_first,
    window_in,
    window_out,
    window_scale,
    gain_second,
    hidden_up,
    hidden_down,
):
    vehicles_here, rows, cols, channels = bev_maps.shape
    devices = lax.axis_size("veh")
    tile_cols = cols // TILE
    group = half_size()
    capacity = tile_cols * max(1, vehicles_here * senders.shape[1] // devices)
    turned, first, second = turn_maps(bev_maps)

    def swap(x):
        return lax.ppermute(x, "veh", [(i, (i + group) % devices) for i in range(devices)])

    def send(messages):
        return [
            lax.ppermute(
                x, "veh", [(i, i // group * group + (i + k + 1) % group) for i in range(devices)]
            )
            for k, x in enumerate(messages)
        ]

    far = swap(first)
    chosen, filled, *plan = plan_of(senders, shifts, counts, tile_cols, capacity)
    entries, listed, sizes_of, live, blank = plan
    plan = (entries, listed, sizes_of, blank)
    live = live.reshape(senders.shape[1], -1)
    near_messages = messages_for(chosen, filled, capacity, {0: first})
    near_tiles = send(near_messages)
    ego_edges = beside(bev_maps[:, rows - 1 :], bev_maps[:, :1])
    join_all = join_weights(agent_query, agent_keyvalue, agent_out, agent_scale)
    present = [present_cells(live, p, rows) for p in range(PHASES)]
    window_all = window_weights(
        conv_weight, gain_first, window_in, window_out, window_scale, gain_second, hidden_up, hidden_down
    )
    far, second, join_all, present, window_all, _ = lax.optimization_barrier(
        (far, second, join_all, present, window_all, near_messages)
    )
    far_tiles = send(messages_for(chosen, filled, capacity, {1: far}))
    later = swap(second)
    later_messages = messages_for(chosen, filled, capacity, {0: second, 1: later})
    later_tiles = send(later_messages)
    arrived = [[first, far, *near_tiles, *far_tiles], [second, later, *later_tiles]]
    origins = [
        [(0, 0), (1, 0)] + [(2 + k + part * (group - 1), 0) for k in range(group - 1) for part in (0, 1)],
        [(0, 0), (1, 0)] + [(2 + k, part * capacity) for k in range(group - 1) for part in (0, 1)],
    ]
    result, pieces = None, []
    for phase, own in enumerate((first, second)):
        if phase:
            plan, result = lax.optimization_barrier((plan, result))
        joined, top, low = join_agents(
            own, arrived[phase], origins[phase], tile_cols, plan, present[phase], join_all
        )
        pieces.append((joined, *beside(low, top)))
        result = window_layer(phase, turned, ego_edges, pieces, result, window_all)
    return result.reshape(vehicles_here, rows, cols, 2 * channels)


def solution(mesh):
    split_maps = P("veh", "row", None, None)
    return jax.shard_map(
        on_device,
        mesh=mesh,
        in_specs=(split_maps,) + (P(),) * 15,
        out_specs=split_maps,
        check_vma=False,
    )
```

```python
import functools
import math

import jax
import jax.numpy as jnp
from jax import lax
from jax.experimental import pallas as pl
from jax.experimental.pallas import tpu as pltpu
from jax.sharding import PartitionSpec as P

TILE = 32
WIN = 8
HEAD = 32
ENTRY_BITS = 10

norm_eps = 1e-05
unit_eps = 1e-06
LOG2E = math.log2(math.e)
VMEM_BYTES = 24 * 2**20
WINDOW_VMEM_BYTES = 40 * 2**20
PHASES = 2

NN = (((1,), (0,)), ((), ()))
NT = (((1,), (1,)), ((), ()))
TN = (((0,), (0,)), ((), ()))


def dot(a, b, dims=NN):
    return lax.dot_general(a, b, dims, preferred_element_type=jnp.float32)


def split(x):
    high = x.astype(jnp.bfloat16)
    return high, (x - high.astype(jnp.float32)).astype(jnp.bfloat16)


def head_sums(x):
    return jnp.sum(x.reshape(x.shape[0] // HEAD, HEAD, x.shape[1]), axis=1, keepdims=True)


def by_head(x, factor):
    return (x.reshape(x.shape[0] // HEAD, HEAD, x.shape[1]) * factor).reshape(x.shape)


def phase_columns(phase):
    run = TILE // PHASES
    return [TILE - 1] + list(range(run + 1)) if phase == 0 else list(range(run + 1, TILE - 1))


def half_size():
    return max(1, lax.axis_size("veh") // 2)


def turn_kernel(maps, turned, first, second, scratch):
    rows, cols, channels = maps.shape[1:]
    run = TILE // PHASES
    for i in range(rows):
        scratch[pl.ds(i, cols, stride=rows), :] = maps[0, i].astype(jnp.float32)
    x = scratch[...].astype(jnp.bfloat16).reshape(cols, rows, channels)
    turned[0] = x
    for t in range(cols // TILE):
        tile = x[t * TILE : (t + 1) * TILE]
        first[t] = jnp.concatenate([tile[TILE - 1 :], tile[: run + 1]], axis=0)
        second[t] = tile[run + 1 : TILE - 1]


def turn_maps(maps):
    vehicles, rows, cols, channels = maps.shape
    tile_cols = cols // TILE
    pieces = [(tile_cols, len(phase_columns(p)), rows, channels) for p in range(PHASES)]
    blocks = [(1, cols, rows, channels), *pieces]
    block = lambda shape: pl.BlockSpec(shape, lambda v: (v, 0, 0, 0))
    return pl.pallas_call(
        turn_kernel,
        out_shape=[jax.ShapeDtypeStruct((vehicles * n[0], *n[1:]), maps.dtype) for n in blocks],
        grid=(vehicles,),
        in_specs=[block((1, rows, cols, channels))],
        out_specs=[block(n) for n in blocks],
        scratch_shapes=[pltpu.VMEM((rows * cols, channels), jnp.float32)],
        compiler_params=pltpu.CompilerParams(vmem_limit_bytes=VMEM_BYTES),
        cost_estimate=pl.CostEstimate(flops=0, bytes_accessed=10 * maps.size, transcendentals=0),
    )(maps)


def plan_kernel(sizes, senders, shifts, counts, ids, chosen, filled, entries, listed, sizes_of, live, blank, sent):
    vehicles, agents, tile_cols, group, capacity = sizes
    me, partner = ids[0], ids[1]
    tiles_held = vehicles * tile_cols
    rank = me % group
    pairs = vehicles * agents

    def clear(i, _):
        sent[i] = 0
        return 0

    def clear_list(i, _):
        listed[i] = 0
        return 0

    spare = chosen.shape[0] - 1
    lax.fori_loop(0, sent.shape[0], clear, 0)
    lax.fori_loop(0, listed.shape[0], clear_list, 0)
    last = blank.shape[0] - 1
    nowhere = listed.shape[0] - 1

    def target(k, _):
        first = (me - rank + (rank + k + 1) % group) * vehicles

        def pair(i, n):
            r, a = first + i // agents, i % agents
            sender, shift = senders[r, a], shifts[r, a]
            tiles = tile_cols - jnp.abs(shift)
            source = sender // vehicles
            far = jnp.where(source == partner, 1, 0)
            filled_here = jnp.where(far == 1, n[1], n[0])
            fits = (a < counts[r]) & ((source == me) | (far == 1)) & (filled_here + tiles <= capacity)

            at = (2 * k + far) * capacity + filled_here
            tile = sender % vehicles * tile_cols + jnp.maximum(shift, 0)
            for t in range(tile_cols):
                chosen[jnp.where(fits & (t < tiles), at + t, spare)] = tile + t
            more = jnp.where(fits, tiles, 0)
            return n[0] + more * (1 - far), n[1] + more * far

        near, far = lax.fori_loop(0, pairs, pair, (0, 0))
        filled[2 * k] = near
        filled[2 * k + 1] = far
        return 0

    lax.fori_loop(0, group - 1, target, 0)

    def pair(i, bare):
        v, a = i // agents, i % agents
        r = me * vehicles + v
        sender, shift = senders[r, a], shifts[r, a]
        alive = a < counts[r]
        source = sender // vehicles
        n = sent[source]
        k = (rank - source % group + group) % group
        apart = jnp.where(source // group == me // group, 0, 1)
        slot = jnp.where(k == 0, sender % vehicles * tile_cols + jnp.maximum(shift, 0), n)
        origin = jnp.where(k == 0, 0, 2 * k) + apart
        tiles = jnp.where(alive, tile_cols - jnp.abs(shift), 0)
        base = a * tiles_held + v * tile_cols
        first = jnp.maximum(-shift, 0)

        here = jnp.where(tiles > 0, origin * tile_cols + tiles - 1, nowhere)
        entries[here * pairs + listed[here]] = ((base + first) << ENTRY_BITS) + slot
        listed[here] = listed[here] + 1
        sizes_of[a * vehicles + v] = tiles
        for t in range(tile_cols):
            inside = (t >= first) & (t < first + tiles)
            live[base + t] = jnp.where(inside, 1, 0)

            blank[jnp.where(inside, last, bare)] = base + t
            bare = bare + jnp.where(inside, 0, 1)

        sent[source] = n + tiles
        return bare

    blank[last] = lax.fori_loop(0, pairs, pair, 0)


def plan_of(senders, shifts, counts, tile_cols, capacity):
    devices = lax.axis_size("veh")
    group = half_size()
    vehicles, agents = senders.shape[0] // devices, senders.shape[1]
    me = lax.axis_index("veh").astype(jnp.int32)
    ids = jnp.stack([me, (me + group) % devices])
    pairs = agents * vehicles
    places = 2 * group * tile_cols
    sizes = [(group - 1) * 2 * capacity + 1, (group - 1) * 2, (places + 1) * pairs, places + 1, pairs]
    sizes += [pairs * tile_cols, pairs * tile_cols + 1]
    smem = pl.BlockSpec(memory_space=pltpu.SMEM)
    return pl.pallas_call(
        functools.partial(plan_kernel, (vehicles, agents, tile_cols, group, capacity)),
        out_shape=[jax.ShapeDtypeStruct((n,), jnp.int32) for n in sizes],
        in_specs=[smem] * 4,
        out_specs=[smem] * 7,
        scratch_shapes=[pltpu.SMEM((devices,), jnp.int32)],
        compiler_params=pltpu.CompilerParams(vmem_limit_bytes=VMEM_BYTES),
        cost_estimate=pl.CostEstimate(flops=0, bytes_accessed=20 * 2**20, transcendentals=0),
    )(senders, shifts, counts, ids)


def send_kernel(sources, capacity, chosen, filled, *refs):
    bufs, messages, sems = refs[: len(sources)], refs[len(sources) : -1], refs[-1]
    copies = []
    for k, message in enumerate(messages):
        for b, source in enumerate(sources):

            def copy(i, tile, k=k, b=b, message=message):
                slot = b * capacity + i
                return pltpu.make_async_copy(bufs[b].at[tile], message.at[slot], sems.at[k, slot])

            copies.append((2 * k + source, copy))
    for at, copy in copies:
        lax.fori_loop(
            0, filled[at], lambda i, _: (copy(i, chosen[at * capacity + i]).start(), 0)[1], 0
        )
    for at, copy in copies:
        lax.fori_loop(0, filled[at], lambda i, _: (copy(i, 0).wait(), 0)[1], 0)


def messages_for(chosen, filled, capacity, sources):
    first = next(iter(sources.values()))
    count = filled.shape[0] // 2
    shape = (len(sources) * capacity, *first.shape[1:])
    anywhere = pl.BlockSpec(memory_space=pl.ANY)
    return pl.pallas_call(
        functools.partial(send_kernel, tuple(sources), capacity),
        out_shape=[jax.ShapeDtypeStruct(shape, first.dtype)] * count,
        grid_spec=pltpu.PrefetchScalarGridSpec(
            num_scalar_prefetch=2,
            grid=(1,),
            in_specs=[anywhere] * len(sources),
            out_specs=[anywhere] * count,
            scratch_shapes=[pltpu.SemaphoreType.DMA((count, shape[0]))],
        ),
        compiler_params=pltpu.CompilerParams(vmem_limit_bytes=VMEM_BYTES),
        cost_estimate=pl.CostEstimate(
            flops=0, bytes_accessed=4 * count * math.prod(shape), transcendentals=0
        ),
    )(chosen, filled, *sources.values())


LANES = 256


def join_kernel(origins, tile_cols, entries, listed, sizes_of, blank, ego, *refs):
    buffers = 1 + max(b for b, _ in origins)
    bufs, refs = refs[:buffers], refs[buffers:]
    present, wq, wkv, wout, scale, out, top_row, low_row, landed, joined, sems = refs
    count, cells, channels = landed.shape
    agents = present.shape[0]
    pieces = count // agents
    vehicles = pieces // tile_cols
    total = pieces * cells
    pairs = agents * vehicles

    def copy(source, at, size, pair):
        return pltpu.make_async_copy(source, landed.at[pl.ds(at, size)], sems.at[pair])

    for origin, (b, offset) in enumerate(origins):
        for size in range(tile_cols, 0, -1):
            place = origin * tile_cols + size - 1

            def fetch(i, _, b=b, offset=offset, size=size, place=place):
                entry = entries[place * pairs + i]
                at, tile = entry >> ENTRY_BITS, entry & ((1 << ENTRY_BITS) - 1)
                copy(bufs[b].at[pl.ds(tile + offset, size)], at, size, at // tile_cols).start()
                return 0

            lax.fori_loop(0, listed[place], fetch, 0)

    def clear(i, _):
        landed[blank[i]] = jnp.zeros((cells, channels), landed.dtype)
        return 0

    lax.fori_loop(0, blank[blank.shape[0] - 1], clear, 0)
    arrived = 0
    heads = channels // HEAD
    scale_col = scale[...].reshape(heads, 1, 1)
    landed_cells = landed.reshape(agents, total, channels)
    for c in range(total // LANES):
        while arrived * tile_cols * cells < (c + 1) * LANES:
            for a in range(agents):
                for size in range(1, tile_cols + 1):
                    pair = a * vehicles + arrived

                    @pl.when(sizes_of[pair] == size)
                    def _(size=size, pair=pair):
                        copy(bufs[0].at[pl.ds(0, size)], pair * tile_cols, size, pair).wait()

            arrived += 1
        span = pl.ds(c * LANES, LANES)
        cells_here = ego[span, :]
        queries = dot(wq[...], cells_here, NT)
        factor = lax.rsqrt(head_sums(queries * queries) + unit_eps) * scale_col

        def agent(x):
            kv = dot(wkv[...], x, NT).astype(jnp.bfloat16).astype(jnp.float32)
            keys, values = kv[:channels], kv[channels:]
            score = head_sums(queries * keys) * factor
            return score * lax.rsqrt(head_sums(keys * keys) + unit_eps), values

        scores, values = zip(
            agent(cells_here),
            *(
                agent(landed_cells[a, span, :])
                for a in range(agents)
            ),
        )
        scores = [scores[0]] + [
            jnp.where(present[a : a + 1, c * LANES : (c + 1) * LANES].reshape(1, 1, LANES) > 0, s, -1e30)
            for a, s in enumerate(scores[1:])
        ]
        top = functools.reduce(jnp.maximum, scores)
        weights = [jnp.exp(s - top) for s in scores]
        inverse = 1.0 / functools.reduce(jnp.add, weights)
        mix = functools.reduce(jnp.add, [by_head(v, w * inverse) for w, v in zip(weights, values)])
        joined[span, :] = dot(mix.astype(jnp.bfloat16), wout[...], TN)
    out[...] = joined[...].astype(jnp.bfloat16)
    edge = top_row.shape[1]
    rows = total // (vehicles * edge)
    for v in range(vehicles):
        start = v * edge * rows
        top_row[v] = joined[pl.ds(start, edge, stride=rows), :].astype(jnp.bfloat16)
        low_row[v] = joined[pl.ds(start + rows - 1, edge, stride=rows), :].astype(jnp.bfloat16)


def join_weights(wq, wkv, wout, scale):
    return wq.T, wkv.T, wout, scale.reshape(-1, 1)


def present_cells(live, phase, rows):
    return jnp.repeat(live.astype(jnp.float32), len(phase_columns(phase)) * rows, axis=1)


def join_agents(pieces, arrived, origins, tile_cols, plan, present, weights):
    count, cols, rows, channels = pieces.shape
    agents = present.shape[0]
    cells = cols * rows
    total = count * cells
    whole = lambda shape: pl.BlockSpec(shape, lambda r, *_: (0,) * len(shape))
    shapes = [(total, channels)] + [(count // tile_cols, tile_cols * cols, channels)] * 2
    return pl.pallas_call(
        functools.partial(join_kernel, origins, tile_cols),
        out_shape=[jax.ShapeDtypeStruct(shape, jnp.bfloat16) for shape in shapes],
        grid_spec=pltpu.PrefetchScalarGridSpec(
            num_scalar_prefetch=4,
            grid=(1,),
            in_specs=[
                whole((total, channels)),
                *[pl.BlockSpec(memory_space=pl.ANY)] * len(arrived),
                whole(present.shape),
            ]
            + [whole(w.shape) for w in weights],
            out_specs=[whole(shape) for shape in shapes],
            scratch_shapes=[
                pltpu.VMEM((agents * count, cells, channels), jnp.bfloat16),
                pltpu.VMEM((total, channels), jnp.float32),
                pltpu.SemaphoreType.DMA((agents * count // tile_cols,)),
            ],
        ),
        compiler_params=pltpu.CompilerParams(vmem_limit_bytes=VMEM_BYTES),
        cost_estimate=pl.CostEstimate(
            flops=total * channels * channels * 40, bytes_accessed=total * channels * 12, transcendentals=total * 20
        ),
    )(
        *plan,
        pieces.reshape(total, channels),
        *(x.reshape(-1, cells, channels) for x in arrived),
        present,
        *weights,
    )


def norm(x, gain):
    average = jnp.mean(x, axis=-1, keepdims=True)
    centred = x - average
    spread = jnp.mean(centred * centred, axis=-1, keepdims=True)
    return (centred * lax.rsqrt(spread + norm_eps) * gain).astype(jnp.bfloat16)


def spread_rows(ref, rows_of, at, rows):
    count, channels = rows_of.shape
    ref[pl.ds(at, count, stride=rows), :] = rows_of.astype(jnp.float32)
    return ref[: count * rows].reshape(count, rows, channels)


def runs_of(phase, tile_cols, whole_map, pieces):
    run = TILE // PHASES
    out = []
    for t in range(tile_cols):
        first = t * TILE + phase * run - 1
        if pieces is None:
            last = first + run + 2
            blank = jnp.zeros_like(whole_map[:1])
            body = whole_map[max(first, 0) : min(last, tile_cols * TILE)]
            parts = ([blank] if first < 0 else []) + [body] + ([blank] if last > tile_cols * TILE else [])
        else:
            size = run + 2
            one = pieces[0]
            blank = jnp.zeros_like(one[:1])
            if phase == 0:
                left = one[(t - 1) * size : (t - 1) * size + 1] if t else blank
                parts = [left, one[t * size + 1 : (t + 1) * size]]
            else:
                rest = TILE - size
                right = one[(t + 1) * size + 1 : (t + 1) * size + 2] if t + 1 < tile_cols else blank
                parts = [
                    one[t * size + run : (t + 1) * size],
                    pieces[1][t * rest : (t + 1) * rest],
                    one[t * size : t * size + 1],
                    right,
                ]
        out.append(jnp.concatenate(parts, axis=0))
    return out


def taps_of(runs, above, below, taps):
    out = []
    for x, first, last in zip(runs, above, below):
        cols, rows, channels = x.shape
        row = lax.broadcasted_iota(jnp.int32, (rows, channels), 0)[None]
        flat = x.reshape(cols * rows, channels)
        over = jnp.where(row == 0, first, pltpu.roll(flat, 1, 0).reshape(x.shape))
        under = jnp.where(row == rows - 1, last, pltpu.roll(flat, cols * rows - 1, 0).reshape(x.shape))
        total = x[1 : cols - 1]
        for j in range(3):
            span = slice(j, cols - 2 + j)
            total = total + over[span] * taps[j] + x[span] * taps[3 + j] + under[span] * taps[6 + j]
        out.append(total.reshape((cols - 2) * rows, channels))
    return out


def window_kernel(phase, rows, *refs):
    ego, ego_up, ego_down, refs = *refs[:3], refs[3:]
    pieces, refs = [refs[3 * p : 3 * p + 3] for p in range(phase + 1)], refs[3 * phase + 3 :]
    taps, gain_one, wq, wk, wv, wo, scale, gain_two, up, down = refs[:10]
    out, mixed_ref, result_ref, halo = refs[10 + phase :]
    group_size, cols, _, channels = ego.shape
    tile_cols = cols // TILE
    run = TILE // PHASES
    width = 2 * channels
    in_window = rows * WIN
    here = tile_cols * run * rows
    cells = group_size * here
    windows = cells // in_window
    heads = width // HEAD
    f32 = jnp.float32
    for v in range(group_size):
        for half in range(2):
            lanes = slice(half * channels, (half + 1) * channels)
            weights = [taps[i : i + 1, lanes].reshape(1, 1, channels) for i in range(9)]
            if half == 0:
                centre = runs_of(phase, tile_cols, ego[v].astype(f32), None)
                above = runs_of(phase, tile_cols, spread_rows(halo.at[0], ego_up[v, 0], 0, rows), None)
                below = runs_of(phase, tile_cols, spread_rows(halo.at[1], ego_down[v, 0], rows - 1, rows), None)
            else:
                centre, above, below = [], [], []
                for p, (x, first, last) in enumerate(pieces):
                    centre.append(x[v].astype(f32).reshape(-1, rows, channels))
                    above.append(spread_rows(halo.at[2 + 2 * p], first[v], 0, rows))
                    below.append(spread_rows(halo.at[3 + 2 * p], last[v], rows - 1, rows))
                centre, above, below = (runs_of(phase, tile_cols, None, x) for x in (centre, above, below))
            for t, part in enumerate(taps_of(centre, above, below, weights)):
                at = v * here + t * run * rows
                mixed_ref[at : at + run * rows, lanes] = part
    hidden = norm(mixed_ref[...], gain_one[...])
    queries = dot(wq[...], hidden, NT)
    values = dot(wv[...], hidden, NT).astype(jnp.bfloat16)
    keys = dot(hidden, wk[...])
    factor = lax.rsqrt(head_sums(queries * queries) + unit_eps) * scale[...].reshape(heads, 1, 1)
    queries = by_head(queries, factor)
    member = (
        lax.broadcasted_iota(jnp.int32, (width, width), 0) // HEAD
        == lax.broadcasted_iota(jnp.int32, (width, width), 1) // HEAD
    ).astype(f32).astype(jnp.bfloat16)
    square_high, square_low = split(keys * keys)
    keys = keys * lax.rsqrt(dot(square_high, member) + dot(square_low, member) + unit_eps)
    key_high, key_low = split(keys)

    pair = 2 * in_window
    group = 4 * HEAD
    lane = lax.broadcasted_iota(jnp.int32, (width, pair), 1) < in_window
    even = (lax.broadcasted_iota(jnp.int32, (width, pair), 0) // HEAD) % 2 == 0
    blank = jnp.zeros((2 * HEAD, pair), jnp.bfloat16)
    blank_p = jnp.zeros((in_window, 4 * in_window), jnp.bfloat16)
    lane_head = lax.broadcasted_iota(jnp.int32, (HEAD, pair), 1) < in_window
    rights = []
    for p in range(windows // 2):
        straight = queries[:, p * pair : (p + 1) * pair]
        turned = pltpu.roll(straight, in_window, 1)
        for w in range(2):
            low, high = (straight, turned) if w == 0 else (turned, straight)
            rights.append(split(jnp.where(even, jnp.where(lane, low, 0.0), jnp.where(lane, 0.0, high))))

    def right(block, g):
        block = block[g * group : (g + 1) * group]
        return jnp.concatenate(
            [
                jnp.concatenate([block[: 2 * HEAD], blank], axis=1),
                jnp.concatenate([blank, block[2 * HEAD :]], axis=1),
            ],
            axis=0,
        )

    groups = width // group
    scores = []
    for w in range(windows):
        for g in range(groups):
            span = slice(w * in_window, (w + 1) * in_window), slice(g * group, (g + 1) * group)
            both = dot(jnp.concatenate([key_high[span], key_low[span]], axis=0), right(rights[w][0], g))
            scores.append(both[:in_window] + both[in_window:] + dot(key_high[span], right(rights[w][1], g)))
    probs = []
    for score in scores:
        weight = jnp.exp2(score - jnp.max(score, axis=0, keepdims=True))
        probs.append((weight * (1.0 / jnp.sum(weight, axis=0, keepdims=True))).astype(jnp.bfloat16))
    attended = []
    for p in range(windows // 2):
        parts = []
        for g in range(groups):
            v = values[g * group : (g + 1) * group, p * pair : (p + 1) * pair]
            first = dot(v, jnp.concatenate([probs[2 * p * groups + g], blank_p], axis=0))
            second = dot(v, jnp.concatenate([blank_p, probs[(2 * p + 1) * groups + g]], axis=0))
            for h in range(4):
                rows_of = slice(h * HEAD, (h + 1) * HEAD)
                cols_of = slice((h // 2) * pair, (h // 2 + 1) * pair)
                a, b = first[rows_of, cols_of], second[rows_of, cols_of]
                if h % 2 == 0:
                    b = pltpu.roll(b, in_window, 1)
                else:
                    a = pltpu.roll(a, in_window, 1)
                parts.append(jnp.where(lane_head, a, b))
        attended.append(jnp.concatenate(parts, axis=0).astype(jnp.bfloat16))
    attended = jnp.concatenate(attended, axis=1)
    mixed = mixed_ref[...] + dot(attended, wo[...], TN)
    hidden = norm(mixed, gain_two[...])
    inner = dot(hidden, up[...])
    inner = (0.5 * inner * (1.0 + jnp.tanh(0.5 * inner))).astype(jnp.bfloat16)
    result = mixed + dot(inner, down[...])
    for half in range(2):
        result_ref[half] = result[:, half * channels : (half + 1) * channels]
    for v in range(group_size):
        for t in range(tile_cols):
            for i in range(rows):
                at = v * here + t * run * rows + i
                for half in range(2):
                    lanes = slice(half * channels, (half + 1) * channels)
                    line = result_ref[half, pl.ds(at, run, stride=rows), :]
                    out[v, i, t, :, lanes] = line.astype(jnp.bfloat16)


def window_weights(conv_weight, gain_first, window_in, window_out, window_scale, gain_second, hidden_up, hidden_down):
    width = conv_weight.shape[-1]
    return (
        conv_weight.reshape(9, width),
        gain_first[None],
        window_in[:, :width].T,
        window_in[:, width : 2 * width],
        window_in[:, 2 * width :].T,
        window_out,
        (window_scale * LOG2E).reshape(-1, 1),
        gain_second[None],
        hidden_up,
        hidden_down,
    )


def window_layer(phase, turned, ego_edges, pieces, before, weights):
    vehicles, cols, rows, channels = turned.shape
    width = 2 * channels
    tile_cols = cols // TILE
    run = TILE // PHASES
    group = vehicles
    whole = lambda x: pl.BlockSpec(x.shape, lambda r: (0,) * x.ndim)
    block = lambda *shape: pl.BlockSpec((group, *shape), lambda r: (r,) + (0,) * len(shape))
    pieces = [x.reshape(vehicles, -1, channels) for three in pieces for x in three]
    cells = vehicles * rows * tile_cols * run
    most = cols * rows
    operands = (turned, *ego_edges, *pieces, *weights)
    in_specs = (
        [block(cols, rows, channels)]
        + [block(1, cols, channels)] * 2
        + [block(*x.shape[1:]) for x in pieces]
        + [whole(w) for w in weights]
    )
    aliases = {}
    if before is not None:
        aliases = {len(operands): 0}
        operands += (before,)
        in_specs += [pl.BlockSpec(memory_space=pl.ANY)]
    return pl.pallas_call(
        functools.partial(window_kernel, phase, rows),
        out_shape=jax.ShapeDtypeStruct((vehicles, rows, tile_cols, PHASES, run, width), jnp.bfloat16),
        grid=(vehicles // group,),
        in_specs=in_specs,
        out_specs=pl.BlockSpec(
            (group, rows, tile_cols, None, run, width), lambda r: (r, 0, 0, phase, 0, 0)
        ),
        scratch_shapes=[
            pltpu.VMEM((group * rows * tile_cols * run, width), jnp.float32),
            pltpu.VMEM((2, group * rows * tile_cols * run, channels), jnp.float32),
            pltpu.VMEM((2 * PHASES + 2, most, channels), jnp.float32),
        ],
        input_output_aliases=aliases,
        compiler_params=pltpu.CompilerParams(vmem_limit_bytes=WINDOW_VMEM_BYTES),
        cost_estimate=pl.CostEstimate(
            flops=cells * width * width * 60, bytes_accessed=cells * width * 6, transcendentals=cells * width * 4
        ),
    )(*operands)


def beside(last, first):
    count = lax.axis_size("row")
    above = lax.ppermute(last, "row", [(i, i + 1) for i in range(count - 1)])
    below = lax.ppermute(first, "row", [(i + 1, i) for i in range(count - 1)])
    return above, below


def on_device(
    bev_maps,
    senders,
    shifts,
    counts,
    agent_query,
    agent_keyvalue,
    agent_out,
    agent_scale,
    conv_weight,
    gain_first,
    window_in,
    window_out,
    window_scale,
    gain_second,
    hidden_up,
    hidden_down,
):
    vehicles_here, rows, cols, channels = bev_maps.shape
    devices = lax.axis_size("veh")
    tile_cols = cols // TILE
    group = half_size()
    capacity = tile_cols * max(1, vehicles_here * senders.shape[1] // devices)
    turned, first, second = turn_maps(bev_maps)

    def swap(x):
        return lax.ppermute(x, "veh", [(i, (i + group) % devices) for i in range(devices)])

    def send(messages):
        return [
            lax.ppermute(
                x, "veh", [(i, i // group * group + (i + k + 1) % group) for i in range(devices)]
            )
            for k, x in enumerate(messages)
        ]

    far = swap(first)
    chosen, filled, *plan = plan_of(senders, shifts, counts, tile_cols, capacity)
    entries, listed, sizes_of, live, blank = plan
    plan = (entries, listed, sizes_of, blank)
    live = live.reshape(senders.shape[1], -1)
    near_messages = messages_for(chosen, filled, capacity, {0: first})
    near_tiles = send(near_messages)
    ego_edges = beside(bev_maps[:, rows - 1 :], bev_maps[:, :1])
    join_all = join_weights(agent_query, agent_keyvalue, agent_out, agent_scale)
    present = [present_cells(live, p, rows) for p in range(PHASES)]
    window_all = window_weights(
        conv_weight, gain_first, window_in, window_out, window_scale, gain_second, hidden_up, hidden_down
    )
    far, second, join_all, present, window_all, _ = lax.optimization_barrier(
        (far, second, join_all, present, window_all, near_messages)
    )
    far_tiles = send(messages_for(chosen, filled, capacity, {1: far}))
    later = swap(second)
    later_messages = messages_for(chosen, filled, capacity, {0: second, 1: later})
    later_tiles = send(later_messages)
    arrived = [[first, far, *near_tiles, *far_tiles], [second, later, *later_tiles]]
    origins = [
        [(0, 0), (1, 0)] + [(2 + k + part * (group - 1), 0) for k in range(group - 1) for part in (0, 1)],
        [(0, 0), (1, 0)] + [(2 + k, part * capacity) for k in range(group - 1) for part in (0, 1)],
    ]
    result, pieces = None, []
    for phase, own in enumerate((first, second)):
        if phase:
            plan, result = lax.optimization_barrier((plan, result))
        joined, top, low = join_agents(
            own, arrived[phase], origins[phase], tile_cols, plan, present[phase], join_all
        )
        pieces.append((joined, *beside(low, top)))
        result = window_layer(phase, turned, ego_edges, pieces, result, window_all)
    return result.reshape(vehicles_here, rows, cols, 2 * channels)


def solution(mesh):
    split_maps = P("veh", "row", None, None)
    return jax.shard_map(
        on_device,
        mesh=mesh,
        in_specs=(split_maps,) + (P(),) * 15,
        out_specs=split_maps,
        check_vma=False,
    )
```

```python
import functools
import math

import jax
import jax.numpy as jnp
from jax import lax
from jax.experimental import pallas as pl
from jax.experimental.pallas import tpu as pltpu
from jax.sharding import PartitionSpec as P

TILE = 32
WIN = 8
HEAD = 32
ENTRY_BITS = 10

norm_eps = 1e-05
unit_eps = 1e-06
LOG2E = math.log2(math.e)
VMEM_BYTES = 24 * 2**20
WINDOW_VMEM_BYTES = 60 * 2**20
PHASES = 2

NN = (((1,), (0,)), ((), ()))
NT = (((1,), (1,)), ((), ()))
TN = (((0,), (0,)), ((), ()))


def dot(a, b, dims=NN):
    return lax.dot_general(a, b, dims, preferred_element_type=jnp.float32)


def split(x):
    high = x.astype(jnp.bfloat16)
    return high, (x - high.astype(jnp.float32)).astype(jnp.bfloat16)


def head_sums(x):
    return jnp.sum(x.reshape(x.shape[0] // HEAD, HEAD, x.shape[1]), axis=1, keepdims=True)


def by_head(x, factor):
    return (x.reshape(x.shape[0] // HEAD, HEAD, x.shape[1]) * factor).reshape(x.shape)


def phase_columns(phase):
    run = TILE // PHASES
    return [TILE - 1] + list(range(run + 1)) if phase == 0 else list(range(run + 1, TILE - 1))


def half_size():
    return max(1, lax.axis_size("veh") // 2)


def turn_kernel(maps, turned, first, second, scratch):
    rows, cols, channels = maps.shape[1:]
    run = TILE // PHASES
    for i in range(rows):
        scratch[pl.ds(i, cols, stride=rows), :] = maps[0, i].astype(jnp.float32)
    x = scratch[...].astype(jnp.bfloat16).reshape(cols, rows, channels)
    turned[0] = x
    for t in range(cols // TILE):
        tile = x[t * TILE : (t + 1) * TILE]
        first[t] = jnp.concatenate([tile[TILE - 1 :], tile[: run + 1]], axis=0)
        second[t] = tile[run + 1 : TILE - 1]


def turn_maps(maps):
    vehicles, rows, cols, channels = maps.shape
    tile_cols = cols // TILE
    pieces = [(tile_cols, len(phase_columns(p)), rows, channels) for p in range(PHASES)]
    blocks = [(1, cols, rows, channels), *pieces]
    block = lambda shape: pl.BlockSpec(shape, lambda v: (v, 0, 0, 0))
    return pl.pallas_call(
        turn_kernel,
        out_shape=[jax.ShapeDtypeStruct((vehicles * n[0], *n[1:]), maps.dtype) for n in blocks],
        grid=(vehicles,),
        in_specs=[block((1, rows, cols, channels))],
        out_specs=[block(n) for n in blocks],
        scratch_shapes=[pltpu.VMEM((rows * cols, channels), jnp.float32)],
        compiler_params=pltpu.CompilerParams(vmem_limit_bytes=VMEM_BYTES),
        cost_estimate=pl.CostEstimate(flops=0, bytes_accessed=10 * maps.size, transcendentals=0),
    )(maps)


def plan_kernel(sizes, senders, shifts, counts, ids, chosen, filled, entries, listed, sizes_of, live, blank, sent):
    vehicles, agents, tile_cols, group, capacity = sizes
    me, partner = ids[0], ids[1]
    tiles_held = vehicles * tile_cols
    rank = me % group
    pairs = vehicles * agents

    def clear(i, _):
        sent[i] = 0
        return 0

    def clear_list(i, _):
        listed[i] = 0
        return 0

    spare = chosen.shape[0] - 1
    lax.fori_loop(0, sent.shape[0], clear, 0)
    lax.fori_loop(0, listed.shape[0], clear_list, 0)
    last = blank.shape[0] - 1
    nowhere = listed.shape[0] - 1

    def target(k, _):
        first = (me - rank + (rank + k + 1) % group) * vehicles

        def pair(i, n):
            r, a = first + i // agents, i % agents
            sender, shift = senders[r, a], shifts[r, a]
            tiles = tile_cols - jnp.abs(shift)
            source = sender // vehicles
            far = jnp.where(source == partner, 1, 0)
            filled_here = jnp.where(far == 1, n[1], n[0])
            fits = (a < counts[r]) & ((source == me) | (far == 1)) & (filled_here + tiles <= capacity)

            at = (2 * k + far) * capacity + filled_here
            tile = sender % vehicles * tile_cols + jnp.maximum(shift, 0)
            for t in range(tile_cols):
                chosen[jnp.where(fits & (t < tiles), at + t, spare)] = tile + t
            more = jnp.where(fits, tiles, 0)
            return n[0] + more * (1 - far), n[1] + more * far

        near, far = lax.fori_loop(0, pairs, pair, (0, 0))
        filled[2 * k] = near
        filled[2 * k + 1] = far
        return 0

    lax.fori_loop(0, group - 1, target, 0)

    def pair(i, bare):
        v, a = i // agents, i % agents
        r = me * vehicles + v
        sender, shift = senders[r, a], shifts[r, a]
        alive = a < counts[r]
        source = sender // vehicles
        n = sent[source]
        k = (rank - source % group + group) % group
        apart = jnp.where(source // group == me // group, 0, 1)
        slot = jnp.where(k == 0, sender % vehicles * tile_cols + jnp.maximum(shift, 0), n)
        origin = jnp.where(k == 0, 0, 2 * k) + apart
        tiles = jnp.where(alive, tile_cols - jnp.abs(shift), 0)
        base = a * tiles_held + v * tile_cols
        first = jnp.maximum(-shift, 0)

        here = jnp.where(tiles > 0, origin * tile_cols + tiles - 1, nowhere)
        entries[here * pairs + listed[here]] = ((base + first) << ENTRY_BITS) + slot
        listed[here] = listed[here] + 1
        sizes_of[a * vehicles + v] = tiles
        for t in range(tile_cols):
            inside = (t >= first) & (t < first + tiles)
            live[base + t] = jnp.where(inside, 1, 0)

            blank[jnp.where(inside, last, bare)] = base + t
            bare = bare + jnp.where(inside, 0, 1)

        sent[source] = n + tiles
        return bare

    blank[last] = lax.fori_loop(0, pairs, pair, 0)


def plan_of(senders, shifts, counts, tile_cols, capacity):
    devices = lax.axis_size("veh")
    group = half_size()
    vehicles, agents = senders.shape[0] // devices, senders.shape[1]
    me = lax.axis_index("veh").astype(jnp.int32)
    ids = jnp.stack([me, (me + group) % devices])
    pairs = agents * vehicles
    places = 2 * group * tile_cols
    sizes = [(group - 1) * 2 * capacity + 1, (group - 1) * 2, (places + 1) * pairs, places + 1, pairs]
    sizes += [pairs * tile_cols, pairs * tile_cols + 1]
    smem = pl.BlockSpec(memory_space=pltpu.SMEM)
    return pl.pallas_call(
        functools.partial(plan_kernel, (vehicles, agents, tile_cols, group, capacity)),
        out_shape=[jax.ShapeDtypeStruct((n,), jnp.int32) for n in sizes],
        in_specs=[smem] * 4,
        out_specs=[smem] * 7,
        scratch_shapes=[pltpu.SMEM((devices,), jnp.int32)],
        compiler_params=pltpu.CompilerParams(vmem_limit_bytes=VMEM_BYTES),
        cost_estimate=pl.CostEstimate(flops=0, bytes_accessed=20 * 2**20, transcendentals=0),
    )(senders, shifts, counts, ids)


def send_kernel(sources, capacity, chosen, filled, *refs):
    bufs, messages, sems = refs[: len(sources)], refs[len(sources) : -1], refs[-1]
    copies = []
    for k, message in enumerate(messages):
        for b, source in enumerate(sources):

            def copy(i, tile, k=k, b=b, message=message):
                slot = b * capacity + i
                return pltpu.make_async_copy(bufs[b].at[tile], message.at[slot], sems.at[k, slot])

            copies.append((2 * k + source, copy))
    for at, copy in copies:
        lax.fori_loop(
            0, filled[at], lambda i, _: (copy(i, chosen[at * capacity + i]).start(), 0)[1], 0
        )
    for at, copy in copies:
        lax.fori_loop(0, filled[at], lambda i, _: (copy(i, 0).wait(), 0)[1], 0)


def messages_for(chosen, filled, capacity, sources):
    first = next(iter(sources.values()))
    count = filled.shape[0] // 2
    shape = (len(sources) * capacity, *first.shape[1:])
    anywhere = pl.BlockSpec(memory_space=pl.ANY)
    return pl.pallas_call(
        functools.partial(send_kernel, tuple(sources), capacity),
        out_shape=[jax.ShapeDtypeStruct(shape, first.dtype)] * count,
        grid_spec=pltpu.PrefetchScalarGridSpec(
            num_scalar_prefetch=2,
            grid=(1,),
            in_specs=[anywhere] * len(sources),
            out_specs=[anywhere] * count,
            scratch_shapes=[pltpu.SemaphoreType.DMA((count, shape[0]))],
        ),
        compiler_params=pltpu.CompilerParams(vmem_limit_bytes=VMEM_BYTES),
        cost_estimate=pl.CostEstimate(
            flops=0, bytes_accessed=4 * count * math.prod(shape), transcendentals=0
        ),
    )(chosen, filled, *sources.values())


LANES = 256


def join_kernel(origins, tile_cols, entries, listed, sizes_of, blank, ego, *refs):
    buffers = 1 + max(b for b, _ in origins)
    bufs, refs = refs[:buffers], refs[buffers:]
    present, wq, wkv, wout, scale, out, top_row, low_row, landed, joined, sems = refs
    count, cells, channels = landed.shape
    agents = present.shape[0]
    pieces = count // agents
    vehicles = pieces // tile_cols
    total = pieces * cells
    pairs = agents * vehicles

    def copy(source, at, size, pair):
        return pltpu.make_async_copy(source, landed.at[pl.ds(at, size)], sems.at[pair])

    for origin, (b, offset) in enumerate(origins):
        for size in range(tile_cols, 0, -1):
            place = origin * tile_cols + size - 1

            def fetch(i, _, b=b, offset=offset, size=size, place=place):
                entry = entries[place * pairs + i]
                at, tile = entry >> ENTRY_BITS, entry & ((1 << ENTRY_BITS) - 1)
                copy(bufs[b].at[pl.ds(tile + offset, size)], at, size, at // tile_cols).start()
                return 0

            lax.fori_loop(0, listed[place], fetch, 0)

    def clear(i, _):
        landed[blank[i]] = jnp.zeros((cells, channels), landed.dtype)
        return 0

    lax.fori_loop(0, blank[blank.shape[0] - 1], clear, 0)
    arrived = 0
    heads = channels // HEAD
    scale_col = scale[...].reshape(heads, 1, 1)
    landed_cells = landed.reshape(agents, total, channels)
    for c in range(total // LANES):
        while arrived * tile_cols * cells < (c + 1) * LANES:
            for a in range(agents):
                for size in range(1, tile_cols + 1):
                    pair = a * vehicles + arrived

                    @pl.when(sizes_of[pair] == size)
                    def _(size=size, pair=pair):
                        copy(bufs[0].at[pl.ds(0, size)], pair * tile_cols, size, pair).wait()

            arrived += 1
        span = pl.ds(c * LANES, LANES)
        cells_here = ego[span, :]
        queries = dot(wq[...], cells_here, NT)
        factor = lax.rsqrt(head_sums(queries * queries) + unit_eps) * scale_col

        def agent(x):
            kv = dot(wkv[...], x, NT).astype(jnp.bfloat16).astype(jnp.float32)
            keys, values = kv[:channels], kv[channels:]
            score = head_sums(queries * keys) * factor
            return score * lax.rsqrt(head_sums(keys * keys) + unit_eps), values

        scores, values = zip(
            agent(cells_here),
            *(
                agent(landed_cells[a, span, :])
                for a in range(agents)
            ),
        )
        scores = [scores[0]] + [
            jnp.where(present[a : a + 1, c * LANES : (c + 1) * LANES].reshape(1, 1, LANES) > 0, s, -1e30)
            for a, s in enumerate(scores[1:])
        ]
        top = functools.reduce(jnp.maximum, scores)
        weights = [jnp.exp(s - top) for s in scores]
        inverse = 1.0 / functools.reduce(jnp.add, weights)
        mix = functools.reduce(jnp.add, [by_head(v, w * inverse) for w, v in zip(weights, values)])
        joined[span, :] = dot(mix.astype(jnp.bfloat16), wout[...], TN)
    out[...] = joined[...].astype(jnp.bfloat16)
    edge = top_row.shape[1]
    rows = total // (vehicles * edge)
    for v in range(vehicles):
        start = v * edge * rows
        top_row[v] = joined[pl.ds(start, edge, stride=rows), :].astype(jnp.bfloat16)
        low_row[v] = joined[pl.ds(start + rows - 1, edge, stride=rows), :].astype(jnp.bfloat16)


def join_weights(wq, wkv, wout, scale):
    return wq.T, wkv.T, wout, scale.reshape(-1, 1)


def present_cells(live, phase, rows):
    return jnp.repeat(live.astype(jnp.float32), len(phase_columns(phase)) * rows, axis=1)


def join_agents(pieces, arrived, origins, tile_cols, plan, present, weights):
    count, cols, rows, channels = pieces.shape
    agents = present.shape[0]
    cells = cols * rows
    total = count * cells
    whole = lambda shape: pl.BlockSpec(shape, lambda r, *_: (0,) * len(shape))
    shapes = [(total, channels)] + [(count // tile_cols, tile_cols * cols, channels)] * 2
    return pl.pallas_call(
        functools.partial(join_kernel, origins, tile_cols),
        out_shape=[jax.ShapeDtypeStruct(shape, jnp.bfloat16) for shape in shapes],
        grid_spec=pltpu.PrefetchScalarGridSpec(
            num_scalar_prefetch=4,
            grid=(1,),
            in_specs=[
                whole((total, channels)),
                *[pl.BlockSpec(memory_space=pl.ANY)] * len(arrived),
                whole(present.shape),
            ]
            + [whole(w.shape) for w in weights],
            out_specs=[whole(shape) for shape in shapes],
            scratch_shapes=[
                pltpu.VMEM((agents * count, cells, channels), jnp.bfloat16),
                pltpu.VMEM((total, channels), jnp.float32),
                pltpu.SemaphoreType.DMA((agents * count // tile_cols,)),
            ],
        ),
        compiler_params=pltpu.CompilerParams(vmem_limit_bytes=VMEM_BYTES),
        cost_estimate=pl.CostEstimate(
            flops=total * channels * channels * 40, bytes_accessed=total * channels * 12, transcendentals=total * 20
        ),
    )(
        *plan,
        pieces.reshape(total, channels),
        *(x.reshape(-1, cells, channels) for x in arrived),
        present,
        *weights,
    )


def norm(x, gain):
    average = jnp.mean(x, axis=-1, keepdims=True)
    centred = x - average
    spread = jnp.mean(centred * centred, axis=-1, keepdims=True)
    return (centred * lax.rsqrt(spread + norm_eps) * gain).astype(jnp.bfloat16)


def spread_rows(ref, rows_of, at, rows):
    count, channels = rows_of.shape
    ref[pl.ds(at, count, stride=rows), :] = rows_of.astype(jnp.float32)
    return ref[: count * rows].reshape(count, rows, channels)


def runs_of(phase, tile_cols, whole_map, pieces):
    run = TILE // PHASES
    out = []
    for t in range(tile_cols):
        first = t * TILE + phase * run - 1
        if pieces is None:
            last = first + run + 2
            blank = jnp.zeros_like(whole_map[:1])
            body = whole_map[max(first, 0) : min(last, tile_cols * TILE)]
            parts = ([blank] if first < 0 else []) + [body] + ([blank] if last > tile_cols * TILE else [])
        else:
            size = run + 2
            one = pieces[0]
            blank = jnp.zeros_like(one[:1])
            if phase == 0:
                left = one[(t - 1) * size : (t - 1) * size + 1] if t else blank
                parts = [left, one[t * size + 1 : (t + 1) * size]]
            else:
                rest = TILE - size
                right = one[(t + 1) * size + 1 : (t + 1) * size + 2] if t + 1 < tile_cols else blank
                parts = [
                    one[t * size + run : (t + 1) * size],
                    pieces[1][t * rest : (t + 1) * rest],
                    one[t * size : t * size + 1],
                    right,
                ]
        out.append(jnp.concatenate(parts, axis=0))
    return out


def taps_of(runs, above, below, taps):
    out = []
    for x, first, last in zip(runs, above, below):
        cols, rows, channels = x.shape
        row = lax.broadcasted_iota(jnp.int32, (rows, channels), 0)[None]
        flat = x.reshape(cols * rows, channels)
        over = jnp.where(row == 0, first, pltpu.roll(flat, 1, 0).reshape(x.shape))
        under = jnp.where(row == rows - 1, last, pltpu.roll(flat, cols * rows - 1, 0).reshape(x.shape))
        total = x[1 : cols - 1]
        for j in range(3):
            span = slice(j, cols - 2 + j)
            total = total + over[span] * taps[j] + x[span] * taps[3 + j] + under[span] * taps[6 + j]
        out.append(total.reshape((cols - 2) * rows, channels))
    return out


def window_kernel(phase, rows, *refs):
    ego, ego_up, ego_down, refs = *refs[:3], refs[3:]
    pieces, refs = [refs[3 * p : 3 * p + 3] for p in range(phase + 1)], refs[3 * phase + 3 :]
    taps, gain_one, wq, wk, wv, wo, scale, gain_two, up, down = refs[:10]
    out, mixed_ref, result_ref, halo = refs[10 + phase :]
    group_size, cols, _, channels = ego.shape
    tile_cols = cols // TILE
    run = TILE // PHASES
    width = 2 * channels
    in_window = rows * WIN
    here = tile_cols * run * rows
    cells = group_size * here
    windows = cells // in_window
    heads = width // HEAD
    f32 = jnp.float32
    for v in range(group_size):
        for half in range(2):
            lanes = slice(half * channels, (half + 1) * channels)
            weights = [taps[i : i + 1, lanes].reshape(1, 1, channels) for i in range(9)]
            if half == 0:
                centre = runs_of(phase, tile_cols, ego[v].astype(f32), None)
                above = runs_of(phase, tile_cols, spread_rows(halo.at[0], ego_up[v, 0], 0, rows), None)
                below = runs_of(phase, tile_cols, spread_rows(halo.at[1], ego_down[v, 0], rows - 1, rows), None)
            else:
                centre, above, below = [], [], []
                for p, (x, first, last) in enumerate(pieces):
                    centre.append(x[v].astype(f32).reshape(-1, rows, channels))
                    above.append(spread_rows(halo.at[2 + 2 * p], first[v], 0, rows))
                    below.append(spread_rows(halo.at[3 + 2 * p], last[v], rows - 1, rows))
                centre, above, below = (runs_of(phase, tile_cols, None, x) for x in (centre, above, below))
            for t, part in enumerate(taps_of(centre, above, below, weights)):
                at = v * here + t * run * rows
                mixed_ref[at : at + run * rows, lanes] = part
    hidden = norm(mixed_ref[...], gain_one[...])
    queries = dot(wq[...], hidden, NT)
    values = dot(wv[...], hidden, NT).astype(jnp.bfloat16)
    keys = dot(hidden, wk[...])
    factor = lax.rsqrt(head_sums(queries * queries) + unit_eps) * scale[...].reshape(heads, 1, 1)
    queries = by_head(queries, factor)
    member = (
        lax.broadcasted_iota(jnp.int32, (width, width), 0) // HEAD
        == lax.broadcasted_iota(jnp.int32, (width, width), 1) // HEAD
    ).astype(f32).astype(jnp.bfloat16)
    square_high, square_low = split(keys * keys)
    keys = keys * lax.rsqrt(dot(square_high, member) + dot(square_low, member) + unit_eps)
    key_high, key_low = split(keys)

    pair = 2 * in_window
    group = 4 * HEAD
    lane = lax.broadcasted_iota(jnp.int32, (width, pair), 1) < in_window
    even = (lax.broadcasted_iota(jnp.int32, (width, pair), 0) // HEAD) % 2 == 0
    blank = jnp.zeros((2 * HEAD, pair), jnp.bfloat16)
    blank_p = jnp.zeros((in_window, 4 * in_window), jnp.bfloat16)
    lane_head = lax.broadcasted_iota(jnp.int32, (HEAD, pair), 1) < in_window
    rights = []
    for p in range(windows // 2):
        straight = queries[:, p * pair : (p + 1) * pair]
        turned = pltpu.roll(straight, in_window, 1)
        for w in range(2):
            low, high = (straight, turned) if w == 0 else (turned, straight)
            rights.append(split(jnp.where(even, jnp.where(lane, low, 0.0), jnp.where(lane, 0.0, high))))

    def right(block, g):
        block = block[g * group : (g + 1) * group]
        return jnp.concatenate(
            [
                jnp.concatenate([block[: 2 * HEAD], blank], axis=1),
                jnp.concatenate([blank, block[2 * HEAD :]], axis=1),
            ],
            axis=0,
        )

    groups = width // group
    scores = []
    for w in range(windows):
        for g in range(groups):
            span = slice(w * in_window, (w + 1) * in_window), slice(g * group, (g + 1) * group)
            both = dot(jnp.concatenate([key_high[span], key_low[span]], axis=0), right(rights[w][0], g))
            scores.append(both[:in_window] + both[in_window:] + dot(key_high[span], right(rights[w][1], g)))
    probs = []
    for score in scores:
        weight = jnp.exp2(score - jnp.max(score, axis=0, keepdims=True))
        probs.append((weight * (1.0 / jnp.sum(weight, axis=0, keepdims=True))).astype(jnp.bfloat16))
    attended = []
    for p in range(windows // 2):
        parts = []
        for g in range(groups):
            v = values[g * group : (g + 1) * group, p * pair : (p + 1) * pair]
            first = dot(v, jnp.concatenate([probs[2 * p * groups + g], blank_p], axis=0))
            second = dot(v, jnp.concatenate([blank_p, probs[(2 * p + 1) * groups + g]], axis=0))
            for h in range(4):
                rows_of = slice(h * HEAD, (h + 1) * HEAD)
                cols_of = slice((h // 2) * pair, (h // 2 + 1) * pair)
                a, b = first[rows_of, cols_of], second[rows_of, cols_of]
                if h % 2 == 0:
                    b = pltpu.roll(b, in_window, 1)
                else:
                    a = pltpu.roll(a, in_window, 1)
                parts.append(jnp.where(lane_head, a, b))
        attended.append(jnp.concatenate(parts, axis=0).astype(jnp.bfloat16))
    attended = jnp.concatenate(attended, axis=1)
    mixed = mixed_ref[...] + dot(attended, wo[...], TN)
    hidden = norm(mixed, gain_two[...])
    inner = dot(hidden, up[...])
    inner = (0.5 * inner * (1.0 + jnp.tanh(0.5 * inner))).astype(jnp.bfloat16)
    result = mixed + dot(inner, down[...])
    for half in range(2):
        result_ref[half] = result[:, half * channels : (half + 1) * channels]
    for v in range(group_size):
        for t in range(tile_cols):
            for i in range(rows):
                at = v * here + t * run * rows + i
                for half in range(2):
                    lanes = slice(half * channels, (half + 1) * channels)
                    line = result_ref[half, pl.ds(at, run, stride=rows), :]
                    out[v, i, t, :, lanes] = line.astype(jnp.bfloat16)


def window_weights(conv_weight, gain_first, window_in, window_out, window_scale, gain_second, hidden_up, hidden_down):
    width = conv_weight.shape[-1]
    return (
        conv_weight.reshape(9, width),
        gain_first[None],
        window_in[:, :width].T,
        window_in[:, width : 2 * width],
        window_in[:, 2 * width :].T,
        window_out,
        (window_scale * LOG2E).reshape(-1, 1),
        gain_second[None],
        hidden_up,
        hidden_down,
    )


def window_layer(phase, turned, ego_edges, pieces, before, weights):
    vehicles, cols, rows, channels = turned.shape
    width = 2 * channels
    tile_cols = cols // TILE
    run = TILE // PHASES
    group = vehicles
    whole = lambda x: pl.BlockSpec(x.shape, lambda r: (0,) * x.ndim)
    block = lambda *shape: pl.BlockSpec((group, *shape), lambda r: (r,) + (0,) * len(shape))
    pieces = [x.reshape(vehicles, -1, channels) for three in pieces for x in three]
    cells = vehicles * rows * tile_cols * run
    most = cols * rows
    operands = (turned, *ego_edges, *pieces, *weights)
    in_specs = (
        [block(cols, rows, channels)]
        + [block(1, cols, channels)] * 2
        + [block(*x.shape[1:]) for x in pieces]
        + [whole(w) for w in weights]
    )
    aliases = {}
    if before is not None:
        aliases = {len(operands): 0}
        operands += (before,)
        in_specs += [pl.BlockSpec(memory_space=pl.ANY)]
    return pl.pallas_call(
        functools.partial(window_kernel, phase, rows),
        out_shape=jax.ShapeDtypeStruct((vehicles, rows, tile_cols, PHASES, run, width), jnp.bfloat16),
        grid=(vehicles // group,),
        in_specs=in_specs,
        out_specs=pl.BlockSpec(
            (group, rows, tile_cols, None, run, width), lambda r: (r, 0, 0, phase, 0, 0)
        ),
        scratch_shapes=[
            pltpu.VMEM((group * rows * tile_cols * run, width), jnp.float32),
            pltpu.VMEM((2, group * rows * tile_cols * run, channels), jnp.float32),
            pltpu.VMEM((2 * PHASES + 2, most, channels), jnp.float32),
        ],
        input_output_aliases=aliases,
        compiler_params=pltpu.CompilerParams(vmem_limit_bytes=WINDOW_VMEM_BYTES),
        cost_estimate=pl.CostEstimate(
            flops=cells * width * width * 60, bytes_accessed=cells * width * 6, transcendentals=cells * width * 4
        ),
    )(*operands)


def beside(last, first):
    count = lax.axis_size("row")
    above = lax.ppermute(last, "row", [(i, i + 1) for i in range(count - 1)])
    below = lax.ppermute(first, "row", [(i + 1, i) for i in range(count - 1)])
    return above, below


def on_device(
    bev_maps,
    senders,
    shifts,
    counts,
    agent_query,
    agent_keyvalue,
    agent_out,
    agent_scale,
    conv_weight,
    gain_first,
    window_in,
    window_out,
    window_scale,
    gain_second,
    hidden_up,
    hidden_down,
):
    vehicles_here, rows, cols, channels = bev_maps.shape
    devices = lax.axis_size("veh")
    tile_cols = cols // TILE
    group = half_size()
    capacity = tile_cols * max(1, vehicles_here * senders.shape[1] // devices)
    turned, first, second = turn_maps(bev_maps)

    def swap(x):
        return lax.ppermute(x, "veh", [(i, (i + group) % devices) for i in range(devices)])

    def send(messages):
        return [
            lax.ppermute(
                x, "veh", [(i, i // group * group + (i + k + 1) % group) for i in range(devices)]
            )
            for k, x in enumerate(messages)
        ]

    far = swap(first)
    chosen, filled, *plan = plan_of(senders, shifts, counts, tile_cols, capacity)
    entries, listed, sizes_of, live, blank = plan
    plan = (entries, listed, sizes_of, blank)
    live = live.reshape(senders.shape[1], -1)
    near_messages = messages_for(chosen, filled, capacity, {0: first})
    near_tiles = send(near_messages)
    ego_edges = beside(bev_maps[:, rows - 1 :], bev_maps[:, :1])
    join_all = join_weights(agent_query, agent_keyvalue, agent_out, agent_scale)
    present = [present_cells(live, p, rows) for p in range(PHASES)]
    window_all = window_weights(
        conv_weight, gain_first, window_in, window_out, window_scale, gain_second, hidden_up, hidden_down
    )
    far, second, join_all, present, window_all, _ = lax.optimization_barrier(
        (far, second, join_all, present, window_all, near_messages)
    )
    far_tiles = send(messages_for(chosen, filled, capacity, {1: far}))
    later = swap(second)
    later_messages = messages_for(chosen, filled, capacity, {0: second, 1: later})
    later_tiles = send(later_messages)
    arrived = [[first, far, *near_tiles, *far_tiles], [second, later, *later_tiles]]
    origins = [
        [(0, 0), (1, 0)] + [(2 + k + part * (group - 1), 0) for k in range(group - 1) for part in (0, 1)],
        [(0, 0), (1, 0)] + [(2 + k, part * capacity) for k in range(group - 1) for part in (0, 1)],
    ]
    result, pieces = None, []
    for phase, own in enumerate((first, second)):
        if phase:
            plan, result = lax.optimization_barrier((plan, result))
        joined, top, low = join_agents(
            own, arrived[phase], origins[phase], tile_cols, plan, present[phase], join_all
        )
        pieces.append((joined, *beside(low, top)))
        result = window_layer(phase, turned, ego_edges, pieces, result, window_all)
    return result.reshape(vehicles_here, rows, cols, 2 * channels)


def solution(mesh):
    split_maps = P("veh", "row", None, None)
    return jax.shard_map(
        on_device,
        mesh=mesh,
        in_specs=(split_maps,) + (P(),) * 15,
        out_specs=split_maps,
        check_vma=False,
    )
```

```python
import functools
import math

import jax
import jax.numpy as jnp
from jax import lax
from jax.experimental import pallas as pl
from jax.experimental.pallas import tpu as pltpu
from jax.sharding import PartitionSpec as P

TILE = 32
WIN = 8
HEAD = 32
ENTRY_BITS = 10

norm_eps = 1e-05
unit_eps = 1e-06
LOG2E = math.log2(math.e)
VMEM_BYTES = 24 * 2**20
WINDOW_VMEM_BYTES = 40 * 2**20
PHASES = 2

NN = (((1,), (0,)), ((), ()))
NT = (((1,), (1,)), ((), ()))
TN = (((0,), (0,)), ((), ()))


def dot(a, b, dims=NN):
    return lax.dot_general(a, b, dims, preferred_element_type=jnp.float32)


def split(x):
    high = x.astype(jnp.bfloat16)
    return high, (x - high.astype(jnp.float32)).astype(jnp.bfloat16)


def head_sums(x):
    return jnp.sum(x.reshape(x.shape[0] // HEAD, HEAD, x.shape[1]), axis=1, keepdims=True)


def by_head(x, factor):
    return (x.reshape(x.shape[0] // HEAD, HEAD, x.shape[1]) * factor).reshape(x.shape)


def phase_columns(phase):
    run = TILE // PHASES
    return [TILE - 1] + list(range(run + 1)) if phase == 0 else list(range(run + 1, TILE - 1))


def half_size():
    return max(1, lax.axis_size("veh") // 2)


def turn_kernel(maps, turned, first, second, scratch):
    rows, cols, channels = maps.shape[1:]
    run = TILE // PHASES
    for i in range(rows):
        scratch[pl.ds(i, cols, stride=rows), :] = maps[0, i].astype(jnp.float32)
    x = scratch[...].astype(jnp.bfloat16).reshape(cols, rows, channels)
    turned[0] = x
    for t in range(cols // TILE):
        tile = x[t * TILE : (t + 1) * TILE]
        first[t] = jnp.concatenate([tile[TILE - 1 :], tile[: run + 1]], axis=0)
        second[t] = tile[run + 1 : TILE - 1]


def turn_maps(maps):
    vehicles, rows, cols, channels = maps.shape
    tile_cols = cols // TILE
    pieces = [(tile_cols, len(phase_columns(p)), rows, channels) for p in range(PHASES)]
    blocks = [(1, cols, rows, channels), *pieces]
    block = lambda shape: pl.BlockSpec(shape, lambda v: (v, 0, 0, 0))
    return pl.pallas_call(
        turn_kernel,
        out_shape=[jax.ShapeDtypeStruct((vehicles * n[0], *n[1:]), maps.dtype) for n in blocks],
        grid=(vehicles,),
        in_specs=[block((1, rows, cols, channels))],
        out_specs=[block(n) for n in blocks],
        scratch_shapes=[pltpu.VMEM((rows * cols, channels), jnp.float32)],
        compiler_params=pltpu.CompilerParams(vmem_limit_bytes=VMEM_BYTES),
        cost_estimate=pl.CostEstimate(flops=0, bytes_accessed=10 * maps.size, transcendentals=0),
    )(maps)


def plan_kernel(sizes, senders, shifts, counts, ids, chosen, filled, entries, listed, sizes_of, live, blank, sent):
    vehicles, agents, tile_cols, group, capacity = sizes
    me, partner = ids[0], ids[1]
    tiles_held = vehicles * tile_cols
    rank = me % group
    pairs = vehicles * agents

    def clear(i, _):
        sent[i] = 0
        return 0

    def clear_list(i, _):
        listed[i] = 0
        return 0

    spare = chosen.shape[0] - 1
    lax.fori_loop(0, sent.shape[0], clear, 0)
    lax.fori_loop(0, listed.shape[0], clear_list, 0)
    last = blank.shape[0] - 1
    nowhere = listed.shape[0] - 1

    def target(k, _):
        first = (me - rank + (rank + k + 1) % group) * vehicles

        def pair(i, n):
            r, a = first + i // agents, i % agents
            sender, shift = senders[r, a], shifts[r, a]
            tiles = tile_cols - jnp.abs(shift)
            source = sender // vehicles
            far = jnp.where(source == partner, 1, 0)
            filled_here = jnp.where(far == 1, n[1], n[0])
            fits = (a < counts[r]) & ((source == me) | (far == 1)) & (filled_here + tiles <= capacity)

            at = (2 * k + far) * capacity + filled_here
            tile = sender % vehicles * tile_cols + jnp.maximum(shift, 0)
            for t in range(tile_cols):
                chosen[jnp.where(fits & (t < tiles), at + t, spare)] = tile + t
            more = jnp.where(fits, tiles, 0)
            return n[0] + more * (1 - far), n[1] + more * far

        near, far = lax.fori_loop(0, pairs, pair, (0, 0))
        filled[2 * k] = near
        filled[2 * k + 1] = far
        return 0

    lax.fori_loop(0, group - 1, target, 0)

    def pair(i, bare):
        v, a = i // agents, i % agents
        r = me * vehicles + v
        sender, shift = senders[r, a], shifts[r, a]
        alive = a < counts[r]
        source = sender // vehicles
        n = sent[source]
        k = (rank - source % group + group) % group
        apart = jnp.where(source // group == me // group, 0, 1)
        slot = jnp.where(k == 0, sender % vehicles * tile_cols + jnp.maximum(shift, 0), n)
        origin = jnp.where(k == 0, 0, 2 * k) + apart
        tiles = jnp.where(alive, tile_cols - jnp.abs(shift), 0)
        base = a * tiles_held + v * tile_cols
        first = jnp.maximum(-shift, 0)

        here = jnp.where(tiles > 0, origin * tile_cols + tiles - 1, nowhere)
        entries[here * pairs + listed[here]] = ((base + first) << ENTRY_BITS) + slot
        listed[here] = listed[here] + 1
        sizes_of[a * vehicles + v] = tiles
        for t in range(tile_cols):
            inside = (t >= first) & (t < first + tiles)
            live[base + t] = jnp.where(inside, 1, 0)

            blank[jnp.where(inside, last, bare)] = base + t
            bare = bare + jnp.where(inside, 0, 1)

        sent[source] = n + tiles
        return bare

    blank[last] = lax.fori_loop(0, pairs, pair, 0)


def plan_of(senders, shifts, counts, tile_cols, capacity):
    devices = lax.axis_size("veh")
    group = half_size()
    vehicles, agents = senders.shape[0] // devices, senders.shape[1]
    me = lax.axis_index("veh").astype(jnp.int32)
    ids = jnp.stack([me, (me + group) % devices])
    pairs = agents * vehicles
    places = 2 * group * tile_cols
    sizes = [(group - 1) * 2 * capacity + 1, (group - 1) * 2, (places + 1) * pairs, places + 1, pairs]
    sizes += [pairs * tile_cols, pairs * tile_cols + 1]
    smem = pl.BlockSpec(memory_space=pltpu.SMEM)
    return pl.pallas_call(
        functools.partial(plan_kernel, (vehicles, agents, tile_cols, group, capacity)),
        out_shape=[jax.ShapeDtypeStruct((n,), jnp.int32) for n in sizes],
        in_specs=[smem] * 4,
        out_specs=[smem] * 7,
        scratch_shapes=[pltpu.SMEM((devices,), jnp.int32)],
        compiler_params=pltpu.CompilerParams(vmem_limit_bytes=VMEM_BYTES),
        cost_estimate=pl.CostEstimate(flops=0, bytes_accessed=20 * 2**20, transcendentals=0),
    )(senders, shifts, counts, ids)


def send_kernel(sources, capacity, chosen, filled, *refs):
    bufs, messages, sems = refs[: len(sources)], refs[len(sources) : -1], refs[-1]
    copies = []
    for k, message in enumerate(messages):
        for b, source in enumerate(sources):

            def copy(i, tile, k=k, b=b, message=message):
                slot = b * capacity + i
                return pltpu.make_async_copy(bufs[b].at[tile], message.at[slot], sems.at[k, slot])

            copies.append((2 * k + source, copy))
    for at, copy in copies:
        lax.fori_loop(
            0, filled[at], lambda i, _: (copy(i, chosen[at * capacity + i]).start(), 0)[1], 0
        )
    for at, copy in copies:
        lax.fori_loop(0, filled[at], lambda i, _: (copy(i, 0).wait(), 0)[1], 0)


def messages_for(chosen, filled, capacity, sources):
    first = next(iter(sources.values()))
    count = filled.shape[0] // 2
    shape = (len(sources) * capacity, *first.shape[1:])
    anywhere = pl.BlockSpec(memory_space=pl.ANY)
    return pl.pallas_call(
        functools.partial(send_kernel, tuple(sources), capacity),
        out_shape=[jax.ShapeDtypeStruct(shape, first.dtype)] * count,
        grid_spec=pltpu.PrefetchScalarGridSpec(
            num_scalar_prefetch=2,
            grid=(1,),
            in_specs=[anywhere] * len(sources),
            out_specs=[anywhere] * count,
            scratch_shapes=[pltpu.SemaphoreType.DMA((count, shape[0]))],
        ),
        compiler_params=pltpu.CompilerParams(vmem_limit_bytes=VMEM_BYTES),
        cost_estimate=pl.CostEstimate(
            flops=0, bytes_accessed=4 * count * math.prod(shape), transcendentals=0
        ),
    )(chosen, filled, *sources.values())


LANES = 256


def join_kernel(origins, tile_cols, entries, listed, sizes_of, blank, ego, *refs):
    buffers = 1 + max(b for b, _ in origins)
    bufs, refs = refs[:buffers], refs[buffers:]
    present, wq, wkv, wout, scale, out, top_row, low_row, landed, joined, sems = refs
    count, cells, channels = landed.shape
    agents = present.shape[0]
    pieces = count // agents
    vehicles = pieces // tile_cols
    total = pieces * cells
    pairs = agents * vehicles

    def copy(source, at, size, pair):
        return pltpu.make_async_copy(source, landed.at[pl.ds(at, size)], sems.at[pair])

    for origin, (b, offset) in enumerate(origins):
        for size in range(tile_cols, 0, -1):
            place = origin * tile_cols + size - 1

            def fetch(i, _, b=b, offset=offset, size=size, place=place):
                entry = entries[place * pairs + i]
                at, tile = entry >> ENTRY_BITS, entry & ((1 << ENTRY_BITS) - 1)
                copy(bufs[b].at[pl.ds(tile + offset, size)], at, size, at // tile_cols).start()
                return 0

            lax.fori_loop(0, listed[place], fetch, 0)

    def clear(i, _):
        landed[blank[i]] = jnp.zeros((cells, channels), landed.dtype)
        return 0

    lax.fori_loop(0, blank[blank.shape[0] - 1], clear, 0)
    arrived = 0
    heads = channels // HEAD
    scale_col = scale[:, :1].reshape(heads, 1, 1)
    landed_cells = landed.reshape(agents, total, channels)
    for c in range(total // LANES):
        while arrived * tile_cols * cells < (c + 1) * LANES:
            for a in range(agents):
                for size in range(1, tile_cols + 1):
                    pair = a * vehicles + arrived

                    @pl.when(sizes_of[pair] == size)
                    def _(size=size, pair=pair):
                        copy(bufs[0].at[pl.ds(0, size)], pair * tile_cols, size, pair).wait()

            arrived += 1
        span = pl.ds(c * LANES, LANES)
        cells_here = ego[span, :]
        queries = dot(wq[...], cells_here, NT)
        factor = lax.rsqrt(head_sums(queries * queries) + unit_eps) * scale_col

        def agent(x):
            kv = dot(wkv[...], x, NT).astype(jnp.bfloat16).astype(jnp.float32)
            keys, values = kv[:channels], kv[channels:]
            score = head_sums(queries * keys) * factor
            return score * lax.rsqrt(head_sums(keys * keys) + unit_eps), values

        scores, values = zip(
            agent(cells_here),
            *(
                agent(landed_cells[a, span, :])
                for a in range(agents)
            ),
        )
        scores = [scores[0]] + [
            jnp.where(present[a : a + 1, c * LANES : (c + 1) * LANES].reshape(1, 1, LANES) > 0, s, -1e30)
            for a, s in enumerate(scores[1:])
        ]
        top = functools.reduce(jnp.maximum, scores)
        weights = [jnp.exp(s - top) for s in scores]
        inverse = 1.0 / functools.reduce(jnp.add, weights)
        mix = functools.reduce(jnp.add, [by_head(v, w * inverse) for w, v in zip(weights, values)])
        joined[span, :] = dot(mix.astype(jnp.bfloat16), wout[...], TN)
    out[...] = joined[...].astype(jnp.bfloat16)
    edge = top_row.shape[1]
    rows = total // (vehicles * edge)
    for v in range(vehicles):
        start = v * edge * rows
        top_row[v] = joined[pl.ds(start, edge, stride=rows), :].astype(jnp.bfloat16)
        low_row[v] = joined[pl.ds(start + rows - 1, edge, stride=rows), :].astype(jnp.bfloat16)


def join_weights(wq, wkv, wout, scale):
    return wq.T, wkv.T, wout, jnp.broadcast_to(scale[:, None], (scale.shape[0], 128))


def present_cells(live, phase, rows):
    return jnp.repeat(live.astype(jnp.float32), len(phase_columns(phase)) * rows, axis=1)


def join_agents(pieces, arrived, origins, tile_cols, plan, present, weights):
    count, cols, rows, channels = pieces.shape
    agents = present.shape[0]
    cells = cols * rows
    total = count * cells
    whole = lambda shape: pl.BlockSpec(shape, lambda r, *_: (0,) * len(shape))
    shapes = [(total, channels)] + [(count // tile_cols, tile_cols * cols, channels)] * 2
    return pl.pallas_call(
        functools.partial(join_kernel, origins, tile_cols),
        out_shape=[jax.ShapeDtypeStruct(shape, jnp.bfloat16) for shape in shapes],
        grid_spec=pltpu.PrefetchScalarGridSpec(
            num_scalar_prefetch=4,
            grid=(1,),
            in_specs=[
                whole((total, channels)),
                *[pl.BlockSpec(memory_space=pl.ANY)] * len(arrived),
                whole(present.shape),
            ]
            + [whole(w.shape) for w in weights],
            out_specs=[whole(shape) for shape in shapes],
            scratch_shapes=[
                pltpu.VMEM((agents * count, cells, channels), jnp.bfloat16),
                pltpu.VMEM((total, channels), jnp.float32),
                pltpu.SemaphoreType.DMA((agents * count // tile_cols,)),
            ],
        ),
        compiler_params=pltpu.CompilerParams(vmem_limit_bytes=VMEM_BYTES),
        cost_estimate=pl.CostEstimate(
            flops=total * channels * channels * 40, bytes_accessed=total * channels * 12, transcendentals=total * 20
        ),
    )(
        *plan,
        pieces.reshape(total, channels),
        *(x.reshape(-1, cells, channels) for x in arrived),
        present,
        *weights,
    )


def norm(x, gain):
    average = jnp.mean(x, axis=-1, keepdims=True)
    centred = x - average
    spread = jnp.mean(centred * centred, axis=-1, keepdims=True)
    return (centred * lax.rsqrt(spread + norm_eps) * gain).astype(jnp.bfloat16)


def spread_rows(ref, rows_of, at, rows):
    count, channels = rows_of.shape
    ref[pl.ds(at, count, stride=rows), :] = rows_of.astype(jnp.float32)
    return ref[: count * rows].reshape(count, rows, channels)


def runs_of(phase, tile_cols, whole_map, pieces):
    run = TILE // PHASES
    out = []
    for t in range(tile_cols):
        first = t * TILE + phase * run - 1
        if pieces is None:
            last = first + run + 2
            blank = jnp.zeros_like(whole_map[:1])
            body = whole_map[max(first, 0) : min(last, tile_cols * TILE)]
            parts = ([blank] if first < 0 else []) + [body] + ([blank] if last > tile_cols * TILE else [])
        else:
            size = run + 2
            one = pieces[0]
            blank = jnp.zeros_like(one[:1])
            if phase == 0:
                left = one[(t - 1) * size : (t - 1) * size + 1] if t else blank
                parts = [left, one[t * size + 1 : (t + 1) * size]]
            else:
                rest = TILE - size
                right = one[(t + 1) * size + 1 : (t + 1) * size + 2] if t + 1 < tile_cols else blank
                parts = [
                    one[t * size + run : (t + 1) * size],
                    pieces[1][t * rest : (t + 1) * rest],
                    one[t * size : t * size + 1],
                    right,
                ]
        out.append(jnp.concatenate(parts, axis=0))
    return out


def taps_of(runs, above, below, taps):
    out = []
    for x, first, last in zip(runs, above, below):
        cols, rows, channels = x.shape
        row = lax.broadcasted_iota(jnp.int32, (rows, channels), 0)[None]
        flat = x.reshape(cols * rows, channels)
        over = jnp.where(row == 0, first, pltpu.roll(flat, 1, 0).reshape(x.shape))
        under = jnp.where(row == rows - 1, last, pltpu.roll(flat, cols * rows - 1, 0).reshape(x.shape))
        total = x[1 : cols - 1]
        for j in range(3):
            span = slice(j, cols - 2 + j)
            total = total + over[span] * taps[j] + x[span] * taps[3 + j] + under[span] * taps[6 + j]
        out.append(total.reshape((cols - 2) * rows, channels))
    return out


def window_kernel(phase, rows, *refs):
    ego, ego_up, ego_down, refs = *refs[:3], refs[3:]
    pieces, refs = [refs[3 * p : 3 * p + 3] for p in range(phase + 1)], refs[3 * phase + 3 :]
    taps, gain_one, wq, wk, wv, wo, scale, gain_two, up, down = refs[:10]
    out, mixed_ref, result_ref, halo = refs[10 + phase :]
    group_size, cols, _, channels = ego.shape
    tile_cols = cols // TILE
    run = TILE // PHASES
    width = 2 * channels
    in_window = rows * WIN
    here = tile_cols * run * rows
    cells = group_size * here
    windows = cells // in_window
    heads = width // HEAD
    f32 = jnp.float32
    for v in range(group_size):
        for half in range(2):
            lanes = slice(half * channels, (half + 1) * channels)
            weights = [taps[i : i + 1, lanes].reshape(1, 1, channels) for i in range(9)]
            if half == 0:
                centre = runs_of(phase, tile_cols, ego[v].astype(f32), None)
                above = runs_of(phase, tile_cols, spread_rows(halo.at[0], ego_up[v, 0], 0, rows), None)
                below = runs_of(phase, tile_cols, spread_rows(halo.at[1], ego_down[v, 0], rows - 1, rows), None)
            else:
                centre, above, below = [], [], []
                for p, (x, first, last) in enumerate(pieces):
                    centre.append(x[v].astype(f32).reshape(-1, rows, channels))
                    above.append(spread_rows(halo.at[2 + 2 * p], first[v], 0, rows))
                    below.append(spread_rows(halo.at[3 + 2 * p], last[v], rows - 1, rows))
                centre, above, below = (runs_of(phase, tile_cols, None, x) for x in (centre, above, below))
            for t, part in enumerate(taps_of(centre, above, below, weights)):
                at = v * here + t * run * rows
                mixed_ref[at : at + run * rows, lanes] = part
    hidden = norm(mixed_ref[...], gain_one[...])
    queries = dot(wq[...], hidden, NT)
    values = dot(wv[...], hidden, NT).astype(jnp.bfloat16)
    keys = dot(hidden, wk[...])
    factor = lax.rsqrt(head_sums(queries * queries) + unit_eps) * scale[:, :1].reshape(heads, 1, 1)
    queries = by_head(queries, factor)
    member = (
        lax.broadcasted_iota(jnp.int32, (width, width), 0) // HEAD
        == lax.broadcasted_iota(jnp.int32, (width, width), 1) // HEAD
    ).astype(f32).astype(jnp.bfloat16)
    square_high, square_low = split(keys * keys)
    keys = keys * lax.rsqrt(dot(square_high, member) + dot(square_low, member) + unit_eps)
    key_high, key_low = split(keys)

    pair = 2 * in_window
    group = 4 * HEAD
    lane = lax.broadcasted_iota(jnp.int32, (width, pair), 1) < in_window
    even = (lax.broadcasted_iota(jnp.int32, (width, pair), 0) // HEAD) % 2 == 0
    blank = jnp.zeros((2 * HEAD, pair), jnp.bfloat16)
    blank_p = jnp.zeros((in_window, 4 * in_window), jnp.bfloat16)
    lane_head = lax.broadcasted_iota(jnp.int32, (HEAD, pair), 1) < in_window
    rights = []
    for p in range(windows // 2):
        straight = queries[:, p * pair : (p + 1) * pair]
        turned = pltpu.roll(straight, in_window, 1)
        for w in range(2):
            low, high = (straight, turned) if w == 0 else (turned, straight)
            rights.append(split(jnp.where(even, jnp.where(lane, low, 0.0), jnp.where(lane, 0.0, high))))

    def right(block, g):
        block = block[g * group : (g + 1) * group]
        return jnp.concatenate(
            [
                jnp.concatenate([block[: 2 * HEAD], blank], axis=1),
                jnp.concatenate([blank, block[2 * HEAD :]], axis=1),
            ],
            axis=0,
        )

    groups = width // group
    scores = []
    for w in range(windows):
        for g in range(groups):
            span = slice(w * in_window, (w + 1) * in_window), slice(g * group, (g + 1) * group)
            both = dot(jnp.concatenate([key_high[span], key_low[span]], axis=0), right(rights[w][0], g))
            scores.append(both[:in_window] + both[in_window:] + dot(key_high[span], right(rights[w][1], g)))
    probs = []
    for score in scores:
        weight = jnp.exp2(score - jnp.max(score, axis=0, keepdims=True))
        probs.append((weight * (1.0 / jnp.sum(weight, axis=0, keepdims=True))).astype(jnp.bfloat16))
    attended = []
    for p in range(windows // 2):
        parts = []
        for g in range(groups):
            v = values[g * group : (g + 1) * group, p * pair : (p + 1) * pair]
            first = dot(v, jnp.concatenate([probs[2 * p * groups + g], blank_p], axis=0))
            second = dot(v, jnp.concatenate([blank_p, probs[(2 * p + 1) * groups + g]], axis=0))
            for h in range(4):
                rows_of = slice(h * HEAD, (h + 1) * HEAD)
                cols_of = slice((h // 2) * pair, (h // 2 + 1) * pair)
                a, b = first[rows_of, cols_of], second[rows_of, cols_of]
                if h % 2 == 0:
                    b = pltpu.roll(b, in_window, 1)
                else:
                    a = pltpu.roll(a, in_window, 1)
                parts.append(jnp.where(lane_head, a, b))
        attended.append(jnp.concatenate(parts, axis=0).astype(jnp.bfloat16))
    attended = jnp.concatenate(attended, axis=1)
    mixed = mixed_ref[...] + dot(attended, wo[...], TN)
    hidden = norm(mixed, gain_two[...])
    inner = dot(hidden, up[...])
    inner = (0.5 * inner * (1.0 + jnp.tanh(0.5 * inner))).astype(jnp.bfloat16)
    result = mixed + dot(inner, down[...])
    for half in range(2):
        result_ref[half] = result[:, half * channels : (half + 1) * channels]
    for v in range(group_size):
        for t in range(tile_cols):
            for i in range(rows):
                at = v * here + t * run * rows + i
                for half in range(2):
                    lanes = slice(half * channels, (half + 1) * channels)
                    line = result_ref[half, pl.ds(at, run, stride=rows), :]
                    out[v, i, t, :, lanes] = line.astype(jnp.bfloat16)


def window_weights(conv_weight, gain_first, window_in, window_out, window_scale, gain_second, hidden_up, hidden_down):
    width = conv_weight.shape[-1]
    return (
        conv_weight.reshape(9, width),
        gain_first[None],
        window_in[:, :width].T,
        window_in[:, width : 2 * width],
        window_in[:, 2 * width :].T,
        window_out,
        jnp.broadcast_to((window_scale * LOG2E)[:, None], (window_scale.shape[0], 128)),
        gain_second[None],
        hidden_up,
        hidden_down,
    )


def window_layer(phase, turned, ego_edges, pieces, before, weights):
    vehicles, cols, rows, channels = turned.shape
    width = 2 * channels
    tile_cols = cols // TILE
    run = TILE // PHASES
    group = vehicles
    whole = lambda x: pl.BlockSpec(x.shape, lambda r: (0,) * x.ndim)
    block = lambda *shape: pl.BlockSpec((group, *shape), lambda r: (r,) + (0,) * len(shape))
    pieces = [x.reshape(vehicles, -1, channels) for three in pieces for x in three]
    cells = vehicles * rows * tile_cols * run
    most = cols * rows
    operands = (turned, *ego_edges, *pieces, *weights)
    in_specs = (
        [block(cols, rows, channels)]
        + [block(1, cols, channels)] * 2
        + [block(*x.shape[1:]) for x in pieces]
        + [whole(w) for w in weights]
    )
    aliases = {}
    if before is not None:
        aliases = {len(operands): 0}
        operands += (before,)
        in_specs += [pl.BlockSpec(memory_space=pl.ANY)]
    return pl.pallas_call(
        functools.partial(window_kernel, phase, rows),
        out_shape=jax.ShapeDtypeStruct((vehicles, rows, tile_cols, PHASES, run, width), jnp.bfloat16),
        grid=(vehicles // group,),
        in_specs=in_specs,
        out_specs=pl.BlockSpec(
            (group, rows, tile_cols, None, run, width), lambda r: (r, 0, 0, phase, 0, 0)
        ),
        scratch_shapes=[
            pltpu.VMEM((group * rows * tile_cols * run, width), jnp.float32),
            pltpu.VMEM((2, group * rows * tile_cols * run, channels), jnp.float32),
            pltpu.VMEM((2 * PHASES + 2, most, channels), jnp.float32),
        ],
        input_output_aliases=aliases,
        compiler_params=pltpu.CompilerParams(vmem_limit_bytes=WINDOW_VMEM_BYTES),
        cost_estimate=pl.CostEstimate(
            flops=cells * width * width * 60, bytes_accessed=cells * width * 6, transcendentals=cells * width * 4
        ),
    )(*operands)


def beside(last, first):
    count = lax.axis_size("row")
    above = lax.ppermute(last, "row", [(i, i + 1) for i in range(count - 1)])
    below = lax.ppermute(first, "row", [(i + 1, i) for i in range(count - 1)])
    return above, below


def on_device(
    bev_maps,
    senders,
    shifts,
    counts,
    agent_query,
    agent_keyvalue,
    agent_out,
    agent_scale,
    conv_weight,
    gain_first,
    window_in,
    window_out,
    window_scale,
    gain_second,
    hidden_up,
    hidden_down,
):
    vehicles_here, rows, cols, channels = bev_maps.shape
    devices = lax.axis_size("veh")
    tile_cols = cols // TILE
    group = half_size()
    capacity = tile_cols * max(1, vehicles_here * senders.shape[1] // devices)
    turned, first, second = turn_maps(bev_maps)

    def swap(x):
        return lax.ppermute(x, "veh", [(i, (i + group) % devices) for i in range(devices)])

    def send(messages):
        return [
            lax.ppermute(
                x, "veh", [(i, i // group * group + (i + k + 1) % group) for i in range(devices)]
            )
            for k, x in enumerate(messages)
        ]

    far = swap(first)
    chosen, filled, *plan = plan_of(senders, shifts, counts, tile_cols, capacity)
    entries, listed, sizes_of, live, blank = plan
    plan = (entries, listed, sizes_of, blank)
    live = live.reshape(senders.shape[1], -1)
    near_messages = messages_for(chosen, filled, capacity, {0: first})
    near_tiles = send(near_messages)
    ego_edges = beside(bev_maps[:, rows - 1 :], bev_maps[:, :1])
    join_all = join_weights(agent_query, agent_keyvalue, agent_out, agent_scale)
    present = [present_cells(live, p, rows) for p in range(PHASES)]
    window_all = window_weights(
        conv_weight, gain_first, window_in, window_out, window_scale, gain_second, hidden_up, hidden_down
    )
    far, second, join_all, present, window_all, _ = lax.optimization_barrier(
        (far, second, join_all, present, window_all, near_messages)
    )
    far_tiles = send(messages_for(chosen, filled, capacity, {1: far}))
    later = swap(second)
    later_messages = messages_for(chosen, filled, capacity, {0: second, 1: later})
    later_tiles = send(later_messages)
    arrived = [[first, far, *near_tiles, *far_tiles], [second, later, *later_tiles]]
    origins = [
        [(0, 0), (1, 0)] + [(2 + k + part * (group - 1), 0) for k in range(group - 1) for part in (0, 1)],
        [(0, 0), (1, 0)] + [(2 + k, part * capacity) for k in range(group - 1) for part in (0, 1)],
    ]
    result, pieces = None, []
    for phase, own in enumerate((first, second)):
        if phase:
            plan, result = lax.optimization_barrier((plan, result))
        joined, top, low = join_agents(
            own, arrived[phase], origins[phase], tile_cols, plan, present[phase], join_all
        )
        pieces.append((joined, *beside(low, top)))
        result = window_layer(phase, turned, ego_edges, pieces, result, window_all)
    return result.reshape(vehicles_here, rows, cols, 2 * channels)


def solution(mesh):
    split_maps = P("veh", "row", None, None)
    return jax.shard_map(
        on_device,
        mesh=mesh,
        in_specs=(split_maps,) + (P(),) * 15,
        out_specs=split_maps,
        check_vma=False,
    )
```
